32 devices in a mesh: grp: 2 (over x), tmpl: 8 (over z, y), tm: 2 (over core).
Axes of the slice: x: 2, y: 2, z: 4, core: 2. Of those that a mesh axis runs over, the one named last changes fastest.
Arguments:
- spectra: bfloat16 [1024, 4, 8192], P(('grp', 'tm', 'tmpl')), parts along dimension 0, may hold values from -6 to 6
- offsets: int32 [1024, 16], P(('grp', 'tm'), 'tmpl'), parts along dimension 0, may hold values from 0 to 1008
- fractions: float32 [4096], P(('grp', 'tmpl')), parts along dimension 0, may hold values from 0.1 to 0.9
- antenna: float32 [1024, 4], P('grp'), parts along dimension 0, may hold values from -2 to 2, as said below
- starts: int32 [64], P('grp'), parts along dimension 0, may hold values from 0 to 255
- durations: int32 [64], P('grp'), parts along dimension 0, may hold values from 48 to 256
Outputs:
- fstat_map: float32 [32, 32, 4096], P('tm', None, ('grp', 'tmpl')), parts along dimension 2
- loudest: float32 [64, 32], P(('grp', 'tm')), parts along dimension 0
The draws below stay inside these ranges and needn't reach their ends.
There are 2 independent parts, one for each index of `grp`. The reference program is written for one: setup_inputs(seed, part) draws one part's arguments, and reference() takes and returns one part's arrays. A program takes and returns all parts, laid end to end along the dimension named above; each array names one. Nothing has to cross between parts.
Inputs may be any that keep to these rules, and one draw needn't show every extreme that they name: `antenna`: each detector's responses a and b turn once every 48 SFTs with magnitudes that vary from SFT to SFT.
All inputs are finite; a program needn't handle non-finite values.
Results may differ from the reference program's by a relative error of at most 0.0051.
Values may be sent and summed in bfloat16 or wider, within the bound.
No kernel may reach another device: no remote copies, remote signals or barrier semaphores. Data moves between devices by JAX's collectives and lax.ppermute only.
A program may use at most 128 MiB of HBM per device.

```python
import jax
import jax.numpy as jnp
from jax import lax

W = 16
TPB = 128
NG = 32
DAY = 48
BAND_DEV = 1024
NB_DEV = 2
NSFT = 512
NBLK = 16
QTOT = 2048
BINS = 8192


def draw_antenna(key, part):
    key_phase, key_size, key_jitter = jax.random.split(key, 3)
    sft_axis = jnp.arange(NSFT, dtype=jnp.float32)[:, None]
    start_phase = jax.random.uniform(key_phase, (1, 2), jnp.float32, 0.0, 2.0 * jnp.pi)
    magnitude = jax.random.uniform(key_size, (NSFT, 2), jnp.float32, 0.5, 1.5)
    jitter = jax.random.uniform(key_jitter, (NSFT, 2), jnp.float32, -0.6, 0.6)
    turn_angle = 2.0 * jnp.pi * sft_axis / DAY + start_phase + jitter
    return jnp.concatenate([magnitude * jnp.cos(turn_angle), magnitude * jnp.sin(turn_angle)], axis=1)


def plant(values, own_key, smallest, top_value):
    index_at = [jax.random.randint(jax.random.fold_in(own_key, axis), (), 0, length) for axis, length in enumerate(values.shape)]
    main_axis = values.shape.index(max(values.shape))
    next_to = index_at[:main_axis] + [(index_at[main_axis] + 1) % values.shape[main_axis]] + index_at[main_axis + 1:]
    return values.at[tuple(index_at)].set(smallest).at[tuple(next_to)].set(top_value)


def shard_levels(rng, extent, cuts, smallest, high):
    def one(position, blocks):
        heights = jax.random.uniform(jax.random.fold_in(jax.random.fold_in(rng, 6), position), (blocks,), jnp.float32, smallest / len(cuts), high / len(cuts))
        return jnp.repeat(jnp.exp(heights), extent[position] // blocks).reshape((-1,) + (1,) * (len(extent) - position - 1))

    level = one(*cuts[0])
    for cut in cuts[1:]:
        level = level * one(*cut)
    return level


def noise(rng, dims, width, limit, cuts=(), held_as=jnp.bfloat16):
    drawn = width * jax.random.normal(rng, dims, jnp.float32)
    if cuts:
        drawn = drawn * shard_levels(rng, dims, cuts, -0.22, 0.18)
    return jnp.clip(drawn, -limit, limit).astype(held_as)


def setup_inputs(seed: int = 0, part: int = 0) -> dict:
    key_of = jax.random.split(jax.random.key(seed), 7)
    own_keys = jax.random.split(jax.random.fold_in(key_of[6], part), 7)
    spectra = noise(own_keys[0], (NSFT, 4, BINS), 1.0, 6.0, ((0, 16),))
    offsets = plant(jax.random.randint(own_keys[1], (NSFT, NBLK), 0, BAND_DEV - W + 1), jax.random.fold_in(own_keys[1], 1), 0, BAND_DEV - W).astype(jnp.int32)
    fractions = jnp.clip(0.1 + 0.79999997 * jax.random.uniform(own_keys[2], (QTOT,), jnp.float32) ** shard_levels(own_keys[2], (QTOT,), ((0, 8),), -0.2, 0.2), 0.1, 0.9)
    antenna = draw_antenna(jax.random.fold_in(jax.random.fold_in(key_of[6], part), 71), part)
    starts = plant(jax.random.randint(own_keys[4], (NG,), 0, NSFT // 2), jax.random.fold_in(own_keys[4], 1), 0, (NSFT // 2) - 1).astype(jnp.int32)
    durations = plant(jax.random.randint(own_keys[5], (NG,), DAY, NSFT // 2 + 1), jax.random.fold_in(own_keys[5], 1), DAY, (NSFT // 2 + 1) - 1).astype(jnp.int32)
    return dict(spectra=spectra, offsets=offsets, fractions=fractions, antenna=antenna, starts=starts, durations=durations)


def pick_bins(spectrum, places):
    return spectrum[:, places]


def weigh(windows, antenna):
    values = windows.astype(jnp.float32)
    detector_one = values[:, 0:2]
    detector_two = values[:, 2:4]
    weighted_a = antenna[:, 0][:, None, None, None] * detector_one + antenna[:, 1][:, None, None, None] * detector_two
    weighted_b = antenna[:, 2][:, None, None, None] * detector_one + antenna[:, 3][:, None, None, None] * detector_two
    return jnp.concatenate([weighted_a, weighted_b], axis=1).astype(jnp.bfloat16)


def dirichlet(fractions):
    bin_shift = jnp.arange(W, dtype=jnp.float32)
    distance = fractions[:, None] + (W // 2 - 1) - bin_shift[None, :]
    parity = (jnp.arange(W, dtype=jnp.int32) % 2).astype(jnp.float32)
    alternate = 1.0 - 2.0 * parity
    return (alternate[None, :] * jnp.sin(jnp.pi * fractions)[:, None] / (jnp.pi * distance)).astype(jnp.bfloat16)


def antenna_prefix(antenna):
    along_a = antenna[:, 0] * antenna[:, 0] + antenna[:, 1] * antenna[:, 1]
    along_b = antenna[:, 2] * antenna[:, 2] + antenna[:, 3] * antenna[:, 3]
    across = antenna[:, 0] * antenna[:, 2] + antenna[:, 1] * antenna[:, 3]
    stacked = jnp.stack([along_a, along_b, across], axis=1)
    return jnp.concatenate([jnp.zeros((1, 3), jnp.float32), jnp.cumsum(stacked, axis=0)], axis=0)


def statistic(interval, weights):
    real_a = interval[..., 0, :]
    imag_a = interval[..., 1, :]
    real_b = interval[..., 2, :]
    imag_b = interval[..., 3, :]
    weight_a = weights[..., 0:1]
    weight_b = weights[..., 1:2]
    weight_c = weights[..., 2:3]
    numerator = weight_b * (real_a * real_a + imag_a * imag_a) + weight_a * (real_b * real_b + imag_b * imag_b) - 2.0 * weight_c * (real_a * real_b + imag_a * imag_b)
    return numerator / (weight_a * weight_b - weight_c * weight_c)


def reference(spectra, offsets, fractions, antenna, starts, durations):
    band_start = (jnp.arange(NBLK, dtype=jnp.int32) // NB_DEV) * BAND_DEV
    bin_index = offsets[:, :, None] + band_start[None, :, None] + jnp.arange(W, dtype=jnp.int32)[None, None, :]
    windows = jax.vmap(pick_bins)(spectra, bin_index)
    weighted = weigh(windows, antenna)
    kernel = dirichlet(fractions).reshape(NBLK, TPB, W)
    atom_rows = jnp.einsum("scbm,bqm->scbq", weighted.astype(jnp.float32), kernel.astype(jnp.float32), precision=lax.Precision.HIGHEST)
    atom_rows = atom_rows.reshape(NSFT, 4 * QTOT)
    running = jnp.concatenate([jnp.zeros((1, 4 * QTOT), jnp.float32), jnp.cumsum(atom_rows, axis=0)], axis=0)
    end_points = starts[None, :] + durations[:, None]
    interval = running[end_points] - running[starts][None]
    cum_weights = antenna_prefix(antenna)
    weights = cum_weights[end_points] - cum_weights[starts][None]
    fstat_map = statistic(interval.reshape(NG, NG, 4, QTOT), weights)
    loudest = jnp.max(fstat_map, axis=2)
    return fstat_map, loudest
```

```python
import functools

import jax
import jax.numpy as jnp
from jax import lax
from jax.experimental import pallas as pl
from jax.experimental.pallas import tpu as pltpu
from jax.sharding import PartitionSpec as P

W = 16
LANES = 128
NT = (((1,), (1,)), ((), ()))


def iota(shape, axis):
    return lax.broadcasted_iota(jnp.int32, shape, axis)


def pick_kernel(bands, rows, band_width, me_ref, *refs):
    offset_refs = refs[:bands]
    spec_ref, out_ref, high_ref, low_ref = refs[bands:]
    me = me_ref[0]
    blocks = offset_refs[0].shape[0]
    sft_count = offset_refs[0].shape[1]
    chunks = band_width // LANES
    offsets = jnp.concatenate([ref[...] for ref in offset_refs], axis=0)
    mine = iota((rows, sft_count), 1) == iota((rows, sft_count), 0) + me * rows
    mine = mine.astype(jnp.bfloat16)
    spread_shape = (bands * blocks, bands * LANES)
    source = iota(spread_shape, 0)
    target = iota(spread_shape, 1)
    wanted = ((source // blocks) ^ me) * blocks + source % blocks
    holds = (target // LANES) * blocks + (target // W) % blocks
    spread = (wanted == holds).astype(jnp.bfloat16)

    def lay_out(values, ref):
        own = lax.dot_general(mine, values.astype(jnp.float32).astype(jnp.bfloat16), NT, preferred_element_type=jnp.float32)
        ref[...] = jnp.dot(own.astype(jnp.bfloat16), spread, preferred_element_type=jnp.float32).astype(jnp.int32)

    lay_out(offsets // LANES, high_ref)
    lay_out(offsets % LANES, low_ref)
    lane = iota((8, LANES), 1)
    shift = lane % W
    component = (lane // (blocks * W)) * chunks
    bands_per_step = max(1, 16 // rows)

    def step(index, carry):
        tiles = []
        for inner in range(bands_per_step):
            band = index * bands_per_step + inner
            at_lane = pl.ds(pl.multiple_of(band * LANES, LANES), LANES)
            for group in range(rows // 8):
                at_row = pl.ds(group * 8, 8)
                place = low_ref[at_row, at_lane] + shift
                lane_id = place % LANES
                chosen = high_ref[at_row, at_lane] + place // LANES + component
                tile = jnp.zeros((8, LANES), jnp.float32)
                for part in range(4):
                    for chunk in range(chunks):
                        start = pl.multiple_of(band * band_width + chunk * LANES, LANES)
                        values = spec_ref[part, at_row, pl.ds(start, LANES)]
                        moved = jnp.take_along_axis(values, lane_id, axis=1, mode="promise_in_bounds")
                        tile = jnp.where(chosen == part * chunks + chunk, moved, tile)
                tiles.append(tile)
        count = len(tiles) * 8
        out_ref[pl.ds(pl.multiple_of(index * count, count), count), :] = jnp.concatenate(tiles, axis=0).astype(jnp.bfloat16)
        return carry

    lax.fori_loop(0, bands // bands_per_step, step, 0)


def pick(me, offset_parts, spec, band_width):
    bands = len(offset_parts)
    rows = spec.shape[1]
    vmem = pl.BlockSpec(memory_space=pltpu.VMEM)
    return pl.pallas_call(
        functools.partial(pick_kernel, bands, rows, band_width),
        out_shape=jax.ShapeDtypeStruct((bands * rows, LANES), jnp.bfloat16),
        in_specs=[pl.BlockSpec(memory_space=pltpu.SMEM)] + [vmem] * (bands + 1),
        out_specs=vmem,
        scratch_shapes=[pltpu.VMEM((rows, bands * LANES), jnp.int32)] * 2,
        compiler_params=pltpu.CompilerParams(vmem_limit_bytes=32 * 1024 * 1024),
        cost_estimate=pl.CostEstimate(flops=10_000_000, bytes_accessed=4 * spec.size, transcendentals=0),
        name="pick",
    )(me, *offset_parts, spec)


def split(values, count):
    parts = []
    for _ in range(count):
        part = values.astype(jnp.bfloat16)
        parts.append(part)
        values = values - part.astype(jnp.float32)
    return parts


def prepare_kernel(durations_ref, starts_ref, antenna_ref, fractions_ref, mask_ref, weigh_ref, coef_ref, kernel_ref):
    rows = starts_ref.shape[0]
    count = durations_ref.shape[0]
    sfts = antenna_ref.shape[1]
    sft = iota((rows, sfts), 1)
    start = starts_ref[:, 0:1]
    after = sft >= start
    for j in range(count):
        inside = after & (sft < start + durations_ref[j])
        mask_ref[pl.ds(j * rows, rows), :] = jnp.where(inside, 1.0, 0.0).astype(jnp.bfloat16)
    antenna = antenna_ref[...]
    a1, a2, b1, b2 = (antenna[n : n + 1] for n in range(4))
    terms = jnp.concatenate([a1 * a1 + a2 * a2, b1 * b1 + b2 * b2, a1 * b1 + a2 * b2, jnp.zeros((5, sfts), jnp.float32)], axis=0)
    weights = sum(lax.dot_general(mask_ref[...], part, NT, preferred_element_type=jnp.float32) for part in split(terms, 3))
    wa, wb, wc = (weights[:, n : n + 1] for n in range(3))
    shape = (rows * count, LANES)
    late = iota(shape, 1) >= LANES // 2
    coef_ref[0] = jnp.broadcast_to(1.0 / wa, shape)
    coef_ref[1] = jnp.broadcast_to(wa / (wa * wb - wc * wc), shape)
    coef_ref[2] = jnp.where(late, jnp.broadcast_to(wc / wa, shape), 0.0)
    upright = jnp.transpose(jnp.concatenate([antenna, jnp.zeros((LANES - 4, sfts), jnp.float32)], axis=0))
    shape = (sfts, LANES)
    late = iota(shape, 1) >= LANES // 2
    weigh_ref[0] = jnp.where(late, upright[:, 3:4], upright[:, 0:1])
    weigh_ref[1] = jnp.where(late, upright[:, 2:3], upright[:, 1:2])
    fractions = fractions_ref[...]
    templates = fractions.shape[1]
    blocks = kernel_ref.shape[1] // (4 * LANES)
    bin_id = iota((W, templates), 0)
    distance = fractions + (W // 2 - 1) - bin_id.astype(jnp.float32)
    alternate = 1.0 - 2.0 * (bin_id % 2).astype(jnp.float32)
    values = (alternate * jnp.sin(jnp.pi * fractions) / (jnp.pi * distance)).astype(jnp.bfloat16)
    kernel_ref[...] = jnp.zeros_like(kernel_ref)
    for part in range(2):
        for c in range(4):
            for b in range(blocks):
                row = ((part * 4 + c) * blocks + b) * W
                column = (c * blocks + b) * LANES
                kernel_ref[pl.ds(row, W), pl.ds(column, LANES)] = values[:, b * LANES : (b + 1) * LANES]


def prepare(durations, starts, antenna, fractions):
    count, rows, sfts = durations.shape[0], starts.shape[0], antenna.shape[0]
    columns = 4 * fractions.shape[0]
    features = 4 * W * (fractions.shape[0] // LANES)
    vmem = pl.BlockSpec(memory_space=pltpu.VMEM)
    return pl.pallas_call(
        prepare_kernel,
        out_shape=(
            jax.ShapeDtypeStruct((count * rows, sfts), jnp.bfloat16),
            jax.ShapeDtypeStruct((2, sfts, LANES), jnp.float32),
            jax.ShapeDtypeStruct((3, count * rows, LANES), jnp.float32),
            jax.ShapeDtypeStruct((2 * features, columns), jnp.bfloat16),
        ),
        in_specs=[pl.BlockSpec(memory_space=pltpu.SMEM), vmem, vmem, vmem],
        out_specs=(vmem,) * 4,
        compiler_params=pltpu.CompilerParams(vmem_limit_bytes=32 * 1024 * 1024),
        cost_estimate=pl.CostEstimate(flops=100_000_000, bytes_accessed=4_000_000, transcendentals=0),
        name="prepare",
    )(durations, jnp.broadcast_to(starts[:, None], (rows, LANES)), antenna.T, fractions[None, :])


def statistic_kernel(windows_ref, mask_ref, weigh_ref, coef_ref, kernel_ref, map_ref, loudest_ref):
    values = windows_ref[...].astype(jnp.float32)
    half = LANES // 2
    weighted = (weigh_ref[0] * values + weigh_ref[1] * pltpu.roll(values, half, 1)).astype(jnp.bfloat16)
    templates = map_ref.shape[1]
    rows = loudest_ref.shape[1]
    per_step = LANES // rows
    for step in range(map_ref.shape[0] // LANES):
        here = pl.ds(step * LANES, LANES)
        sums = jnp.dot(mask_ref[here, :], weighted, preferred_element_type=jnp.float32)
        sums = sums - coef_ref[2, here, :] * pltpu.roll(sums, half, 1)
        parts = jnp.concatenate(split(sums, 2), axis=1)
        found = jnp.dot(parts, kernel_ref[...], preferred_element_type=jnp.float32)
        ra, ia, rb, ib = (found[:, c * templates : (c + 1) * templates] for c in range(4))
        power_a, power_b = ra * ra + ia * ia, rb * rb + ib * ib
        best = None
        for b in range(templates // LANES):
            columns = slice(b * LANES, (b + 1) * LANES)
            result = coef_ref[0, here, :] * power_a[:, columns] + coef_ref[1, here, :] * power_b[:, columns]
            map_ref[here, columns] = result
            best = result if best is None else jnp.maximum(best, result)
        best = jnp.max(jnp.transpose(best), axis=0, keepdims=True)
        for n in range(per_step):
            turned = best if n == 0 else pltpu.roll(best, LANES - n * rows, 1)
            loudest_ref[pl.ds(step * per_step + n, 1), :] = turned[:, :rows]


def statistic(windows, mask, weigh, coef, kernel, rows):
    count = mask.shape[0] // rows
    templates = kernel.shape[1] // 4
    vmem = pl.BlockSpec(memory_space=pltpu.VMEM)
    return pl.pallas_call(
        statistic_kernel,
        out_shape=(
            jax.ShapeDtypeStruct((count * rows, templates), jnp.float32),
            jax.ShapeDtypeStruct((count, rows), jnp.float32),
        ),
        in_specs=[vmem] * 5,
        out_specs=(vmem, vmem),
        compiler_params=pltpu.CompilerParams(vmem_limit_bytes=32 * 1024 * 1024),
        cost_estimate=pl.CostEstimate(flops=400_000_000, bytes_accessed=4_000_000, transcendentals=0),
        name="statistic",
    )(windows, mask, weigh, coef, kernel)


def to_all(values, axis):
    size = lax.axis_size(axis)
    return [values] + [lax.ppermute(values, axis, [(n, n ^ r) for n in range(size)]) for r in range(1, size)]


def body(spectra, offsets, fractions, antenna, starts, durations):
    bands, cores = lax.axis_size("tmpl"), lax.axis_size("tm")
    sft_rows = spectra.shape[0]
    band_width = spectra.shape[2] // bands
    grid_size = starts.shape[0]
    my_rows = grid_size // cores
    me = lax.axis_index("tmpl").astype(jnp.int32)[None]
    offset_parts = to_all(offsets.T, "tmpl")
    spec = jnp.transpose(spectra, (1, 0, 2)).astype(jnp.float32)
    my_durations = lax.dynamic_slice_in_dim(durations, lax.axis_index("tm") * my_rows, my_rows, 0)
    prepared = prepare(my_durations, starts, antenna, fractions)
    windows = pick(me, offset_parts, spec, band_width).reshape(1, bands, sft_rows, LANES)
    windows = jnp.broadcast_to(windows, (cores, bands, sft_rows, LANES)).reshape(cores * bands, sft_rows, LANES)
    arrived = lax.all_to_all(windows, ("tm", "tmpl"), split_axis=0, concat_axis=0, tiled=True)
    arrived = arrived.reshape(cores * bands * sft_rows, LANES)
    fstat_map, loudest = statistic(arrived, *prepared, grid_size)
    loudest = functools.reduce(jnp.maximum, to_all(loudest, "tmpl"))
    return (fstat_map.reshape(my_rows, grid_size, -1), loudest)


def solution(mesh):
    in_specs = (
        P(("grp", "tm", "tmpl"), None, None),
        P(("grp", "tm"), "tmpl"),
        P(("grp", "tmpl")),
        P("grp", None),
        P("grp"),
        P("grp"),
    )
    out_specs = (P("tm", None, ("grp", "tmpl")), P(("grp", "tm"), None))
    return jax.shard_map(body, mesh=mesh, in_specs=in_specs, out_specs=out_specs, check_vma=False)
```

```python
import functools

import jax
import jax.numpy as jnp
from jax import lax
from jax.experimental import pallas as pl
from jax.experimental.pallas import tpu as pltpu
from jax.sharding import PartitionSpec as P

W = 16
LANES = 128
NT = (((1,), (1,)), ((), ()))


def iota(shape, axis):
    return lax.broadcasted_iota(jnp.int32, shape, axis)


def pick_kernel(bands, band_width, me_ref, *refs):
    *offset_refs, spec_ref, out_ref, high_ref, low_ref = refs
    me = me_ref[0]
    rows = spec_ref.shape[1]
    sft_count = offset_refs[0].shape[1]
    blocks = sum(ref.shape[0] for ref in offset_refs) // bands
    chunks = band_width // LANES
    offsets = jnp.concatenate([ref[...] for ref in offset_refs], axis=0)
    mine = iota((rows, sft_count), 1) == iota((rows, sft_count), 0) + me * rows
    mine = mine.astype(jnp.bfloat16)
    spread_shape = (bands * blocks, bands * LANES)
    source = iota(spread_shape, 0)
    target = iota(spread_shape, 1)
    wanted = ((source // blocks) ^ me) * blocks + source % blocks
    holds = (target // LANES) * blocks + (target // W) % blocks
    spread = (wanted == holds).astype(jnp.bfloat16)

    def lay_out(values, ref):
        own = lax.dot_general(mine, values.astype(jnp.float32).astype(jnp.bfloat16), NT, preferred_element_type=jnp.float32)
        ref[...] = jnp.dot(own.astype(jnp.bfloat16), spread, preferred_element_type=jnp.float32).astype(jnp.int32)

    lay_out(offsets // LANES, high_ref)
    lay_out(offsets % LANES, low_ref)
    lane = iota((8, LANES), 1)
    shift = lane % W
    component = (lane // (blocks * W)) * chunks
    bands_per_step = max(1, 16 // rows)

    def step(index, carry):
        tiles = []
        for inner in range(bands_per_step):
            band = index * bands_per_step + inner
            at_lane = pl.ds(pl.multiple_of(band * LANES, LANES), LANES)
            for group in range(rows // 8):
                at_row = pl.ds(group * 8, 8)
                place = low_ref[at_row, at_lane] + shift
                lane_id = place % LANES
                chosen = high_ref[at_row, at_lane] + place // LANES + component
                tile = jnp.zeros((8, LANES), jnp.float32)
                for part in range(4):
                    for chunk in range(chunks):
                        start = pl.multiple_of(band * band_width + chunk * LANES, LANES)
                        values = spec_ref[part, at_row, pl.ds(start, LANES)]
                        moved = jnp.take_along_axis(values, lane_id, axis=1, mode="promise_in_bounds")
                        tile = jnp.where(chosen == part * chunks + chunk, moved, tile)
                tiles.append(tile)
        count = len(tiles) * 8
        tiles = jnp.concatenate(tiles, axis=0).astype(jnp.bfloat16)
        for core in range(out_ref.shape[0]):
            out_ref[core, pl.ds(pl.multiple_of(index * count, count), count), :] = tiles
        return carry

    lax.fori_loop(0, bands // bands_per_step, step, 0)


def pick(me, offset_parts, spec, bands, cores):
    rows = spec.shape[1]
    band_width = spec.shape[2] // bands
    vmem = pl.BlockSpec(memory_space=pltpu.VMEM)
    return pl.pallas_call(
        functools.partial(pick_kernel, bands, band_width),
        out_shape=jax.ShapeDtypeStruct((cores, bands * rows, LANES), jnp.bfloat16),
        in_specs=[pl.BlockSpec(memory_space=pltpu.SMEM)] + [vmem] * (len(offset_parts) + 1),
        out_specs=vmem,
        scratch_shapes=[pltpu.VMEM((rows, bands * LANES), jnp.int32)] * 2,
        compiler_params=pltpu.CompilerParams(vmem_limit_bytes=32 * 1024 * 1024),
        cost_estimate=pl.CostEstimate(flops=10_000_000, bytes_accessed=4 * spec.size, transcendentals=0),
        name="pick",
    )(me, *offset_parts, spec)


def split(values, count):
    parts = []
    for _ in range(count):
        part = values.astype(jnp.bfloat16)
        parts.append(part)
        values = values - part.astype(jnp.float32)
    return parts


def prepare_kernel(durations_ref, starts_ref, antenna_ref, fractions_ref, mask_ref, weigh_ref, coef_ref, kernel_ref):
    rows = starts_ref.shape[0]
    count = durations_ref.shape[0]
    sfts = antenna_ref.shape[1]
    sft = iota((rows, sfts), 1)
    start = starts_ref[:, 0:1]
    after = sft >= start
    for j in range(count):
        inside = after & (sft < start + durations_ref[j])
        mask_ref[pl.ds(j * rows, rows), :] = jnp.where(inside, 1.0, 0.0).astype(jnp.bfloat16)
    antenna = antenna_ref[...]
    a1, a2, b1, b2 = (antenna[n : n + 1] for n in range(4))
    terms = jnp.concatenate([a1 * a1 + a2 * a2, b1 * b1 + b2 * b2, a1 * b1 + a2 * b2, jnp.zeros((5, sfts), jnp.float32)], axis=0)
    weights = sum(lax.dot_general(mask_ref[...], part, NT, preferred_element_type=jnp.float32) for part in split(terms, 3))
    wa, wb, wc = (weights[:, n : n + 1] for n in range(3))
    shape = (rows * count, LANES)
    late = iota(shape, 1) >= LANES // 2
    coef_ref[0] = jnp.broadcast_to(1.0 / wa, shape)
    coef_ref[1] = jnp.broadcast_to(wa / (wa * wb - wc * wc), shape)
    coef_ref[2] = jnp.where(late, jnp.broadcast_to(wc / wa, shape), 0.0)
    upright = jnp.transpose(jnp.concatenate([antenna, jnp.zeros((LANES - 4, sfts), jnp.float32)], axis=0))
    shape = (sfts, LANES)
    late = iota(shape, 1) >= LANES // 2
    weigh_ref[0] = jnp.where(late, upright[:, 3:4], upright[:, 0:1])
    weigh_ref[1] = jnp.where(late, upright[:, 2:3], upright[:, 1:2])
    fractions = fractions_ref[...]
    templates = fractions.shape[1]
    blocks = kernel_ref.shape[1] // (4 * LANES)
    bin_id = iota((W, templates), 0)
    distance = fractions + (W // 2 - 1) - bin_id.astype(jnp.float32)
    alternate = 1.0 - 2.0 * (bin_id % 2).astype(jnp.float32)
    values = (alternate * jnp.sin(jnp.pi * fractions) / (jnp.pi * distance)).astype(jnp.bfloat16)
    kernel_ref[...] = jnp.zeros_like(kernel_ref)
    for part in range(2):
        for c in range(4):
            for b in range(blocks):
                row = ((part * 4 + c) * blocks + b) * W
                column = (c * blocks + b) * LANES
                kernel_ref[pl.ds(row, W), pl.ds(column, LANES)] = values[:, b * LANES : (b + 1) * LANES]


def prepare(durations, starts, antenna, fractions):
    count, rows, sfts = durations.shape[0], starts.shape[0], antenna.shape[0]
    columns = 4 * fractions.shape[0]
    features = 4 * W * (fractions.shape[0] // LANES)
    vmem = pl.BlockSpec(memory_space=pltpu.VMEM)
    return pl.pallas_call(
        prepare_kernel,
        out_shape=(
            jax.ShapeDtypeStruct((count * rows, sfts), jnp.bfloat16),
            jax.ShapeDtypeStruct((2, sfts, LANES), jnp.float32),
            jax.ShapeDtypeStruct((3, count * rows, LANES), jnp.float32),
            jax.ShapeDtypeStruct((2 * features, columns), jnp.bfloat16),
        ),
        in_specs=[pl.BlockSpec(memory_space=pltpu.SMEM), vmem, vmem, vmem],
        out_specs=(vmem,) * 4,
        compiler_params=pltpu.CompilerParams(vmem_limit_bytes=32 * 1024 * 1024),
        cost_estimate=pl.CostEstimate(flops=100_000_000, bytes_accessed=4_000_000, transcendentals=0),
        name="prepare",
    )(durations, jnp.broadcast_to(starts[:, None], (rows, LANES)), antenna.T, fractions[None, :])


def statistic_kernel(windows_ref, mask_ref, weigh_ref, coef_ref, kernel_ref, map_ref, loudest_ref):
    values = windows_ref[...].astype(jnp.float32)
    half = LANES // 2
    weighted = (weigh_ref[0] * values + weigh_ref[1] * pltpu.roll(values, half, 1)).astype(jnp.bfloat16)
    templates = map_ref.shape[1]
    rows = loudest_ref.shape[1]
    per_step = LANES // rows
    for step in range(map_ref.shape[0] // LANES):
        here = pl.ds(step * LANES, LANES)
        sums = jnp.dot(mask_ref[here, :], weighted, preferred_element_type=jnp.float32)
        sums = sums - coef_ref[2, here, :] * pltpu.roll(sums, half, 1)
        parts = jnp.concatenate(split(sums, 2), axis=1)
        found = jnp.dot(parts, kernel_ref[...], preferred_element_type=jnp.float32)
        ra, ia, rb, ib = (found[:, c * templates : (c + 1) * templates] for c in range(4))
        power_a, power_b = ra * ra + ia * ia, rb * rb + ib * ib
        best = None
        for b in range(templates // LANES):
            columns = slice(b * LANES, (b + 1) * LANES)
            result = coef_ref[0, here, :] * power_a[:, columns] + coef_ref[1, here, :] * power_b[:, columns]
            map_ref[here, columns] = result
            best = result if best is None else jnp.maximum(best, result)
        best = jnp.max(jnp.transpose(best), axis=0, keepdims=True)
        for n in range(per_step):
            turned = best if n == 0 else pltpu.roll(best, LANES - n * rows, 1)
            loudest_ref[pl.ds(step * per_step + n, 1), :] = turned[:, :rows]


def statistic(windows, mask, weigh, coef, kernel, rows):
    count = mask.shape[0] // rows
    templates = kernel.shape[1] // 4
    vmem = pl.BlockSpec(memory_space=pltpu.VMEM)
    return pl.pallas_call(
        statistic_kernel,
        out_shape=(
            jax.ShapeDtypeStruct((count * rows, templates), jnp.float32),
            jax.ShapeDtypeStruct((count, rows), jnp.float32),
        ),
        in_specs=[vmem] * 5,
        out_specs=(vmem, vmem),
        compiler_params=pltpu.CompilerParams(vmem_limit_bytes=32 * 1024 * 1024),
        cost_estimate=pl.CostEstimate(flops=400_000_000, bytes_accessed=4_000_000, transcendentals=0),
        name="statistic",
    )(windows, mask, weigh, coef, kernel)


def across(values, axis, distance):
    return lax.ppermute(values, axis, [(n, n ^ distance) for n in range(lax.axis_size(axis))])


def bits(axis):
    return [1 << n for n in range(lax.axis_size(axis).bit_length() - 1)]


def body(spectra, offsets, fractions, antenna, starts, durations):
    bands, cores = lax.axis_size("tmpl"), lax.axis_size("tm")
    sft_rows = spectra.shape[0]
    grid_size = starts.shape[0]
    my_rows = grid_size // cores
    me = lax.axis_index("tmpl").astype(jnp.int32)[None]
    offset_parts = [offsets.T]
    for bit in bits("tmpl"):
        known = offset_parts[0] if len(offset_parts) == 1 else jnp.concatenate(offset_parts, axis=0)
        offset_parts = [known, across(known, "tmpl", bit)]
    spec = jnp.transpose(spectra, (1, 0, 2)).astype(jnp.float32)
    my_durations = lax.dynamic_slice_in_dim(durations, lax.axis_index("tm") * my_rows, my_rows, 0)
    prepared = prepare(my_durations, starts, antenna, fractions)
    windows = pick(me, offset_parts, spec, bands, cores).reshape(cores * bands, sft_rows, LANES)
    arrived = lax.all_to_all(windows, ("tm", "tmpl"), split_axis=0, concat_axis=0, tiled=True)
    arrived = arrived.reshape(cores * bands * sft_rows, LANES)
    fstat_map, loudest = statistic(arrived, *prepared, grid_size)
    for bit in bits("tmpl"):
        loudest = jnp.maximum(loudest, across(loudest, "tmpl", bit))
    return (fstat_map.reshape(my_rows, grid_size, -1), loudest)


def solution(mesh):
    in_specs = (
        P(("grp", "tm", "tmpl"), None, None),
        P(("grp", "tm"), "tmpl"),
        P(("grp", "tmpl")),
        P("grp", None),
        P("grp"),
        P("grp"),
    )
    out_specs = (P("tm", None, ("grp", "tmpl")), P(("grp", "tm"), None))
    return jax.shard_map(body, mesh=mesh, in_specs=in_specs, out_specs=out_specs, check_vma=False)
```

```python
import functools

import jax
import jax.numpy as jnp
from jax import lax
from jax.experimental import pallas as pl
from jax.experimental.pallas import tpu as pltpu
from jax.sharding import PartitionSpec as P

W = 16
LANES = 128
NT = (((1,), (1,)), ((), ()))


def iota(shape, axis):
    return lax.broadcasted_iota(jnp.int32, shape, axis)


def pick_kernel(bands, band_width, me_ref, *refs):
    *offset_refs, spec_ref, out_ref, high_ref, low_ref, turn_ref = refs
    me = me_ref[0]
    rows = spec_ref.shape[0]
    groups = rows // 8
    sft_count = offset_refs[0].shape[1]
    blocks = sum(ref.shape[0] for ref in offset_refs) // bands
    chunks = band_width // LANES
    width = blocks * W
    offsets = jnp.concatenate([ref[...] for ref in offset_refs], axis=0)
    count = bands * blocks
    shape = (32, sft_count)
    wanted = [iota(shape, 1) == iota(shape, 0) // 4 + (me * rows + group * 8) for group in range(groups)]
    wanted = [one.astype(jnp.bfloat16) for one in wanted]
    shape = (groups * count, bands * LANES)
    source, target = iota(shape, 0), iota(shape, 1)
    source_band = ((source % count) // blocks) ^ me
    held = (target // LANES == source_band) & ((target // width) % (LANES // width) == source // count)
    spread = (held & ((target // W) % blocks == source % blocks)).astype(jnp.bfloat16)

    def lay_out(values, ref):
        values = values.astype(jnp.float32).astype(jnp.bfloat16)
        own = [lax.dot_general(one, values, NT, preferred_element_type=jnp.float32) for one in wanted]
        own = jnp.concatenate(own, axis=1).astype(jnp.bfloat16)
        ref[...] = jnp.dot(own, spread, preferred_element_type=jnp.float32).astype(jnp.int32)

    lay_out(offsets // LANES, high_ref)
    lay_out(offsets % LANES, low_ref)
    lane = iota((8, LANES), 1)
    shift = lane % W
    lane_group = lane // width
    bands_per_step = max(1, 16 // rows)

    def step(index, carry):
        tiles = []
        for inner in range(bands_per_step):
            band = index * bands_per_step + inner
            at_lane = pl.ds(pl.multiple_of(band * LANES, LANES), LANES)
            for pair in range(4):
                at_row = pl.ds(pair * 8, 8)
                place = low_ref[at_row, at_lane] + shift
                lane_id = place % LANES
                chosen = high_ref[at_row, at_lane] + place // LANES + lane_group * chunks
                tile = jnp.zeros((8, LANES), jnp.float32)
                for group in range(groups):
                    for chunk in range(chunks):
                        start = pl.multiple_of(band * band_width + chunk * LANES, LANES)
                        values = spec_ref[pl.ds(group * 8 + pair * 2, 2), :, pl.ds(start, LANES)]
                        values = values.astype(jnp.float32).reshape(8, LANES)
                        moved = jnp.take_along_axis(values, lane_id, axis=1, mode="promise_in_bounds")
                        tile = jnp.where(chosen == group * chunks + chunk, moved, tile)
                turn_ref[inner, at_row, :] = tile
            parts = [turn_ref[inner, pl.ds(part, 8, stride=4), :] for part in range(4)]
            for group in range(groups):
                tile = jnp.zeros((8, LANES), jnp.float32)
                for part in range(4):
                    amount = (part - group) * width % LANES
                    turned = pltpu.roll(parts[part], amount, 1) if amount else parts[part]
                    tile = jnp.where(lane_group == part, turned, tile)
                tiles.append(tile)
        total = len(tiles) * 8
        tiles = jnp.concatenate(tiles, axis=0).astype(jnp.bfloat16)
        for core in range(out_ref.shape[0]):
            out_ref[core, pl.ds(pl.multiple_of(index * total, total), total), :] = tiles
        return carry

    lax.fori_loop(0, bands // bands_per_step, step, 0)


def pick(me, offset_parts, spec, bands, cores):
    rows = spec.shape[0]
    band_width = spec.shape[2] // bands
    vmem = pl.BlockSpec(memory_space=pltpu.VMEM)
    return pl.pallas_call(
        functools.partial(pick_kernel, bands, band_width),
        out_shape=jax.ShapeDtypeStruct((cores, bands * rows, LANES), jnp.bfloat16),
        in_specs=[pl.BlockSpec(memory_space=pltpu.SMEM)] + [vmem] * (len(offset_parts) + 1),
        out_specs=vmem,
        scratch_shapes=[
            pltpu.VMEM((32, bands * LANES), jnp.int32),
            pltpu.VMEM((32, bands * LANES), jnp.int32),
            pltpu.VMEM((max(1, 16 // rows), 32, LANES), jnp.float32),
        ],
        compiler_params=pltpu.CompilerParams(vmem_limit_bytes=32 * 1024 * 1024),
        cost_estimate=pl.CostEstimate(flops=10_000_000, bytes_accessed=2 * spec.size, transcendentals=0),
        name="pick",
    )(me, *offset_parts, spec)


def split(values, count):
    parts = []
    for _ in range(count):
        part = values.astype(jnp.bfloat16)
        parts.append(part)
        values = values - part.astype(jnp.float32)
    return parts


def prepare_kernel(durations_ref, starts_ref, antenna_ref, fractions_ref, mask_ref, weigh_ref, coef_ref, kernel_ref):
    rows = starts_ref.shape[0]
    count = durations_ref.shape[0]
    sfts = antenna_ref.shape[1]
    sft = iota((rows, sfts), 1)
    start = starts_ref[:, 0:1]
    after = sft >= start
    for j in range(count):
        inside = after & (sft < start + durations_ref[j])
        mask_ref[pl.ds(j * rows, rows), :] = jnp.where(inside, 1.0, 0.0).astype(jnp.bfloat16)
    antenna = antenna_ref[...]
    a1, a2, b1, b2 = (antenna[n : n + 1] for n in range(4))
    terms = jnp.concatenate([a1 * a1 + a2 * a2, b1 * b1 + b2 * b2, a1 * b1 + a2 * b2, jnp.zeros((5, sfts), jnp.float32)], axis=0)
    weights = sum(lax.dot_general(mask_ref[...], part, NT, preferred_element_type=jnp.float32) for part in split(terms, 3))
    wa, wb, wc = (weights[:, n : n + 1] for n in range(3))
    shape = (rows * count, LANES)
    late = iota(shape, 1) >= LANES // 2
    coef_ref[0] = jnp.broadcast_to(1.0 / wa, shape)
    coef_ref[1] = jnp.broadcast_to(wa / (wa * wb - wc * wc), shape)
    coef_ref[2] = jnp.where(late, jnp.broadcast_to(wc / wa, shape), 0.0)
    upright = jnp.transpose(jnp.concatenate([antenna, jnp.zeros((LANES - 4, sfts), jnp.float32)], axis=0))
    shape = (sfts, LANES)
    late = iota(shape, 1) >= LANES // 2
    weigh_ref[0] = jnp.where(late, upright[:, 3:4], upright[:, 0:1])
    weigh_ref[1] = jnp.where(late, upright[:, 2:3], upright[:, 1:2])
    fractions = fractions_ref[...]
    templates = fractions.shape[1]
    blocks = kernel_ref.shape[1] // (4 * LANES)
    bin_id = iota((W, templates), 0)
    distance = fractions + (W // 2 - 1) - bin_id.astype(jnp.float32)
    alternate = 1.0 - 2.0 * (bin_id % 2).astype(jnp.float32)
    values = (alternate * jnp.sin(jnp.pi * fractions) / (jnp.pi * distance)).astype(jnp.bfloat16)
    kernel_ref[...] = jnp.zeros_like(kernel_ref)
    for part in range(2):
        for c in range(4):
            for b in range(blocks):
                row = ((part * 4 + c) * blocks + b) * W
                column = (c * blocks + b) * LANES
                kernel_ref[pl.ds(row, W), pl.ds(column, LANES)] = values[:, b * LANES : (b + 1) * LANES]


def prepare(durations, starts, antenna, fractions):
    count, rows, sfts = durations.shape[0], starts.shape[0], antenna.shape[0]
    columns = 4 * fractions.shape[0]
    features = 4 * W * (fractions.shape[0] // LANES)
    vmem = pl.BlockSpec(memory_space=pltpu.VMEM)
    return pl.pallas_call(
        prepare_kernel,
        out_shape=(
            jax.ShapeDtypeStruct((count * rows, sfts), jnp.bfloat16),
            jax.ShapeDtypeStruct((2, sfts, LANES), jnp.float32),
            jax.ShapeDtypeStruct((3, count * rows, LANES), jnp.float32),
            jax.ShapeDtypeStruct((2 * features, columns), jnp.bfloat16),
        ),
        in_specs=[pl.BlockSpec(memory_space=pltpu.SMEM), vmem, vmem, vmem],
        out_specs=(vmem,) * 4,
        compiler_params=pltpu.CompilerParams(vmem_limit_bytes=32 * 1024 * 1024),
        cost_estimate=pl.CostEstimate(flops=100_000_000, bytes_accessed=4_000_000, transcendentals=0),
        name="prepare",
    )(durations, jnp.broadcast_to(starts[:, None], (rows, LANES)), antenna.T, fractions[None, :])


def statistic_kernel(windows_ref, mask_ref, weigh_ref, coef_ref, kernel_ref, map_ref, loudest_ref):
    values = windows_ref[...].astype(jnp.float32)
    half = LANES // 2
    weighted = (weigh_ref[0] * values + weigh_ref[1] * pltpu.roll(values, half, 1)).astype(jnp.bfloat16)
    templates = map_ref.shape[1]
    rows = loudest_ref.shape[1]
    per_step = LANES // rows
    for step in range(map_ref.shape[0] // LANES):
        here = pl.ds(step * LANES, LANES)
        sums = jnp.dot(mask_ref[here, :], weighted, preferred_element_type=jnp.float32)
        sums = sums - coef_ref[2, here, :] * pltpu.roll(sums, half, 1)
        parts = jnp.concatenate(split(sums, 2), axis=1)
        found = jnp.dot(parts, kernel_ref[...], preferred_element_type=jnp.float32)
        ra, ia, rb, ib = (found[:, c * templates : (c + 1) * templates] for c in range(4))
        power_a, power_b = ra * ra + ia * ia, rb * rb + ib * ib
        best = None
        for b in range(templates // LANES):
            columns = slice(b * LANES, (b + 1) * LANES)
            result = coef_ref[0, here, :] * power_a[:, columns] + coef_ref[1, here, :] * power_b[:, columns]
            map_ref[here, columns] = result
            best = result if best is None else jnp.maximum(best, result)
        best = jnp.max(jnp.transpose(best), axis=0, keepdims=True)
        for n in range(per_step):
            turned = best if n == 0 else pltpu.roll(best, LANES - n * rows, 1)
            loudest_ref[pl.ds(step * per_step + n, 1), :] = turned[:, :rows]


def statistic(windows, mask, weigh, coef, kernel, rows):
    count = mask.shape[0] // rows
    templates = kernel.shape[1] // 4
    vmem = pl.BlockSpec(memory_space=pltpu.VMEM)
    return pl.pallas_call(
        statistic_kernel,
        out_shape=(
            jax.ShapeDtypeStruct((count * rows, templates), jnp.float32),
            jax.ShapeDtypeStruct((count, rows), jnp.float32),
        ),
        in_specs=[vmem] * 5,
        out_specs=(vmem, vmem),
        compiler_params=pltpu.CompilerParams(vmem_limit_bytes=32 * 1024 * 1024),
        cost_estimate=pl.CostEstimate(flops=400_000_000, bytes_accessed=4_000_000, transcendentals=0),
        name="statistic",
    )(windows, mask, weigh, coef, kernel)


def across(values, axis, distance):
    return lax.ppermute(values, axis, [(n, n ^ distance) for n in range(lax.axis_size(axis))])


def bits(axis):
    return [1 << n for n in range(lax.axis_size(axis).bit_length() - 1)]


def body(spectra, offsets, fractions, antenna, starts, durations):
    bands, cores = lax.axis_size("tmpl"), lax.axis_size("tm")
    sft_rows = spectra.shape[0]
    grid_size = starts.shape[0]
    my_rows = grid_size // cores
    me = lax.axis_index("tmpl").astype(jnp.int32)[None]
    offset_parts = [offsets.T]
    for bit in bits("tmpl"):
        known = offset_parts[0] if len(offset_parts) == 1 else jnp.concatenate(offset_parts, axis=0)
        offset_parts = [known, across(known, "tmpl", bit)]
    my_durations = lax.dynamic_slice_in_dim(durations, lax.axis_index("tm") * my_rows, my_rows, 0)
    prepared = prepare(my_durations, starts, antenna, fractions)
    windows = pick(me, offset_parts, spectra, bands, cores).reshape(cores * bands, sft_rows, LANES)
    arrived = lax.all_to_all(windows, ("tm", "tmpl"), split_axis=0, concat_axis=0, tiled=True)
    arrived = arrived.reshape(cores * bands * sft_rows, LANES)
    fstat_map, loudest = statistic(arrived, *prepared, grid_size)
    for bit in bits("tmpl"):
        loudest = jnp.maximum(loudest, across(loudest, "tmpl", bit))
    return (fstat_map.reshape(my_rows, grid_size, -1), loudest)


def solution(mesh):
    in_specs = (
        P(("grp", "tm", "tmpl"), None, None),
        P(("grp", "tm"), "tmpl"),
        P(("grp", "tmpl")),
        P("grp", None),
        P("grp"),
        P("grp"),
    )
    out_specs = (P("tm", None, ("grp", "tmpl")), P(("grp", "tm"), None))
    return jax.shard_map(body, mesh=mesh, in_specs=in_specs, out_specs=out_specs, check_vma=False)
```

```python
import functools

import jax
import jax.numpy as jnp
from jax import lax
from jax.experimental import pallas as pl
from jax.experimental.pallas import tpu as pltpu
from jax.sharding import PartitionSpec as P

W = 16
LANES = 128
NT = (((1,), (1,)), ((), ()))


def iota(shape, axis):
    return lax.broadcasted_iota(jnp.int32, shape, axis)


def lay_rows_kernel(spec_ref, out_ref):
    rows, _, bins = spec_ref.shape
    width = min(bins, 2048)

    def step(pair, carry):
        here = pl.ds(pl.multiple_of(pair * 8, 8), 8)
        for start in range(0, bins, width):
            values = spec_ref[pl.ds(pair * 2, 2), :, start : start + width].astype(jnp.float32)
            out_ref[here, start : start + width] = values.reshape(8, width)
        return carry

    lax.fori_loop(0, rows // 2, step, 0)


def lay_rows(spectra):
    rows, components, bins = spectra.shape
    vmem = pl.BlockSpec(memory_space=pltpu.VMEM)
    return pl.pallas_call(
        lay_rows_kernel,
        out_shape=jax.ShapeDtypeStruct((rows * components, bins), jnp.float32),
        in_specs=[vmem],
        out_specs=vmem,
        compiler_params=pltpu.CompilerParams(vmem_limit_bytes=32 * 1024 * 1024),
        cost_estimate=pl.CostEstimate(flops=spectra.size, bytes_accessed=6 * spectra.size, transcendentals=0),
        name="lay_rows",
    )(spectra)


def pick_kernel(bands, band_width, me_ref, offset_ref, spec_ref, out_ref, high_ref, low_ref, turn_ref):
    me = me_ref[0]
    rows = spec_ref.shape[0] // 4
    groups = rows // 8
    blocks, sft_count = offset_ref.shape[1:]
    chunks = band_width // LANES
    width = blocks * W
    offsets = jnp.concatenate([offset_ref[band] for band in range(bands)], axis=0)
    count = bands * blocks
    shape = (32, sft_count)
    wanted = [iota(shape, 1) == iota(shape, 0) // 4 + (me * rows + group * 8) for group in range(groups)]
    wanted = [one.astype(jnp.bfloat16) for one in wanted]
    shape = (groups * count, bands * LANES)
    source, target = iota(shape, 0), iota(shape, 1)
    held = (target // LANES == (source % count) // blocks) & ((target // width) % (LANES // width) == source // count)
    spread = (held & ((target // W) % blocks == source % blocks)).astype(jnp.bfloat16)

    def lay_out(values, ref):
        values = values.astype(jnp.float32).astype(jnp.bfloat16)
        own = [lax.dot_general(one, values, NT, preferred_element_type=jnp.float32) for one in wanted]
        own = jnp.concatenate(own, axis=1).astype(jnp.bfloat16)
        ref[...] = jnp.dot(own, spread, preferred_element_type=jnp.float32).astype(jnp.int32)

    lay_out(offsets // LANES, high_ref)
    lay_out(offsets % LANES, low_ref)
    lane = iota((8, LANES), 1)
    shift = lane % W
    lane_group = lane // width
    bands_per_step = max(1, 16 // rows)

    def step(index, carry):
        tiles = []
        for inner in range(bands_per_step):
            band = index * bands_per_step + inner
            at_lane = pl.ds(pl.multiple_of(band * LANES, LANES), LANES)
            for pair in range(4):
                at_row = pl.ds(pair * 8, 8)
                place = low_ref[at_row, at_lane] + shift
                lane_id = place % LANES
                chosen = high_ref[at_row, at_lane] + place // LANES + lane_group * chunks
                tile = jnp.zeros((8, LANES), jnp.float32)
                for group in range(groups):
                    for chunk in range(chunks):
                        start = pl.multiple_of(band * band_width + chunk * LANES, LANES)
                        values = spec_ref[pl.ds((group * 4 + pair) * 8, 8), pl.ds(start, LANES)]
                        moved = jnp.take_along_axis(values, lane_id, axis=1, mode="promise_in_bounds")
                        tile = jnp.where(chosen == group * chunks + chunk, moved, tile)
                turn_ref[inner, at_row, :] = tile
            parts = [turn_ref[inner, pl.ds(part, 8, stride=4), :] for part in range(4)]
            for group in range(groups):
                tile = jnp.zeros((8, LANES), jnp.float32)
                for part in range(4):
                    amount = (part - group) * width % LANES
                    turned = pltpu.roll(parts[part], amount, 1) if amount else parts[part]
                    tile = jnp.where(lane_group == part, turned, tile)
                tiles.append(tile)
        total = len(tiles) * 8
        tiles = jnp.concatenate(tiles, axis=0).astype(jnp.bfloat16)
        for core in range(out_ref.shape[0]):
            out_ref[core, pl.ds(pl.multiple_of(index * total, total), total), :] = tiles
        return carry

    lax.fori_loop(0, bands // bands_per_step, step, 0)


def pick(me, offsets, spec, bands, cores):
    rows = spec.shape[0] // 4
    band_width = spec.shape[1] // bands
    vmem = pl.BlockSpec(memory_space=pltpu.VMEM)
    return pl.pallas_call(
        functools.partial(pick_kernel, bands, band_width),
        out_shape=jax.ShapeDtypeStruct((cores, bands * rows, LANES), jnp.bfloat16),
        in_specs=[pl.BlockSpec(memory_space=pltpu.SMEM), vmem, vmem],
        out_specs=vmem,
        scratch_shapes=[
            pltpu.VMEM((32, bands * LANES), jnp.int32),
            pltpu.VMEM((32, bands * LANES), jnp.int32),
            pltpu.VMEM((max(1, 16 // rows), 32, LANES), jnp.float32),
        ],
        compiler_params=pltpu.CompilerParams(vmem_limit_bytes=32 * 1024 * 1024),
        cost_estimate=pl.CostEstimate(flops=10_000_000, bytes_accessed=4 * spec.size, transcendentals=0),
        name="pick",
    )(me, offsets, spec)


def split(values, count):
    parts = []
    for _ in range(count):
        part = values.astype(jnp.bfloat16)
        parts.append(part)
        values = values - part.astype(jnp.float32)
    return parts


def prepare_kernel(durations_ref, starts_ref, antenna_ref, fractions_ref, mask_ref, weigh_ref, coef_ref, kernel_ref):
    rows = starts_ref.shape[0]
    count = durations_ref.shape[0]
    sfts = antenna_ref.shape[1]
    sft = iota((rows, sfts), 1)
    start = starts_ref[:, 0:1]
    after = sft >= start
    for j in range(count):
        inside = after & (sft < start + durations_ref[j])
        mask_ref[pl.ds(j * rows, rows), :] = jnp.where(inside, 1.0, 0.0).astype(jnp.bfloat16)
    antenna = antenna_ref[...]
    a1, a2, b1, b2 = (antenna[n : n + 1] for n in range(4))
    terms = jnp.concatenate([a1 * a1 + a2 * a2, b1 * b1 + b2 * b2, a1 * b1 + a2 * b2, jnp.zeros((5, sfts), jnp.float32)], axis=0)
    weights = sum(lax.dot_general(mask_ref[...], part, NT, preferred_element_type=jnp.float32) for part in split(terms, 3))
    wa, wb, wc = (weights[:, n : n + 1] for n in range(3))
    shape = (rows * count, LANES)
    late = iota(shape, 1) >= LANES // 2
    coef_ref[0] = jnp.broadcast_to(1.0 / wa, shape)
    coef_ref[1] = jnp.broadcast_to(wa / (wa * wb - wc * wc), shape)
    coef_ref[2] = jnp.where(late, jnp.broadcast_to(wc / wa, shape), 0.0)
    upright = jnp.transpose(jnp.concatenate([antenna, jnp.zeros((LANES - 4, sfts), jnp.float32)], axis=0))
    shape = (sfts, LANES)
    late = iota(shape, 1) >= LANES // 2
    weigh_ref[0] = jnp.where(late, upright[:, 3:4], upright[:, 0:1])
    weigh_ref[1] = jnp.where(late, upright[:, 2:3], upright[:, 1:2])
    fractions = fractions_ref[...]
    templates = fractions.shape[1]
    blocks = kernel_ref.shape[1] // (4 * LANES)
    bin_id = iota((W, templates), 0)
    distance = fractions + (W // 2 - 1) - bin_id.astype(jnp.float32)
    alternate = 1.0 - 2.0 * (bin_id % 2).astype(jnp.float32)
    values = (alternate * jnp.sin(jnp.pi * fractions) / (jnp.pi * distance)).astype(jnp.bfloat16)
    kernel_ref[...] = jnp.zeros_like(kernel_ref)
    for part in range(2):
        for c in range(4):
            for b in range(blocks):
                row = ((part * 4 + c) * blocks + b) * W
                column = (c * blocks + b) * LANES
                kernel_ref[pl.ds(row, W), pl.ds(column, LANES)] = values[:, b * LANES : (b + 1) * LANES]


def prepare(durations, starts, antenna, fractions):
    count, rows, sfts = durations.shape[0], starts.shape[0], antenna.shape[0]
    columns = 4 * fractions.shape[0]
    features = 4 * W * (fractions.shape[0] // LANES)
    vmem = pl.BlockSpec(memory_space=pltpu.VMEM)
    return pl.pallas_call(
        prepare_kernel,
        out_shape=(
            jax.ShapeDtypeStruct((count * rows, sfts), jnp.bfloat16),
            jax.ShapeDtypeStruct((2, sfts, LANES), jnp.float32),
            jax.ShapeDtypeStruct((3, count * rows, LANES), jnp.float32),
            jax.ShapeDtypeStruct((2 * features, columns), jnp.bfloat16),
        ),
        in_specs=[pl.BlockSpec(memory_space=pltpu.SMEM), vmem, vmem, vmem],
        out_specs=(vmem,) * 4,
        compiler_params=pltpu.CompilerParams(vmem_limit_bytes=32 * 1024 * 1024),
        cost_estimate=pl.CostEstimate(flops=100_000_000, bytes_accessed=4_000_000, transcendentals=0),
        name="prepare",
    )(durations, jnp.broadcast_to(starts[:, None], (rows, LANES)), antenna.T, fractions[None, :])


def statistic_kernel(windows_ref, mask_ref, weigh_ref, coef_ref, kernel_ref, map_ref, loudest_ref):
    values = windows_ref[...].astype(jnp.float32)
    half = LANES // 2
    weighted = (weigh_ref[0] * values + weigh_ref[1] * pltpu.roll(values, half, 1)).astype(jnp.bfloat16)
    templates = map_ref.shape[1]
    rows = map_ref.shape[0] // loudest_ref.shape[1]
    copies = loudest_ref.shape[0]
    per_step = LANES // rows
    for step in range(map_ref.shape[0] // LANES):
        here = pl.ds(step * LANES, LANES)
        sums = jnp.dot(mask_ref[here, :], weighted, preferred_element_type=jnp.float32)
        sums = sums - coef_ref[2, here, :] * pltpu.roll(sums, half, 1)
        parts = jnp.concatenate(split(sums, 2), axis=1)
        found = jnp.dot(parts, kernel_ref[...], preferred_element_type=jnp.float32)
        ra, ia, rb, ib = (found[:, c * templates : (c + 1) * templates] for c in range(4))
        power_a, power_b = ra * ra + ia * ia, rb * rb + ib * ib
        best = None
        for b in range(templates // LANES):
            columns = slice(b * LANES, (b + 1) * LANES)
            result = coef_ref[0, here, :] * power_a[:, columns] + coef_ref[1, here, :] * power_b[:, columns]
            map_ref[here, columns] = result
            best = result if best is None else jnp.maximum(best, result)
        best = jnp.max(jnp.transpose(best), axis=0, keepdims=True)
        for n in range(per_step):
            turned = best if n == 0 else pltpu.roll(best, LANES - n * rows, 1)
            for copy in range(copies):
                loudest_ref[copy, pl.ds(step * per_step + n, 1), :] = turned


def statistic(windows, mask, weigh, coef, kernel, rows, copies):
    count = mask.shape[0] // rows
    templates = kernel.shape[1] // 4
    vmem = pl.BlockSpec(memory_space=pltpu.VMEM)
    return pl.pallas_call(
        statistic_kernel,
        out_shape=(
            jax.ShapeDtypeStruct((count * rows, templates), jnp.float32),
            jax.ShapeDtypeStruct((copies, count, LANES), jnp.float32),
        ),
        in_specs=[vmem] * 5,
        out_specs=(vmem, vmem),
        compiler_params=pltpu.CompilerParams(vmem_limit_bytes=32 * 1024 * 1024),
        cost_estimate=pl.CostEstimate(flops=400_000_000, bytes_accessed=4_000_000, transcendentals=0),
        name="statistic",
    )(windows, mask, weigh, coef, kernel)


def to_all(values, axis):
    copies = jnp.broadcast_to(values[None], (lax.axis_size(axis),) + values.shape)
    return lax.all_to_all(copies, axis, split_axis=0, concat_axis=0, tiled=True)


def body(spectra, offsets, fractions, antenna, starts, durations):
    bands, cores = lax.axis_size("tmpl"), lax.axis_size("tm")
    sft_rows = spectra.shape[0]
    grid_size = starts.shape[0]
    my_rows = grid_size // cores
    me = lax.axis_index("tmpl").astype(jnp.int32)[None]
    known = to_all(offsets.T, "tmpl")
    spec = lay_rows(spectra)
    my_durations = lax.dynamic_slice_in_dim(durations, lax.axis_index("tm") * my_rows, my_rows, 0)
    windows = pick(me, known, spec, bands, cores).reshape(cores * bands, sft_rows, LANES)
    windows, my_durations = lax.optimization_barrier((windows, my_durations))
    prepared = prepare(my_durations, starts, antenna, fractions)
    arrived = lax.all_to_all(windows, ("tm", "tmpl"), split_axis=0, concat_axis=0, tiled=True)
    arrived = arrived.reshape(cores * bands * sft_rows, LANES)
    fstat_map, loudest = statistic(arrived, *prepared, grid_size, bands)
    loudest = lax.all_to_all(loudest, "tmpl", split_axis=0, concat_axis=0, tiled=True)
    loudest = jnp.max(loudest[:, :, :grid_size], axis=0)
    return (fstat_map.reshape(my_rows, grid_size, -1), loudest)


def solution(mesh):
    in_specs = (
        P(("grp", "tm", "tmpl"), None, None),
        P(("grp", "tm"), "tmpl"),
        P(("grp", "tmpl")),
        P("grp", None),
        P("grp"),
        P("grp"),
    )
    out_specs = (P("tm", None, ("grp", "tmpl")), P(("grp", "tm"), None))
    return jax.shard_map(body, mesh=mesh, in_specs=in_specs, out_specs=out_specs, check_vma=False)
```

```python
import functools

import jax
import jax.numpy as jnp
from jax import lax
from jax.experimental import pallas as pl
from jax.experimental.pallas import tpu as pltpu
from jax.sharding import PartitionSpec as P

W = 16
LANES = 128
NT = (((1,), (1,)), ((), ()))


def iota(shape, axis):
    return lax.broadcasted_iota(jnp.int32, shape, axis)


def pick_kernel(me_ref, offset_ref, spec_ref, out_ref, held_ref, place_ref, turn_ref, tile_ref, in_sems, out_sems):
    rows, _, bins = spec_ref.shape
    bands, blocks, _ = offset_ref.shape
    cores = out_ref.shape[0]
    band_width = bins // bands
    groups = rows // 8
    chunks = band_width // LANES
    width = blocks * W
    steps = in_sems.shape[0]
    bands_per_step = bands // steps
    count = bands_per_step * rows

    def copy_in(index):
        columns = pl.ds(pl.multiple_of(index * (bands_per_step * band_width), LANES), bands_per_step * band_width)
        return pltpu.make_async_copy(spec_ref.at[:, :, columns], held_ref.at[:, :, columns], in_sems.at[index])

    def copy_out(index, core):
        here = pl.ds(pl.multiple_of(index * count, count), count)
        return pltpu.make_async_copy(tile_ref.at[here, :], out_ref.at[core, here, :], out_sems.at[index, core])

    for index in range(steps):
        copy_in(index).start()
    first = me_ref[0] * rows
    columns = pl.ds(pl.multiple_of(first // LANES * LANES, LANES), LANES)
    offsets = jnp.concatenate([offset_ref[band, :, columns] for band in range(bands)], axis=0).astype(jnp.float32)
    lane = iota(offsets.shape, 1)
    offsets = jnp.take_along_axis(offsets, (lane >> 2) + first & (LANES - 1), axis=1, mode="promise_in_bounds")
    offsets = jnp.concatenate([offsets, jnp.zeros((LANES - bands * blocks, LANES), jnp.float32)], axis=0)
    upright = jnp.transpose(offsets).astype(jnp.int32)
    lane = iota((32, LANES), 1)
    places = upright[0:32]
    for group in range(1, groups):
        turned = pltpu.roll(upright[group * 32 : group * 32 + 32], group * bands * blocks, 1)
        places = jnp.where(lane < group * bands * blocks, places, turned)
    place_ref[...] = places
    lane = iota((8, LANES), 1)
    shift = lane & (W - 1)
    lane_group = lane // width
    source = lane_group * (bands * blocks) + lane // W % blocks

    def step(index, carry):
        copy_in(index).wait()
        tiles = []
        for inner in range(bands_per_step):
            band = index * bands_per_step + inner
            for pair in range(4):
                at_row = pl.ds(pair * 8, 8)
                place = jnp.take_along_axis(place_ref[at_row, :], source + band * blocks, axis=1, mode="promise_in_bounds") + shift
                lane_id = place & (LANES - 1)
                chosen = (place >> 7) + lane_group * chunks
                tile = jnp.zeros((8, LANES), jnp.float32)
                for group in range(groups):
                    for chunk in range(chunks):
                        start = pl.multiple_of(band * band_width + chunk * LANES, LANES)
                        values = held_ref[pl.ds(group * 8 + pair * 2, 2), :, pl.ds(start, LANES)]
                        values = values.astype(jnp.float32).reshape(8, LANES)
                        moved = jnp.take_along_axis(values, lane_id, axis=1, mode="promise_in_bounds")
                        tile = jnp.where(chosen == group * chunks + chunk, moved, tile)
                turn_ref[inner, at_row, :] = tile
            parts = [turn_ref[inner, pl.ds(part, 8, stride=4), :] for part in range(4)]
            for group in range(groups):
                tile = jnp.zeros((8, LANES), jnp.float32)
                for part in range(4):
                    amount = (part - group) * width % LANES
                    turned = pltpu.roll(parts[part], amount, 1) if amount else parts[part]
                    tile = jnp.where(lane_group == part, turned, tile)
                tiles.append(tile)
        tile_ref[pl.ds(pl.multiple_of(index * count, count), count), :] = jnp.concatenate(tiles, axis=0).astype(jnp.bfloat16)
        for core in range(cores):
            copy_out(index, core).start()
        return carry

    lax.fori_loop(0, steps, step, 0)
    for index in range(steps):
        for core in range(cores):
            copy_out(index, core).wait()


def pick(me, offsets, spectra, cores):
    rows, bands = spectra.shape[0], offsets.shape[0]
    bands_per_step = max(1, 16 // rows)
    steps = bands // bands_per_step
    return pl.pallas_call(
        pick_kernel,
        out_shape=jax.ShapeDtypeStruct((cores, bands * rows, LANES), jnp.bfloat16),
        in_specs=[
            pl.BlockSpec(memory_space=pltpu.SMEM),
            pl.BlockSpec(memory_space=pltpu.VMEM),
            pl.BlockSpec(memory_space=pl.ANY),
        ],
        out_specs=pl.BlockSpec(memory_space=pl.ANY),
        scratch_shapes=[
            pltpu.VMEM(spectra.shape, jnp.bfloat16),
            pltpu.VMEM((32, LANES), jnp.int32),
            pltpu.VMEM((bands_per_step, 32, LANES), jnp.float32),
            pltpu.VMEM((bands * rows, LANES), jnp.bfloat16),
            pltpu.SemaphoreType.DMA((steps,)),
            pltpu.SemaphoreType.DMA((steps, cores)),
        ],
        cost_estimate=pl.CostEstimate(flops=10_000_000, bytes_accessed=2 * spectra.size, transcendentals=0),
        name="pick",
    )(me, offsets, spectra)


def split(values, count):
    parts = []
    for _ in range(count):
        part = values.astype(jnp.bfloat16)
        parts.append(part)
        values = values - part.astype(jnp.float32)
    return parts


def prepare_kernel(durations_ref, starts_ref, antenna_ref, fractions_ref, mask_ref, weigh_ref, coef_ref, kernel_ref):
    rows = starts_ref.shape[0]
    count = durations_ref.shape[0]
    sfts = antenna_ref.shape[1]
    sft = iota((rows, sfts), 1)
    start = starts_ref[:, 0:1]
    after = sft >= start
    for j in range(count):
        inside = after & (sft < start + durations_ref[j])
        mask_ref[pl.ds(j * rows, rows), :] = jnp.where(inside, 1.0, 0.0).astype(jnp.bfloat16)
    antenna = antenna_ref[...]
    a1, a2, b1, b2 = (antenna[n : n + 1] for n in range(4))
    terms = jnp.concatenate([a1 * a1 + a2 * a2, b1 * b1 + b2 * b2, a1 * b1 + a2 * b2, jnp.zeros((5, sfts), jnp.float32)], axis=0)
    weights = sum(lax.dot_general(mask_ref[...], part, NT, preferred_element_type=jnp.float32) for part in split(terms, 3))
    wa, wb, wc = (weights[:, n : n + 1] for n in range(3))
    shape = (rows * count, LANES)
    late = iota(shape, 1) >= LANES // 2
    coef_ref[0] = jnp.broadcast_to(1.0 / wa, shape)
    coef_ref[1] = jnp.broadcast_to(wa / (wa * wb - wc * wc), shape)
    coef_ref[2] = jnp.where(late, jnp.broadcast_to(wc / wa, shape), 0.0)
    upright = jnp.transpose(jnp.concatenate([antenna, jnp.zeros((LANES - 4, sfts), jnp.float32)], axis=0))
    shape = (sfts, LANES)
    late = iota(shape, 1) >= LANES // 2
    weigh_ref[0] = jnp.where(late, upright[:, 3:4], upright[:, 0:1])
    weigh_ref[1] = jnp.where(late, upright[:, 2:3], upright[:, 1:2])
    fractions = fractions_ref[...]
    templates = fractions.shape[1]
    blocks = kernel_ref.shape[1] // (4 * LANES)
    bin_id = iota((W, templates), 0)
    distance = fractions + (W // 2 - 1) - bin_id.astype(jnp.float32)
    alternate = 1.0 - 2.0 * (bin_id % 2).astype(jnp.float32)
    values = (alternate * jnp.sin(jnp.pi * fractions) / (jnp.pi * distance)).astype(jnp.bfloat16)
    kernel_ref[...] = jnp.zeros_like(kernel_ref)
    for part in range(2):
        for c in range(4):
            for b in range(blocks):
                row = ((part * 4 + c) * blocks + b) * W
                column = (c * blocks + b) * LANES
                kernel_ref[pl.ds(row, W), pl.ds(column, LANES)] = values[:, b * LANES : (b + 1) * LANES]


def prepare(durations, starts, antenna, fractions):
    count, rows, sfts = durations.shape[0], starts.shape[0], antenna.shape[0]
    columns = 4 * fractions.shape[0]
    features = 4 * W * (fractions.shape[0] // LANES)
    vmem = pl.BlockSpec(memory_space=pltpu.VMEM)
    return pl.pallas_call(
        prepare_kernel,
        out_shape=(
            jax.ShapeDtypeStruct((count * rows, sfts), jnp.bfloat16),
            jax.ShapeDtypeStruct((2, sfts, LANES), jnp.float32),
            jax.ShapeDtypeStruct((3, count * rows, LANES), jnp.float32),
            jax.ShapeDtypeStruct((2 * features, columns), jnp.bfloat16),
        ),
        in_specs=[pl.BlockSpec(memory_space=pltpu.SMEM), vmem, vmem, vmem],
        out_specs=(vmem,) * 4,
        compiler_params=pltpu.CompilerParams(vmem_limit_bytes=16 * 1024 * 1024),
        cost_estimate=pl.CostEstimate(flops=100_000_000, bytes_accessed=4_000_000, transcendentals=0),
        name="prepare",
    )(durations, jnp.broadcast_to(starts[:, None], (rows, LANES)), antenna.T, fractions[None, :])


def statistic_kernel(windows_ref, mask_ref, weigh_ref, coef_ref, kernel_ref, map_ref, loudest_ref):
    values = windows_ref[...].astype(jnp.float32)
    half = LANES // 2
    weighted = (weigh_ref[0] * values + weigh_ref[1] * pltpu.roll(values, half, 1)).astype(jnp.bfloat16)
    templates = map_ref.shape[1]
    rows = map_ref.shape[0] // loudest_ref.shape[1]
    copies = loudest_ref.shape[0]
    per_step = LANES // rows
    for step in range(map_ref.shape[0] // LANES):
        here = pl.ds(step * LANES, LANES)
        sums = jnp.dot(mask_ref[here, :], weighted, preferred_element_type=jnp.float32)
        sums = sums - coef_ref[2, here, :] * pltpu.roll(sums, half, 1)
        parts = jnp.concatenate(split(sums, 2), axis=1)
        found = jnp.dot(parts, kernel_ref[...], preferred_element_type=jnp.float32)
        ra, ia, rb, ib = (found[:, c * templates : (c + 1) * templates] for c in range(4))
        power_a, power_b = ra * ra + ia * ia, rb * rb + ib * ib
        best = None
        for b in range(templates // LANES):
            columns = slice(b * LANES, (b + 1) * LANES)
            result = coef_ref[0, here, :] * power_a[:, columns] + coef_ref[1, here, :] * power_b[:, columns]
            map_ref[here, columns] = result
            best = result if best is None else jnp.maximum(best, result)
        best = jnp.max(jnp.transpose(best), axis=0, keepdims=True)
        for n in range(per_step):
            turned = best if n == 0 else pltpu.roll(best, LANES - n * rows, 1)
            for copy in range(copies):
                loudest_ref[copy, pl.ds(step * per_step + n, 1), :] = turned


def statistic(windows, mask, weigh, coef, kernel, rows, copies):
    count = mask.shape[0] // rows
    templates = kernel.shape[1] // 4
    vmem = pl.BlockSpec(memory_space=pltpu.VMEM)
    return pl.pallas_call(
        statistic_kernel,
        out_shape=(
            jax.ShapeDtypeStruct((count * rows, templates), jnp.float32),
            jax.ShapeDtypeStruct((copies, count, LANES), jnp.float32),
        ),
        in_specs=[vmem] * 5,
        out_specs=(vmem, vmem),
        compiler_params=pltpu.CompilerParams(vmem_limit_bytes=16 * 1024 * 1024),
        cost_estimate=pl.CostEstimate(flops=400_000_000, bytes_accessed=4_000_000, transcendentals=0),
        name="statistic",
    )(windows, mask, weigh, coef, kernel)


def to_all(values, axis):
    copies = jnp.broadcast_to(values[None], (lax.axis_size(axis),) + values.shape)
    return lax.all_to_all(copies, axis, split_axis=0, concat_axis=0, tiled=True)


def body(spectra, offsets, fractions, antenna, starts, durations):
    bands, cores = lax.axis_size("tmpl"), lax.axis_size("tm")
    sft_rows = spectra.shape[0]
    grid_size = starts.shape[0]
    my_rows = grid_size // cores
    me = lax.axis_index("tmpl").astype(jnp.int32)[None]
    known = to_all(offsets.T, "tmpl")
    my_durations = lax.dynamic_slice_in_dim(durations, lax.axis_index("tm") * my_rows, my_rows, 0)
    windows = pick(me, known, spectra, cores).reshape(cores * bands, sft_rows, LANES)
    windows, my_durations = lax.optimization_barrier((windows, my_durations))
    prepared = prepare(my_durations, starts, antenna, fractions)
    arrived = lax.all_to_all(windows, ("tm", "tmpl"), split_axis=0, concat_axis=0, tiled=True)
    arrived = arrived.reshape(cores * bands * sft_rows, LANES)
    fstat_map, loudest = statistic(arrived, *prepared, grid_size, bands)
    loudest = lax.all_to_all(loudest, "tmpl", split_axis=0, concat_axis=0, tiled=True)
    loudest = jnp.max(loudest[:, :, :grid_size], axis=0)
    return (fstat_map.reshape(my_rows, grid_size, -1), loudest)


def solution(mesh):
    in_specs = (
        P(("grp", "tm", "tmpl"), None, None),
        P(("grp", "tm"), "tmpl"),
        P(("grp", "tmpl")),
        P("grp", None),
        P("grp"),
        P("grp"),
    )
    out_specs = (P("tm", None, ("grp", "tmpl")), P(("grp", "tm"), None))
    return jax.shard_map(body, mesh=mesh, in_specs=in_specs, out_specs=out_specs, check_vma=False)
```

```python
import functools

import jax
import jax.numpy as jnp
from jax import lax
from jax.experimental import pallas as pl
from jax.experimental.pallas import tpu as pltpu
from jax.sharding import PartitionSpec as P

W = 16
LANES = 128
NT = (((1,), (1,)), ((), ()))


def iota(shape, axis):
    return lax.broadcasted_iota(jnp.int32, shape, axis)


def hold_kernel(spec_ref, out_ref, sem):
    copy = pltpu.make_async_copy(spec_ref, out_ref, sem)
    copy.start()
    copy.wait()


def hold(spectra):
    return pl.pallas_call(
        hold_kernel,
        out_shape=jax.ShapeDtypeStruct(spectra.shape, spectra.dtype),
        in_specs=[pl.BlockSpec(memory_space=pl.ANY)],
        out_specs=pl.BlockSpec(memory_space=pltpu.VMEM),
        scratch_shapes=[pltpu.SemaphoreType.DMA],
        compiler_params=pltpu.CompilerParams(vmem_limit_bytes=8 * 1024 * 1024),
        cost_estimate=pl.CostEstimate(flops=0, bytes_accessed=4 * spectra.size, transcendentals=0),
        name="hold",
    )(spectra)


def pick_kernel(me_ref, offset_ref, spec_ref, out_ref, place_ref, turn_ref, tile_ref, sems):
    rows, _, bins = spec_ref.shape
    bands, blocks, _ = offset_ref.shape
    cores = out_ref.shape[0]
    band_width = bins // bands
    groups = rows // 8
    chunks = band_width // LANES
    width = blocks * W
    first = me_ref[0] * rows
    columns = pl.ds(pl.multiple_of(first // LANES * LANES, LANES), LANES)
    offsets = jnp.concatenate([offset_ref[band, :, columns] for band in range(bands)], axis=0).astype(jnp.float32)
    lane = iota(offsets.shape, 1)
    offsets = jnp.take_along_axis(offsets, (lane >> 2) + first & (LANES - 1), axis=1, mode="promise_in_bounds")
    offsets = jnp.concatenate([offsets, jnp.zeros((LANES - bands * blocks, LANES), jnp.float32)], axis=0)
    upright = jnp.transpose(offsets).astype(jnp.int32)
    lane = iota((32, LANES), 1)
    places = upright[0:32]
    for group in range(1, groups):
        turned = pltpu.roll(upright[group * 32 : group * 32 + 32], group * bands * blocks, 1)
        places = jnp.where(lane < group * bands * blocks, places, turned)
    lane = iota((8, LANES), 1)
    lane_group = lane // width
    source = lane_group * (bands * blocks) + lane // W % blocks
    for band in range(bands):
        for pair in range(4):
            place = jnp.take_along_axis(places[pair * 8 : pair * 8 + 8], source + band * blocks, axis=1, mode="promise_in_bounds")
            place_ref[band, pair] = place + ((lane & (W - 1)) + lane_group * band_width)

    def step(band, carry):
        for pair in range(4):
            place = place_ref[band, pair]
            lane_id = place & (LANES - 1)
            chosen = place >> 7
            tile = jnp.zeros((8, LANES), jnp.float32)
            for group in range(groups):
                for chunk in range(chunks):
                    start = pl.multiple_of(band * band_width + chunk * LANES, LANES)
                    values = spec_ref[pl.ds(group * 8 + pair * 2, 2), :, pl.ds(start, LANES)]
                    values = values.astype(jnp.float32).reshape(8, LANES)
                    moved = jnp.take_along_axis(values, lane_id, axis=1, mode="promise_in_bounds")
                    tile = jnp.where(chosen == group * chunks + chunk, moved, tile)
            turn_ref[band, pl.ds(pair * 8, 8), :] = tile
        return carry

    lax.fori_loop(0, bands, step, 0)
    tiles = []
    for band in range(bands):
        parts = [turn_ref[band, pl.ds(part, 8, stride=4), :] for part in range(4)]
        for group in range(groups):
            tile = jnp.zeros((8, LANES), jnp.float32)
            for part in range(4):
                amount = (part - group) * width % LANES
                turned = pltpu.roll(parts[part], amount, 1) if amount else parts[part]
                tile = jnp.where(lane_group == part, turned, tile)
            tiles.append(tile)
        if len(tiles) >= 2:
            first_row = (band + 1) * rows - len(tiles) * 8
            tile_ref[first_row : (band + 1) * rows, :] = jnp.concatenate(tiles, axis=0).astype(jnp.bfloat16)
            tiles = []
    copies = [pltpu.make_async_copy(tile_ref, out_ref.at[core], sems.at[core]) for core in range(cores)]
    for copy in copies:
        copy.start()
    for copy in copies:
        copy.wait()


def pick(me, offsets, spectra, cores):
    rows, bands = spectra.shape[0], offsets.shape[0]
    vmem = pl.BlockSpec(memory_space=pltpu.VMEM)
    return pl.pallas_call(
        pick_kernel,
        out_shape=jax.ShapeDtypeStruct((cores, bands * rows, LANES), jnp.bfloat16),
        in_specs=[pl.BlockSpec(memory_space=pltpu.SMEM), vmem, vmem],
        out_specs=pl.BlockSpec(memory_space=pl.ANY),
        scratch_shapes=[
            pltpu.VMEM((bands, 4, 8, LANES), jnp.int32),
            pltpu.VMEM((bands, 32, LANES), jnp.float32),
            pltpu.VMEM((bands * rows, LANES), jnp.bfloat16),
            pltpu.SemaphoreType.DMA((cores,)),
        ],
        compiler_params=pltpu.CompilerParams(vmem_limit_bytes=8 * 1024 * 1024),
        cost_estimate=pl.CostEstimate(flops=10_000_000, bytes_accessed=2 * spectra.size, transcendentals=0),
        name="pick",
    )(me, offsets, spectra)


def split(values, count):
    parts = []
    for _ in range(count):
        part = values.astype(jnp.bfloat16)
        parts.append(part)
        values = values - part.astype(jnp.float32)
    return parts


def prepare_kernel(durations_ref, starts_ref, antenna_ref, fractions_ref, mask_ref, weigh_ref, coef_ref, kernel_ref):
    rows = starts_ref.shape[0]
    count = durations_ref.shape[0]
    sfts = antenna_ref.shape[1]
    sft = iota((rows, sfts), 1)
    start = starts_ref[:, 0:1]
    after = sft >= start
    for j in range(count):
        inside = after & (sft < start + durations_ref[j])
        mask_ref[pl.ds(j * rows, rows), :] = jnp.where(inside, 1.0, 0.0).astype(jnp.bfloat16)
    antenna = antenna_ref[...]
    a1, a2, b1, b2 = (antenna[n : n + 1] for n in range(4))
    terms = jnp.concatenate([a1 * a1 + a2 * a2, b1 * b1 + b2 * b2, a1 * b1 + a2 * b2, jnp.zeros((5, sfts), jnp.float32)], axis=0)
    weights = sum(lax.dot_general(mask_ref[...], part, NT, preferred_element_type=jnp.float32) for part in split(terms, 3))
    wa, wb, wc = (weights[:, n : n + 1] for n in range(3))
    shape = (rows * count, LANES)
    late = iota(shape, 1) >= LANES // 2
    coef_ref[0] = jnp.broadcast_to(1.0 / wa, shape)
    coef_ref[1] = jnp.broadcast_to(wa / (wa * wb - wc * wc), shape)
    coef_ref[2] = jnp.where(late, jnp.broadcast_to(wc / wa, shape), 0.0)
    upright = jnp.transpose(jnp.concatenate([antenna, jnp.zeros((LANES - 4, sfts), jnp.float32)], axis=0))
    shape = (sfts, LANES)
    late = iota(shape, 1) >= LANES // 2
    weigh_ref[0] = jnp.where(late, upright[:, 3:4], upright[:, 0:1])
    weigh_ref[1] = jnp.where(late, upright[:, 2:3], upright[:, 1:2])
    fractions = fractions_ref[...]
    templates = fractions.shape[1]
    blocks = kernel_ref.shape[1] // (4 * LANES)
    bin_id = iota((W, templates), 0)
    distance = fractions + (W // 2 - 1) - bin_id.astype(jnp.float32)
    alternate = 1.0 - 2.0 * (bin_id % 2).astype(jnp.float32)
    values = (alternate * jnp.sin(jnp.pi * fractions) / (jnp.pi * distance)).astype(jnp.bfloat16)
    kernel_ref[...] = jnp.zeros_like(kernel_ref)
    for part in range(2):
        for c in range(4):
            for b in range(blocks):
                row = ((part * 4 + c) * blocks + b) * W
                column = (c * blocks + b) * LANES
                kernel_ref[pl.ds(row, W), pl.ds(column, LANES)] = values[:, b * LANES : (b + 1) * LANES]


def prepare(durations, starts, antenna, fractions):
    count, rows, sfts = durations.shape[0], starts.shape[0], antenna.shape[0]
    columns = 4 * fractions.shape[0]
    features = 4 * W * (fractions.shape[0] // LANES)
    vmem = pl.BlockSpec(memory_space=pltpu.VMEM)
    return pl.pallas_call(
        prepare_kernel,
        out_shape=(
            jax.ShapeDtypeStruct((count * rows, sfts), jnp.bfloat16),
            jax.ShapeDtypeStruct((2, sfts, LANES), jnp.float32),
            jax.ShapeDtypeStruct((3, count * rows, LANES), jnp.float32),
            jax.ShapeDtypeStruct((2 * features, columns), jnp.bfloat16),
        ),
        in_specs=[pl.BlockSpec(memory_space=pltpu.SMEM), vmem, vmem, vmem],
        out_specs=(vmem,) * 4,
        compiler_params=pltpu.CompilerParams(vmem_limit_bytes=16 * 1024 * 1024),
        cost_estimate=pl.CostEstimate(flops=100_000_000, bytes_accessed=4_000_000, transcendentals=0),
        name="prepare",
    )(durations, jnp.broadcast_to(starts[:, None], (rows, LANES)), antenna.T, fractions[None, :])


def statistic_kernel(windows_ref, mask_ref, weigh_ref, coef_ref, kernel_ref, map_ref, loudest_ref):
    values = windows_ref[...].astype(jnp.float32)
    half = LANES // 2
    weighted = (weigh_ref[0] * values + weigh_ref[1] * pltpu.roll(values, half, 1)).astype(jnp.bfloat16)
    templates = map_ref.shape[1]
    rows = map_ref.shape[0] // loudest_ref.shape[1]
    copies = loudest_ref.shape[0]
    per_step = LANES // rows
    for step in range(map_ref.shape[0] // LANES):
        here = pl.ds(step * LANES, LANES)
        sums = jnp.dot(mask_ref[here, :], weighted, preferred_element_type=jnp.float32)
        sums = sums - coef_ref[2, here, :] * pltpu.roll(sums, half, 1)
        parts = jnp.concatenate(split(sums, 2), axis=1)
        found = jnp.dot(parts, kernel_ref[...], preferred_element_type=jnp.float32)
        ra, ia, rb, ib = (found[:, c * templates : (c + 1) * templates] for c in range(4))
        power_a, power_b = ra * ra + ia * ia, rb * rb + ib * ib
        best = None
        for b in range(templates // LANES):
            columns = slice(b * LANES, (b + 1) * LANES)
            result = coef_ref[0, here, :] * power_a[:, columns] + coef_ref[1, here, :] * power_b[:, columns]
            map_ref[here, columns] = result
            best = result if best is None else jnp.maximum(best, result)
        best = jnp.max(jnp.transpose(best), axis=0, keepdims=True)
        for n in range(per_step):
            turned = best if n == 0 else pltpu.roll(best, LANES - n * rows, 1)
            for copy in range(copies):
                loudest_ref[copy, pl.ds(step * per_step + n, 1), :] = turned


def statistic(windows, mask, weigh, coef, kernel, rows, copies):
    count = mask.shape[0] // rows
    templates = kernel.shape[1] // 4
    vmem = pl.BlockSpec(memory_space=pltpu.VMEM)
    return pl.pallas_call(
        statistic_kernel,
        out_shape=(
            jax.ShapeDtypeStruct((count * rows, templates), jnp.float32),
            jax.ShapeDtypeStruct((copies, count, LANES), jnp.float32),
        ),
        in_specs=[vmem] * 5,
        out_specs=(vmem, vmem),
        compiler_params=pltpu.CompilerParams(vmem_limit_bytes=16 * 1024 * 1024),
        cost_estimate=pl.CostEstimate(flops=400_000_000, bytes_accessed=4_000_000, transcendentals=0),
        name="statistic",
    )(windows, mask, weigh, coef, kernel)


def to_all(values, axis):
    copies = jnp.broadcast_to(values[None], (lax.axis_size(axis),) + values.shape)
    return lax.all_to_all(copies, axis, split_axis=0, concat_axis=0, tiled=True)


def body(spectra, offsets, fractions, antenna, starts, durations):
    bands, cores = lax.axis_size("tmpl"), lax.axis_size("tm")
    sft_rows = spectra.shape[0]
    grid_size = starts.shape[0]
    my_rows = grid_size // cores
    me = lax.axis_index("tmpl").astype(jnp.int32)[None]
    known = to_all(offsets.T, "tmpl")
    my_durations = lax.dynamic_slice_in_dim(durations, lax.axis_index("tm") * my_rows, my_rows, 0)
    windows = pick(me, known, hold(spectra), cores).reshape(cores * bands, sft_rows, LANES)
    windows, my_durations = lax.optimization_barrier((windows, my_durations))
    prepared = prepare(my_durations, starts, antenna, fractions)
    arrived = lax.all_to_all(windows, ("tm", "tmpl"), split_axis=0, concat_axis=0, tiled=True)
    arrived = arrived.reshape(cores * bands * sft_rows, LANES)
    fstat_map, loudest = statistic(arrived, *prepared, grid_size, bands)
    loudest = lax.all_to_all(loudest, "tmpl", split_axis=0, concat_axis=0, tiled=True)
    loudest = jnp.max(loudest[:, :, :grid_size], axis=0)
    return (fstat_map.reshape(my_rows, grid_size, -1), loudest)


def solution(mesh):
    in_specs = (
        P(("grp", "tm", "tmpl"), None, None),
        P(("grp", "tm"), "tmpl"),
        P(("grp", "tmpl")),
        P("grp", None),
        P("grp"),
        P("grp"),
    )
    out_specs = (P("tm", None, ("grp", "tmpl")), P(("grp", "tm"), None))
    return jax.shard_map(body, mesh=mesh, in_specs=in_specs, out_specs=out_specs, check_vma=False)
```

```python
import functools

import jax
import jax.numpy as jnp
from jax import lax
from jax.experimental import pallas as pl
from jax.experimental.pallas import tpu as pltpu
from jax.sharding import PartitionSpec as P

W = 16
LANES = 128
NT = (((1,), (1,)), ((), ()))


def iota(shape, axis):
    return lax.broadcasted_iota(jnp.int32, shape, axis)


def hold_kernel(spec_ref, out_ref, sem):
    copy = pltpu.make_async_copy(spec_ref, out_ref, sem)
    copy.start()
    copy.wait()


def hold(spectra):
    return pl.pallas_call(
        hold_kernel,
        out_shape=jax.ShapeDtypeStruct(spectra.shape, spectra.dtype),
        in_specs=[pl.BlockSpec(memory_space=pl.ANY)],
        out_specs=pl.BlockSpec(memory_space=pltpu.VMEM),
        scratch_shapes=[pltpu.SemaphoreType.DMA],
        compiler_params=pltpu.CompilerParams(vmem_limit_bytes=8 * 1024 * 1024),
        cost_estimate=pl.CostEstimate(flops=0, bytes_accessed=4 * spectra.size, transcendentals=0),
        name="hold",
    )(spectra)


def pick_kernel(me_ref, offset_ref, spec_ref, out_ref, place_ref, turn_ref, tile_ref, sems):
    rows, _, bins = spec_ref.shape
    bands, blocks, _ = offset_ref.shape
    cores = out_ref.shape[0]
    band_width = bins // bands
    groups = rows // 8
    chunks = band_width // LANES
    width = blocks * W
    first = me_ref[0] * rows
    columns = pl.ds(pl.multiple_of(first // LANES * LANES, LANES), LANES)
    offsets = jnp.concatenate([offset_ref[band, :, columns] for band in range(bands)], axis=0).astype(jnp.float32)
    lane = iota(offsets.shape, 1)
    offsets = jnp.take_along_axis(offsets, (lane >> 2) + first & (LANES - 1), axis=1, mode="promise_in_bounds")
    offsets = jnp.concatenate([offsets, jnp.zeros((LANES - bands * blocks, LANES), jnp.float32)], axis=0)
    upright = jnp.transpose(offsets).astype(jnp.int32)
    lane = iota((32, LANES), 1)
    places = upright[0:32]
    for group in range(1, groups):
        turned = pltpu.roll(upright[group * 32 : group * 32 + 32], group * bands * blocks, 1)
        places = jnp.where(lane < group * bands * blocks, places, turned)
    lane = iota((8, LANES), 1)
    lane_group = lane // width
    source = lane_group * (bands * blocks) + lane // W % blocks
    for band in range(bands):
        for pair in range(4):
            place = jnp.take_along_axis(places[pair * 8 : pair * 8 + 8], source + band * blocks, axis=1, mode="promise_in_bounds")
            place_ref[band, pair] = place + ((lane & (W - 1)) + lane_group * band_width)

    def step(band, carry):
        for pair in range(4):
            place = place_ref[band, pair]
            lane_id = place & (LANES - 1)
            chosen = place >> 7
            tile = jnp.zeros((8, LANES), jnp.float32)
            for group in range(groups):
                for chunk in range(chunks):
                    start = pl.multiple_of(band * band_width + chunk * LANES, LANES)
                    values = spec_ref[pl.ds(group * 8 + pair * 2, 2), :, pl.ds(start, LANES)]
                    values = values.astype(jnp.float32).reshape(8, LANES)
                    moved = jnp.take_along_axis(values, lane_id, axis=1, mode="promise_in_bounds")
                    tile = jnp.where(chosen == group * chunks + chunk, moved, tile)
            turn_ref[band, pl.ds(pair * 8, 8), :] = tile
        return carry

    lax.fori_loop(0, bands, step, 0)
    tiles = []
    for band in range(bands):
        parts = [turn_ref[band, pl.ds(part, 8, stride=4), :] for part in range(4)]
        for group in range(groups):
            tile = jnp.zeros((8, LANES), jnp.float32)
            for part in range(4):
                amount = (part - group) * width % LANES
                turned = pltpu.roll(parts[part], amount, 1) if amount else parts[part]
                tile = jnp.where(lane_group == part, turned, tile)
            tiles.append(tile)
        if len(tiles) >= 2:
            first_row = (band + 1) * rows - len(tiles) * 8
            tile_ref[first_row : (band + 1) * rows, :] = jnp.concatenate(tiles, axis=0).astype(jnp.bfloat16)
            tiles = []
    copies = [pltpu.make_async_copy(tile_ref, out_ref.at[core], sems.at[core]) for core in range(cores)]
    for copy in copies:
        copy.start()
    for copy in copies:
        copy.wait()


def pick(me, offsets, spectra, cores):
    rows, bands = spectra.shape[0], offsets.shape[0]
    vmem = pl.BlockSpec(memory_space=pltpu.VMEM)
    return pl.pallas_call(
        pick_kernel,
        out_shape=jax.ShapeDtypeStruct((cores, bands * rows, LANES), jnp.bfloat16),
        in_specs=[pl.BlockSpec(memory_space=pltpu.SMEM), vmem, vmem],
        out_specs=pl.BlockSpec(memory_space=pl.ANY),
        scratch_shapes=[
            pltpu.VMEM((bands, 4, 8, LANES), jnp.int32),
            pltpu.VMEM((bands, 32, LANES), jnp.float32),
            pltpu.VMEM((bands * rows, LANES), jnp.bfloat16),
            pltpu.SemaphoreType.DMA((cores,)),
        ],
        compiler_params=pltpu.CompilerParams(vmem_limit_bytes=8 * 1024 * 1024),
        cost_estimate=pl.CostEstimate(flops=10_000_000, bytes_accessed=2 * spectra.size, transcendentals=0),
        name="pick",
    )(me, offsets, spectra)


def split(values, count):
    parts = []
    for _ in range(count):
        part = values.astype(jnp.bfloat16)
        parts.append(part)
        values = values - part.astype(jnp.float32)
    return parts


def prepare_kernel(durations_ref, starts_ref, antenna_ref, fractions_ref, mask_ref, weigh_ref, coef_ref, kernel_ref):
    rows = starts_ref.shape[0]
    count = durations_ref.shape[0]
    sfts = antenna_ref.shape[1]
    sft = iota((rows, sfts), 1)
    start = starts_ref[:, 0:1]
    after = sft >= start
    for j in range(count):
        inside = after & (sft < start + durations_ref[j])
        mask_ref[pl.ds(j * rows, rows), :] = jnp.where(inside, 1.0, 0.0).astype(jnp.bfloat16)
    antenna = antenna_ref[...]
    a1, a2, b1, b2 = (antenna[n : n + 1] for n in range(4))
    terms = jnp.concatenate([a1 * a1 + a2 * a2, b1 * b1 + b2 * b2, a1 * b1 + a2 * b2, jnp.zeros((5, sfts), jnp.float32)], axis=0)
    weights = sum(lax.dot_general(mask_ref[...], part, NT, preferred_element_type=jnp.float32) for part in split(terms, 3))
    wa, wb, wc = (weights[:, n : n + 1] for n in range(3))
    shape = (rows * count, LANES)
    late = iota(shape, 1) >= LANES // 2
    coef_ref[0] = jnp.broadcast_to(1.0 / wa, shape)
    coef_ref[1] = jnp.broadcast_to(wa / (wa * wb - wc * wc), shape)
    coef_ref[2] = jnp.where(late, jnp.broadcast_to(wc / wa, shape), 0.0)
    upright = jnp.transpose(jnp.concatenate([antenna, jnp.zeros((LANES - 4, sfts), jnp.float32)], axis=0))
    shape = (sfts, LANES)
    late = iota(shape, 1) >= LANES // 2
    weigh_ref[0] = jnp.where(late, upright[:, 3:4], upright[:, 0:1])
    weigh_ref[1] = jnp.where(late, upright[:, 2:3], upright[:, 1:2])
    fractions = fractions_ref[...]
    templates = fractions.shape[1]
    blocks = kernel_ref.shape[1] // (4 * LANES)
    bin_id = iota((W, templates), 0)
    distance = fractions + (W // 2 - 1) - bin_id.astype(jnp.float32)
    alternate = 1.0 - 2.0 * (bin_id % 2).astype(jnp.float32)
    values = (alternate * jnp.sin(jnp.pi * fractions) / (jnp.pi * distance)).astype(jnp.bfloat16)
    kernel_ref[...] = jnp.zeros_like(kernel_ref)
    for part in range(2):
        for c in range(4):
            for b in range(blocks):
                row = ((part * 4 + c) * blocks + b) * W
                column = (c * blocks + b) * LANES
                kernel_ref[pl.ds(row, W), pl.ds(column, LANES)] = values[:, b * LANES : (b + 1) * LANES]


def prepare(durations, starts, antenna, fractions):
    count, rows, sfts = durations.shape[0], starts.shape[0], antenna.shape[0]
    columns = 4 * fractions.shape[0]
    features = 4 * W * (fractions.shape[0] // LANES)
    vmem = pl.BlockSpec(memory_space=pltpu.VMEM)
    return pl.pallas_call(
        prepare_kernel,
        out_shape=(
            jax.ShapeDtypeStruct((count * rows, sfts), jnp.bfloat16),
            jax.ShapeDtypeStruct((2, sfts, LANES), jnp.float32),
            jax.ShapeDtypeStruct((3, count * rows, LANES), jnp.float32),
            jax.ShapeDtypeStruct((2 * features, columns), jnp.bfloat16),
        ),
        in_specs=[pl.BlockSpec(memory_space=pltpu.SMEM), vmem, vmem, vmem],
        out_specs=(vmem,) * 4,
        compiler_params=pltpu.CompilerParams(vmem_limit_bytes=16 * 1024 * 1024),
        cost_estimate=pl.CostEstimate(flops=100_000_000, bytes_accessed=4_000_000, transcendentals=0),
        name="prepare",
    )(durations, jnp.broadcast_to(starts[:, None], (rows, LANES)), antenna.T, fractions[None, :])


def statistic_kernel(windows_ref, mask_ref, weigh_ref, coef_ref, kernel_ref, map_ref, loudest_ref):
    values = windows_ref[...].astype(jnp.float32)
    half = LANES // 2
    weighted = (weigh_ref[0] * values + weigh_ref[1] * pltpu.roll(values, half, 1)).astype(jnp.bfloat16)
    templates = map_ref.shape[1]
    rows = map_ref.shape[0] // loudest_ref.shape[1]
    copies = loudest_ref.shape[0]
    per_step = LANES // rows
    for step in range(map_ref.shape[0] // LANES):
        here = pl.ds(step * LANES, LANES)
        sums = jnp.dot(mask_ref[here, :], weighted, preferred_element_type=jnp.float32)
        sums = sums - coef_ref[2, here, :] * pltpu.roll(sums, half, 1)
        parts = jnp.concatenate(split(sums, 2), axis=1)
        found = jnp.dot(parts, kernel_ref[...], preferred_element_type=jnp.float32)
        ra, ia, rb, ib = (found[:, c * templates : (c + 1) * templates] for c in range(4))
        power_a, power_b = ra * ra + ia * ia, rb * rb + ib * ib
        best = None
        for b in range(templates // LANES):
            columns = slice(b * LANES, (b + 1) * LANES)
            result = coef_ref[0, here, :] * power_a[:, columns] + coef_ref[1, here, :] * power_b[:, columns]
            map_ref[here, columns] = result
            best = result if best is None else jnp.maximum(best, result)
        best = jnp.max(jnp.transpose(best), axis=0, keepdims=True)
        for n in range(per_step):
            turned = best if n == 0 else pltpu.roll(best, LANES - n * rows, 1)
            for copy in range(copies):
                loudest_ref[copy, pl.ds(step * per_step + n, 1), :] = turned


def statistic(windows, mask, weigh, coef, kernel, rows, copies):
    count = mask.shape[0] // rows
    templates = kernel.shape[1] // 4
    vmem = pl.BlockSpec(memory_space=pltpu.VMEM)
    return pl.pallas_call(
        statistic_kernel,
        out_shape=(
            jax.ShapeDtypeStruct((count * rows, templates), jnp.float32),
            jax.ShapeDtypeStruct((copies, count, LANES), jnp.float32),
        ),
        in_specs=[vmem] * 5,
        out_specs=(vmem, vmem),
        compiler_params=pltpu.CompilerParams(vmem_limit_bytes=16 * 1024 * 1024),
        cost_estimate=pl.CostEstimate(flops=400_000_000, bytes_accessed=4_000_000, transcendentals=0),
        name="statistic",
    )(windows, mask, weigh, coef, kernel)


def body(spectra, offsets, fractions, antenna, starts, durations):
    bands, cores = lax.axis_size("tmpl"), lax.axis_size("tm")
    sft_rows = spectra.shape[0]
    grid_size = starts.shape[0]
    my_rows = grid_size // cores
    me = lax.axis_index("tmpl").astype(jnp.int32)[None]
    known = lax.all_gather(offsets.T, "tmpl")
    my_durations = lax.dynamic_slice_in_dim(durations, lax.axis_index("tm") * my_rows, my_rows, 0)
    windows = pick(me, known, hold(spectra), cores).reshape(cores * bands, sft_rows, LANES)
    windows, my_durations = lax.optimization_barrier((windows, my_durations))
    prepared = prepare(my_durations, starts, antenna, fractions)
    arrived = lax.all_to_all(windows, ("tm", "tmpl"), split_axis=0, concat_axis=0, tiled=True)
    arrived = arrived.reshape(cores * bands * sft_rows, LANES)
    fstat_map, loudest = statistic(arrived, *prepared, grid_size, 1)
    loudest = lax.all_gather(loudest[0], "tmpl")
    loudest = jnp.max(loudest[:, :, :grid_size], axis=0)
    return (fstat_map.reshape(my_rows, grid_size, -1), loudest)


def solution(mesh):
    in_specs = (
        P(("grp", "tm", "tmpl"), None, None),
        P(("grp", "tm"), "tmpl"),
        P(("grp", "tmpl")),
        P("grp", None),
        P("grp"),
        P("grp"),
    )
    out_specs = (P("tm", None, ("grp", "tmpl")), P(("grp", "tm"), None))
    return jax.shard_map(body, mesh=mesh, in_specs=in_specs, out_specs=out_specs, check_vma=False)
```

```python
import functools

import jax
import jax.numpy as jnp
from jax import lax
from jax.experimental import pallas as pl
from jax.experimental.pallas import tpu as pltpu
from jax.sharding import PartitionSpec as P

W = 16
LANES = 128
NT = (((1,), (1,)), ((), ()))


def iota(shape, axis):
    return lax.broadcasted_iota(jnp.int32, shape, axis)


def hold_kernel(spec_ref, out_ref, sem):
    copy = pltpu.make_async_copy(spec_ref, out_ref, sem)
    copy.start()
    copy.wait()


def hold(spectra):
    return pl.pallas_call(
        hold_kernel,
        out_shape=jax.ShapeDtypeStruct(spectra.shape, spectra.dtype),
        in_specs=[pl.BlockSpec(memory_space=pl.ANY)],
        out_specs=pl.BlockSpec(memory_space=pltpu.VMEM),
        scratch_shapes=[pltpu.SemaphoreType.DMA],
        compiler_params=pltpu.CompilerParams(vmem_limit_bytes=8 * 1024 * 1024),
        cost_estimate=pl.CostEstimate(flops=0, bytes_accessed=4 * spectra.size, transcendentals=0),
        name="hold",
    )(spectra)


def join_kernel(*refs):
    *parts, out_ref = refs
    out_ref[...] = jnp.concatenate([part[...] for part in parts], axis=0)


def join(*parts):
    vmem = pl.BlockSpec(memory_space=pltpu.VMEM)
    rows = sum(part.shape[0] for part in parts)
    return pl.pallas_call(
        join_kernel,
        out_shape=jax.ShapeDtypeStruct((rows, parts[0].shape[1]), parts[0].dtype),
        in_specs=[vmem] * len(parts),
        out_specs=vmem,
        compiler_params=pltpu.CompilerParams(vmem_limit_bytes=8 * 1024 * 1024),
        name="join",
    )(*parts)


def pick_kernel(me_ref, *refs):
    *offset_refs, spec_ref, out_ref, place_ref, turn_ref, tile_ref, sems = refs
    rows, _, bins = spec_ref.shape
    cores = out_ref.shape[0]
    bands = out_ref.shape[1] // rows
    blocks = sum(ref.shape[0] for ref in offset_refs) // bands
    band_width = bins // bands
    groups = rows // 8
    chunks = band_width // LANES
    width = blocks * W
    me = me_ref[0]
    first = me * rows
    columns = pl.ds(pl.multiple_of(first // LANES * LANES, LANES), LANES)
    offsets = jnp.concatenate([ref[:, columns] for ref in offset_refs], axis=0).astype(jnp.float32)
    lane = iota(offsets.shape, 1)
    offsets = jnp.take_along_axis(offsets, (lane >> 2) + first & (LANES - 1), axis=1, mode="promise_in_bounds")
    offsets = jnp.concatenate([offsets, jnp.zeros((LANES - bands * blocks, LANES), jnp.float32)], axis=0)
    upright = jnp.transpose(offsets).astype(jnp.int32)
    lane = iota((32, LANES), 1)
    places = upright[0:32]
    for group in range(1, groups):
        turned = pltpu.roll(upright[group * 32 : group * 32 + 32], group * bands * blocks, 1)
        places = jnp.where(lane < group * bands * blocks, places, turned)
    lane = iota((8, LANES), 1)
    lane_group = lane // width
    source = lane_group * (bands * blocks) + lane // W % blocks
    for band in range(bands):
        for pair in range(4):
            place = jnp.take_along_axis(places[pair * 8 : pair * 8 + 8], source + (band ^ me) * blocks, axis=1, mode="promise_in_bounds")
            place_ref[band, pair] = place + ((lane & (W - 1)) + lane_group * band_width)

    def step(band, carry):
        for pair in range(4):
            place = place_ref[band, pair]
            lane_id = place & (LANES - 1)
            chosen = place >> 7
            tile = jnp.zeros((8, LANES), jnp.float32)
            for group in range(groups):
                for chunk in range(chunks):
                    start = pl.multiple_of(band * band_width + chunk * LANES, LANES)
                    values = spec_ref[pl.ds(group * 8 + pair * 2, 2), :, pl.ds(start, LANES)]
                    values = values.astype(jnp.float32).reshape(8, LANES)
                    moved = jnp.take_along_axis(values, lane_id, axis=1, mode="promise_in_bounds")
                    tile = jnp.where(chosen == group * chunks + chunk, moved, tile)
            turn_ref[band, pl.ds(pair * 8, 8), :] = tile
        return carry

    lax.fori_loop(0, bands, step, 0)
    tiles = []
    for band in range(bands):
        parts = [turn_ref[band, pl.ds(part, 8, stride=4), :] for part in range(4)]
        for group in range(groups):
            tile = jnp.zeros((8, LANES), jnp.float32)
            for part in range(4):
                amount = (part - group) * width % LANES
                turned = pltpu.roll(parts[part], amount, 1) if amount else parts[part]
                tile = jnp.where(lane_group == part, turned, tile)
            tiles.append(tile)
        if len(tiles) >= 2:
            first_row = (band + 1) * rows - len(tiles) * 8
            tile_ref[first_row : (band + 1) * rows, :] = jnp.concatenate(tiles, axis=0).astype(jnp.bfloat16)
            tiles = []
    copies = [pltpu.make_async_copy(tile_ref, out_ref.at[core], sems.at[core]) for core in range(cores)]
    for copy in copies:
        copy.start()
    for copy in copies:
        copy.wait()


def pick(me, offsets, spectra, bands, cores):
    rows = spectra.shape[0]
    vmem = pl.BlockSpec(memory_space=pltpu.VMEM)
    return pl.pallas_call(
        pick_kernel,
        out_shape=jax.ShapeDtypeStruct((cores, bands * rows, LANES), jnp.bfloat16),
        in_specs=[pl.BlockSpec(memory_space=pltpu.SMEM)] + [vmem] * (len(offsets) + 1),
        out_specs=pl.BlockSpec(memory_space=pl.ANY),
        scratch_shapes=[
            pltpu.VMEM((bands, 4, 8, LANES), jnp.int32),
            pltpu.VMEM((bands, 32, LANES), jnp.float32),
            pltpu.VMEM((bands * rows, LANES), jnp.bfloat16),
            pltpu.SemaphoreType.DMA((cores,)),
        ],
        compiler_params=pltpu.CompilerParams(vmem_limit_bytes=8 * 1024 * 1024),
        cost_estimate=pl.CostEstimate(flops=10_000_000, bytes_accessed=2 * spectra.size, transcendentals=0),
        name="pick",
    )(me, *offsets, spectra)


def split(values, count):
    parts = []
    for _ in range(count):
        part = values.astype(jnp.bfloat16)
        parts.append(part)
        values = values - part.astype(jnp.float32)
    return parts


def prepare_kernel(durations_ref, starts_ref, antenna_ref, fractions_ref, mask_ref, weigh_ref, coef_ref, kernel_ref):
    rows = starts_ref.shape[0]
    count = durations_ref.shape[0]
    sfts = antenna_ref.shape[1]
    sft = iota((rows, sfts), 1)
    start = starts_ref[:, 0:1]
    after = sft >= start
    for j in range(count):
        inside = after & (sft < start + durations_ref[j])
        mask_ref[pl.ds(j * rows, rows), :] = jnp.where(inside, 1.0, 0.0).astype(jnp.bfloat16)
    antenna = antenna_ref[...]
    a1, a2, b1, b2 = (antenna[n : n + 1] for n in range(4))
    terms = jnp.concatenate([a1 * a1 + a2 * a2, b1 * b1 + b2 * b2, a1 * b1 + a2 * b2, jnp.zeros((5, sfts), jnp.float32)], axis=0)
    weights = sum(lax.dot_general(mask_ref[...], part, NT, preferred_element_type=jnp.float32) for part in split(terms, 3))
    wa, wb, wc = (weights[:, n : n + 1] for n in range(3))
    shape = (rows * count, LANES)
    late = iota(shape, 1) >= LANES // 2
    coef_ref[0] = jnp.broadcast_to(1.0 / wa, shape)
    coef_ref[1] = jnp.broadcast_to(wa / (wa * wb - wc * wc), shape)
    coef_ref[2] = jnp.where(late, jnp.broadcast_to(wc / wa, shape), 0.0)
    upright = jnp.transpose(jnp.concatenate([antenna, jnp.zeros((LANES - 4, sfts), jnp.float32)], axis=0))
    shape = (sfts, LANES)
    late = iota(shape, 1) >= LANES // 2
    weigh_ref[0] = jnp.where(late, upright[:, 3:4], upright[:, 0:1])
    weigh_ref[1] = jnp.where(late, upright[:, 2:3], upright[:, 1:2])
    fractions = fractions_ref[...]
    templates = fractions.shape[1]
    blocks = kernel_ref.shape[1] // (4 * LANES)
    bin_id = iota((W, templates), 0)
    distance = fractions + (W // 2 - 1) - bin_id.astype(jnp.float32)
    alternate = 1.0 - 2.0 * (bin_id % 2).astype(jnp.float32)
    values = (alternate * jnp.sin(jnp.pi * fractions) / (jnp.pi * distance)).astype(jnp.bfloat16)
    kernel_ref[...] = jnp.zeros_like(kernel_ref)
    for part in range(2):
        for c in range(4):
            for b in range(blocks):
                row = ((part * 4 + c) * blocks + b) * W
                column = (c * blocks + b) * LANES
                kernel_ref[pl.ds(row, W), pl.ds(column, LANES)] = values[:, b * LANES : (b + 1) * LANES]


def prepare(durations, starts, antenna, fractions):
    count, rows, sfts = durations.shape[0], starts.shape[0], antenna.shape[0]
    columns = 4 * fractions.shape[0]
    features = 4 * W * (fractions.shape[0] // LANES)
    vmem = pl.BlockSpec(memory_space=pltpu.VMEM)
    return pl.pallas_call(
        prepare_kernel,
        out_shape=(
            jax.ShapeDtypeStruct((count * rows, sfts), jnp.bfloat16),
            jax.ShapeDtypeStruct((2, sfts, LANES), jnp.float32),
            jax.ShapeDtypeStruct((3, count * rows, LANES), jnp.float32),
            jax.ShapeDtypeStruct((2 * features, columns), jnp.bfloat16),
        ),
        in_specs=[pl.BlockSpec(memory_space=pltpu.SMEM), vmem, vmem, vmem],
        out_specs=(vmem,) * 4,
        compiler_params=pltpu.CompilerParams(vmem_limit_bytes=16 * 1024 * 1024),
        cost_estimate=pl.CostEstimate(flops=100_000_000, bytes_accessed=4_000_000, transcendentals=0),
        name="prepare",
    )(durations, jnp.broadcast_to(starts[:, None], (rows, LANES)), antenna.T, fractions[None, :])


def statistic_kernel(windows_ref, mask_ref, weigh_ref, coef_ref, kernel_ref, map_ref, loudest_ref):
    values = windows_ref[...].astype(jnp.float32)
    half = LANES // 2
    weighted = (weigh_ref[0] * values + weigh_ref[1] * pltpu.roll(values, half, 1)).astype(jnp.bfloat16)
    templates = map_ref.shape[1]
    rows = loudest_ref.shape[1]
    per_step = LANES // rows
    for step in range(map_ref.shape[0] // LANES):
        here = pl.ds(step * LANES, LANES)
        sums = jnp.dot(mask_ref[here, :], weighted, preferred_element_type=jnp.float32)
        sums = sums - coef_ref[2, here, :] * pltpu.roll(sums, half, 1)
        parts = jnp.concatenate(split(sums, 2), axis=1)
        found = jnp.dot(parts, kernel_ref[...], preferred_element_type=jnp.float32)
        ra, ia, rb, ib = (found[:, c * templates : (c + 1) * templates] for c in range(4))
        power_a, power_b = ra * ra + ia * ia, rb * rb + ib * ib
        best = None
        for b in range(templates // LANES):
            columns = slice(b * LANES, (b + 1) * LANES)
            result = coef_ref[0, here, :] * power_a[:, columns] + coef_ref[1, here, :] * power_b[:, columns]
            map_ref[here, columns] = result
            best = result if best is None else jnp.maximum(best, result)
        best = jnp.max(jnp.transpose(best), axis=0, keepdims=True)
        for n in range(per_step):
            turned = best if n == 0 else pltpu.roll(best, LANES - n * rows, 1)
            loudest_ref[pl.ds(step * per_step + n, 1), :] = turned[:, :rows]


def statistic(windows, mask, weigh, coef, kernel, rows):
    count = mask.shape[0] // rows
    templates = kernel.shape[1] // 4
    vmem = pl.BlockSpec(memory_space=pltpu.VMEM)
    return pl.pallas_call(
        statistic_kernel,
        out_shape=(
            jax.ShapeDtypeStruct((count * rows, templates), jnp.float32),
            jax.ShapeDtypeStruct((count, rows), jnp.float32),
        ),
        in_specs=[vmem] * 5,
        out_specs=(vmem, vmem),
        compiler_params=pltpu.CompilerParams(vmem_limit_bytes=16 * 1024 * 1024),
        cost_estimate=pl.CostEstimate(flops=400_000_000, bytes_accessed=4_000_000, transcendentals=0),
        name="statistic",
    )(windows, mask, weigh, coef, kernel)


def across(values, axis, distance):
    return lax.ppermute(values, axis, [(n, n ^ distance) for n in range(lax.axis_size(axis))])


def body(spectra, offsets, fractions, antenna, starts, durations):
    bands, cores = lax.axis_size("tmpl"), lax.axis_size("tm")
    sft_rows = spectra.shape[0]
    grid_size = starts.shape[0]
    my_rows = grid_size // cores
    me = lax.axis_index("tmpl").astype(jnp.int32)[None]
    known = offsets.T
    known = join(known, across(known, "tmpl", 1))
    known = [known] + [across(known, "tmpl", distance) for distance in range(2, bands, 2)]
    my_durations = lax.dynamic_slice_in_dim(durations, lax.axis_index("tm") * my_rows, my_rows, 0)
    windows = pick(me, known, hold(spectra), bands, cores).reshape(cores * bands, sft_rows, LANES)
    windows, my_durations = lax.optimization_barrier((windows, my_durations))
    prepared = prepare(my_durations, starts, antenna, fractions)
    arrived = lax.all_to_all(windows, ("tm", "tmpl"), split_axis=0, concat_axis=0, tiled=True)
    arrived = arrived.reshape(cores * bands * sft_rows, LANES)
    fstat_map, loudest = statistic(arrived, *prepared, grid_size)
    for distances in (range(2, bands, 2), [1]):
        loudest = functools.reduce(jnp.maximum, [across(loudest, "tmpl", distance) for distance in distances], loudest)
    return (fstat_map.reshape(my_rows, grid_size, -1), loudest)


def solution(mesh):
    in_specs = (
        P(("grp", "tm", "tmpl"), None, None),
        P(("grp", "tm"), "tmpl"),
        P(("grp", "tmpl")),
        P("grp", None),
        P("grp"),
        P("grp"),
    )
    out_specs = (P("tm", None, ("grp", "tmpl")), P(("grp", "tm"), None))
    return jax.shard_map(body, mesh=mesh, in_specs=in_specs, out_specs=out_specs, check_vma=False)
```

```python
import functools

import jax
import jax.numpy as jnp
from jax import lax
from jax.experimental import pallas as pl
from jax.experimental.pallas import tpu as pltpu
from jax.sharding import PartitionSpec as P

W = 16
LANES = 128
NT = (((1,), (1,)), ((), ()))


def iota(shape, axis):
    return lax.broadcasted_iota(jnp.int32, shape, axis)


def order(size, first):
    members = list(range(size))
    members[0], members[first] = first, 0
    return members


def hold_kernel(spec_ref, out_ref, sem):
    copy = pltpu.make_async_copy(spec_ref, out_ref, sem)
    copy.start()
    copy.wait()


def hold(spectra):
    return pl.pallas_call(
        hold_kernel,
        out_shape=jax.ShapeDtypeStruct(spectra.shape, spectra.dtype),
        in_specs=[pl.BlockSpec(memory_space=pl.ANY)],
        out_specs=pl.BlockSpec(memory_space=pltpu.VMEM),
        scratch_shapes=[pltpu.SemaphoreType.DMA],
        compiler_params=pltpu.CompilerParams(vmem_limit_bytes=8 * 1024 * 1024),
        cost_estimate=pl.CostEstimate(flops=0, bytes_accessed=4 * spectra.size, transcendentals=0),
        name="hold",
    )(spectra)


def pick_kernel(bands_in, bands_out, me_ref, offset_ref, spec_ref, out_ref, place_ref, turn_ref, tile_ref, sem):
    rows, _, bins = spec_ref.shape
    bands, blocks, _ = offset_ref.shape
    band_width = bins // bands
    groups = rows // 8
    chunks = band_width // LANES
    width = blocks * W
    first = me_ref[0] * rows
    columns = pl.ds(pl.multiple_of(first // LANES * LANES, LANES), LANES)
    offsets = jnp.concatenate([offset_ref[bands_in.index(band), :, columns] for band in range(bands)], axis=0).astype(jnp.float32)
    lane = iota(offsets.shape, 1)
    offsets = jnp.take_along_axis(offsets, (lane >> 2) + first & (LANES - 1), axis=1, mode="promise_in_bounds")
    offsets = jnp.concatenate([offsets, jnp.zeros((LANES - bands * blocks, LANES), jnp.float32)], axis=0)
    upright = jnp.transpose(offsets).astype(jnp.int32)
    lane = iota((32, LANES), 1)
    places = upright[0:32]
    for group in range(1, groups):
        turned = pltpu.roll(upright[group * 32 : group * 32 + 32], group * bands * blocks, 1)
        places = jnp.where(lane < group * bands * blocks, places, turned)
    lane = iota((8, LANES), 1)
    lane_group = lane // width
    source = lane_group * (bands * blocks) + lane // W % blocks
    for band in range(bands):
        for pair in range(4):
            place = jnp.take_along_axis(places[pair * 8 : pair * 8 + 8], source + band * blocks, axis=1, mode="promise_in_bounds")
            place_ref[band, pair] = place + ((lane & (W - 1)) + lane_group * band_width)

    def step(band, carry):
        for pair in range(4):
            place = place_ref[band, pair]
            lane_id = place & (LANES - 1)
            chosen = place >> 7
            tile = jnp.zeros((8, LANES), jnp.float32)
            for group in range(groups):
                for chunk in range(chunks):
                    start = pl.multiple_of(band * band_width + chunk * LANES, LANES)
                    values = spec_ref[pl.ds(group * 8 + pair * 2, 2), :, pl.ds(start, LANES)]
                    values = values.astype(jnp.float32).reshape(8, LANES)
                    moved = jnp.take_along_axis(values, lane_id, axis=1, mode="promise_in_bounds")
                    tile = jnp.where(chosen == group * chunks + chunk, moved, tile)
            turn_ref[band, pl.ds(pair * 8, 8), :] = tile
        return carry

    lax.fori_loop(0, bands, step, 0)
    tiles = {}
    for band in range(bands):
        parts = [turn_ref[band, pl.ds(part, 8, stride=4), :] for part in range(4)]
        for group in range(groups):
            tile = jnp.zeros((8, LANES), jnp.float32)
            for part in range(4):
                amount = (part - group) * width % LANES
                turned = pltpu.roll(parts[part], amount, 1) if amount else parts[part]
                tile = jnp.where(lane_group == part, turned, tile)
            tiles[band, group] = tile
    wanted = [tiles[band, group] for band in bands_out for group in range(groups)]
    for n in range(0, len(wanted), 2):
        tile_ref[n * 8 : n * 8 + 16, :] = jnp.concatenate(wanted[n : n + 2], axis=0).astype(jnp.bfloat16)
    copy = pltpu.make_async_copy(tile_ref, out_ref, sem)
    copy.start()
    copy.wait()


def pick(me, offsets, spectra, bands_in, bands_out):
    rows, bands = spectra.shape[0], offsets.shape[0]
    out_rows = len(bands_out) * rows
    vmem = pl.BlockSpec(memory_space=pltpu.VMEM)
    return pl.pallas_call(
        functools.partial(pick_kernel, bands_in, bands_out),
        out_shape=jax.ShapeDtypeStruct((out_rows, LANES), jnp.bfloat16),
        in_specs=[pl.BlockSpec(memory_space=pltpu.SMEM), vmem, vmem],
        out_specs=pl.BlockSpec(memory_space=pl.ANY),
        scratch_shapes=[
            pltpu.VMEM((bands, 4, 8, LANES), jnp.int32),
            pltpu.VMEM((bands, 32, LANES), jnp.float32),
            pltpu.VMEM((out_rows, LANES), jnp.bfloat16),
            pltpu.SemaphoreType.DMA,
        ],
        compiler_params=pltpu.CompilerParams(vmem_limit_bytes=8 * 1024 * 1024),
        cost_estimate=pl.CostEstimate(flops=10_000_000, bytes_accessed=2 * spectra.size, transcendentals=0),
        name="pick",
    )(me, offsets, spectra)


def split(values, count):
    parts = []
    for _ in range(count):
        part = values.astype(jnp.bfloat16)
        parts.append(part)
        values = values - part.astype(jnp.float32)
    return parts


def prepare_kernel(first, run, durations_ref, starts_ref, antenna_ref, fractions_ref, mask_ref, weigh_ref, coef_ref, kernel_ref):
    rows = starts_ref.shape[0]
    count = durations_ref.shape[0]
    sfts = antenna_ref.shape[1]
    sft = iota((rows, sfts), 1)
    sft = jnp.where(sft // run == 0, sft + first * run, jnp.where(sft // run == first, sft - first * run, sft))
    start = starts_ref[:, 0:1]
    after = sft >= start
    for j in range(count):
        inside = after & (sft < start + durations_ref[j])
        mask_ref[pl.ds(j * rows, rows), :] = jnp.where(inside, 1.0, 0.0).astype(jnp.bfloat16)
    antenna = jnp.concatenate([antenna_ref[...], jnp.zeros((4, sfts), jnp.float32)], axis=0)
    place = iota(antenna.shape, 1) // run
    after = pltpu.roll(antenna, sfts - first * run, 1)
    before = pltpu.roll(antenna, first * run, 1)
    antenna = jnp.where(place == 0, after, jnp.where(place == first, before, antenna))
    a1, a2, b1, b2 = (antenna[n : n + 1] for n in range(4))
    terms = jnp.concatenate([a1 * a1 + a2 * a2, b1 * b1 + b2 * b2, a1 * b1 + a2 * b2, jnp.zeros((5, sfts), jnp.float32)], axis=0)
    weights = sum(lax.dot_general(mask_ref[...], part, NT, preferred_element_type=jnp.float32) for part in split(terms, 3))
    wa, wb, wc = (weights[:, n : n + 1] for n in range(3))
    shape = (rows * count, LANES)
    late = iota(shape, 1) >= LANES // 2
    coef_ref[0] = jnp.broadcast_to(1.0 / wa, shape)
    coef_ref[1] = jnp.broadcast_to(wa / (wa * wb - wc * wc), shape)
    coef_ref[2] = jnp.where(late, jnp.broadcast_to(wc / wa, shape), 0.0)
    upright = jnp.transpose(jnp.concatenate([antenna, jnp.zeros((LANES - 8, sfts), jnp.float32)], axis=0))
    shape = (sfts, LANES)
    late = iota(shape, 1) >= LANES // 2
    weigh_ref[0] = jnp.where(late, upright[:, 3:4], upright[:, 0:1])
    weigh_ref[1] = jnp.where(late, upright[:, 2:3], upright[:, 1:2])
    fractions = fractions_ref[...]
    templates = fractions.shape[1]
    blocks = kernel_ref.shape[1] // (4 * LANES)
    bin_id = iota((W, templates), 0)
    distance = fractions + (W // 2 - 1) - bin_id.astype(jnp.float32)
    alternate = 1.0 - 2.0 * (bin_id % 2).astype(jnp.float32)
    values = (alternate * jnp.sin(jnp.pi * fractions) / (jnp.pi * distance)).astype(jnp.bfloat16)
    kernel_ref[...] = jnp.zeros_like(kernel_ref)
    for part in range(2):
        for c in range(4):
            for b in range(blocks):
                row = ((part * 4 + c) * blocks + b) * W
                column = (c * blocks + b) * LANES
                kernel_ref[pl.ds(row, W), pl.ds(column, LANES)] = values[:, b * LANES : (b + 1) * LANES]


def prepare(durations, starts, antenna, fractions, first, run):
    count, rows, sfts = durations.shape[0], starts.shape[0], antenna.shape[0]
    columns = 4 * fractions.shape[0]
    features = 4 * W * (fractions.shape[0] // LANES)
    vmem = pl.BlockSpec(memory_space=pltpu.VMEM)
    return pl.pallas_call(
        functools.partial(prepare_kernel, first, run),
        out_shape=(
            jax.ShapeDtypeStruct((count * rows, sfts), jnp.bfloat16),
            jax.ShapeDtypeStruct((2, sfts, LANES), jnp.float32),
            jax.ShapeDtypeStruct((3, count * rows, LANES), jnp.float32),
            jax.ShapeDtypeStruct((2 * features, columns), jnp.bfloat16),
        ),
        in_specs=[pl.BlockSpec(memory_space=pltpu.SMEM), vmem, vmem, vmem],
        out_specs=(vmem,) * 4,
        compiler_params=pltpu.CompilerParams(vmem_limit_bytes=16 * 1024 * 1024),
        cost_estimate=pl.CostEstimate(flops=100_000_000, bytes_accessed=4_000_000, transcendentals=0),
        name="prepare",
    )(durations, jnp.broadcast_to(starts[:, None], (rows, LANES)), antenna.T, fractions[None, :])


def statistic_kernel(windows_ref, mask_ref, weigh_ref, coef_ref, kernel_ref, map_ref, loudest_ref):
    values = windows_ref[...].astype(jnp.float32)
    half = LANES // 2
    weighted = (weigh_ref[0] * values + weigh_ref[1] * pltpu.roll(values, half, 1)).astype(jnp.bfloat16)
    templates = map_ref.shape[1]
    rows = map_ref.shape[0] // loudest_ref.shape[1]
    copies = loudest_ref.shape[0]
    per_step = LANES // rows
    for step in range(map_ref.shape[0] // LANES):
        here = pl.ds(step * LANES, LANES)
        sums = jnp.dot(mask_ref[here, :], weighted, preferred_element_type=jnp.float32)
        sums = sums - coef_ref[2, here, :] * pltpu.roll(sums, half, 1)
        parts = jnp.concatenate(split(sums, 2), axis=1)
        found = jnp.dot(parts, kernel_ref[...], preferred_element_type=jnp.float32)
        ra, ia, rb, ib = (found[:, c * templates : (c + 1) * templates] for c in range(4))
        power_a, power_b = ra * ra + ia * ia, rb * rb + ib * ib
        best = None
        for b in range(templates // LANES):
            columns = slice(b * LANES, (b + 1) * LANES)
            result = coef_ref[0, here, :] * power_a[:, columns] + coef_ref[1, here, :] * power_b[:, columns]
            map_ref[here, columns] = result
            best = result if best is None else jnp.maximum(best, result)
        best = jnp.max(jnp.transpose(best), axis=0, keepdims=True)
        for n in range(per_step):
            turned = best if n == 0 else pltpu.roll(best, LANES - n * rows, 1)
            for copy in range(copies):
                loudest_ref[copy, pl.ds(step * per_step + n, 1), :] = turned


def statistic(windows, mask, weigh, coef, kernel, rows, copies):
    count = mask.shape[0] // rows
    templates = kernel.shape[1] // 4
    vmem = pl.BlockSpec(memory_space=pltpu.VMEM)
    return pl.pallas_call(
        statistic_kernel,
        out_shape=(
            jax.ShapeDtypeStruct((count * rows, templates), jnp.float32),
            jax.ShapeDtypeStruct((copies, count, LANES), jnp.float32),
        ),
        in_specs=[vmem] * 5,
        out_specs=(vmem, vmem),
        compiler_params=pltpu.CompilerParams(vmem_limit_bytes=16 * 1024 * 1024),
        cost_estimate=pl.CostEstimate(flops=400_000_000, bytes_accessed=4_000_000, transcendentals=0),
        name="statistic",
    )(windows, mask, weigh, coef, kernel)


def exchange(values, axis, members):
    return lax.all_to_all(values, axis, split_axis=0, concat_axis=0, axis_index_groups=[members], tiled=True)


def body(spectra, offsets, fractions, antenna, starts, durations):
    bands, cores = lax.axis_size("tmpl"), lax.axis_size("tm")
    sft_rows = spectra.shape[0]
    grid_size = starts.shape[0]
    my_rows = grid_size // cores
    me = lax.axis_index("tmpl").astype(jnp.int32)[None]
    by_band = order(bands, bands // 2)
    first = (cores - 1) * bands + bands // 2
    by_run = order(cores * bands, first)
    known = exchange(jnp.broadcast_to(offsets.T[None], (bands,) + offsets.T.shape), "tmpl", by_band)
    my_durations = lax.dynamic_slice_in_dim(durations, lax.axis_index("tm") * my_rows, my_rows, 0)
    windows = pick(me, known, hold(spectra), by_band, [run % bands for run in by_run])
    windows, my_durations = lax.optimization_barrier((windows, my_durations))
    prepared = prepare(my_durations, starts, antenna, fractions, first, sft_rows)
    arrived = exchange(windows.reshape(cores * bands, sft_rows, LANES), ("tm", "tmpl"), by_run)
    fstat_map, loudest = statistic(arrived.reshape(-1, LANES), *prepared, grid_size, bands)
    loudest = jnp.max(exchange(loudest, "tmpl", by_band)[:, :, :grid_size], axis=0)
    return (fstat_map.reshape(my_rows, grid_size, -1), loudest)


def solution(mesh):
    in_specs = (
        P(("grp", "tm", "tmpl"), None, None),
        P(("grp", "tm"), "tmpl"),
        P(("grp", "tmpl")),
        P("grp", None),
        P("grp"),
        P("grp"),
    )
    out_specs = (P("tm", None, ("grp", "tmpl")), P(("grp", "tm"), None))
    return jax.shard_map(body, mesh=mesh, in_specs=in_specs, out_specs=out_specs, check_vma=False)
```

```python
import functools

import jax
import jax.numpy as jnp
from jax import lax
from jax.experimental import pallas as pl
from jax.experimental.pallas import tpu as pltpu
from jax.sharding import PartitionSpec as P

W = 16
LANES = 128
NT = (((1,), (1,)), ((), ()))


def iota(shape, axis):
    return lax.broadcasted_iota(jnp.int32, shape, axis)


def order(size, first):
    members = list(range(size))
    members[0], members[first] = first, 0
    return members


def hold_kernel(spec_ref, out_ref, sem):
    copy = pltpu.make_async_copy(spec_ref, out_ref, sem)
    copy.start()
    copy.wait()


def hold(spectra):
    return pl.pallas_call(
        hold_kernel,
        out_shape=jax.ShapeDtypeStruct(spectra.shape, spectra.dtype),
        in_specs=[pl.BlockSpec(memory_space=pl.ANY)],
        out_specs=pl.BlockSpec(memory_space=pltpu.VMEM),
        scratch_shapes=[pltpu.SemaphoreType.DMA],
        compiler_params=pltpu.CompilerParams(vmem_limit_bytes=8 * 1024 * 1024),
        cost_estimate=pl.CostEstimate(flops=0, bytes_accessed=4 * spectra.size, transcendentals=0),
        name="hold",
    )(spectra)


def pick_kernel(bands_in, bands_out, me_ref, offset_ref, spec_ref, out_ref, place_ref, turn_ref, tile_ref, sem):
    rows, _, bins = spec_ref.shape
    bands, blocks, _ = offset_ref.shape
    band_width = bins // bands
    groups = rows // 8
    chunks = band_width // LANES
    width = blocks * W
    first = me_ref[0] * rows
    columns = pl.ds(pl.multiple_of(first // LANES * LANES, LANES), LANES)
    offsets = jnp.concatenate([offset_ref[bands_in.index(band), :, columns] for band in range(bands)], axis=0).astype(jnp.float32)
    lane = iota(offsets.shape, 1)
    offsets = jnp.take_along_axis(offsets, (lane >> 2) + first & (LANES - 1), axis=1, mode="promise_in_bounds")
    offsets = jnp.concatenate([offsets, jnp.zeros((LANES - bands * blocks, LANES), jnp.float32)], axis=0)
    upright = jnp.transpose(offsets).astype(jnp.int32)
    lane = iota((32, LANES), 1)
    places = upright[0:32]
    for group in range(1, groups):
        turned = pltpu.roll(upright[group * 32 : group * 32 + 32], group * bands * blocks, 1)
        places = jnp.where(lane < group * bands * blocks, places, turned)
    lane = iota((8, LANES), 1)
    lane_group = lane // width
    source = lane_group * (bands * blocks) + lane // W % blocks
    for band in range(bands):
        for pair in range(4):
            place = jnp.take_along_axis(places[pair * 8 : pair * 8 + 8], source + band * blocks, axis=1, mode="promise_in_bounds")
            place_ref[band, pair] = place + ((lane & (W - 1)) + lane_group * band_width)

    def step(band, carry):
        for pair in range(4):
            place = place_ref[band, pair]
            lane_id = place & (LANES - 1)
            chosen = place >> 7
            tile = jnp.zeros((8, LANES), jnp.float32)
            for group in range(groups):
                for chunk in range(chunks):
                    start = pl.multiple_of(band * band_width + chunk * LANES, LANES)
                    values = spec_ref[pl.ds(group * 8 + pair * 2, 2), :, pl.ds(start, LANES)]
                    values = values.astype(jnp.float32).reshape(8, LANES)
                    moved = jnp.take_along_axis(values, lane_id, axis=1, mode="promise_in_bounds")
                    tile = jnp.where(chosen == group * chunks + chunk, moved, tile)
            turn_ref[band, pl.ds(pair * 8, 8), :] = tile
        return carry

    lax.fori_loop(0, bands, step, 0)
    tiles = {}
    for band in range(bands):
        parts = [turn_ref[band, pl.ds(part, 8, stride=4), :] for part in range(4)]
        for group in range(groups):
            tile = jnp.zeros((8, LANES), jnp.float32)
            for part in range(4):
                amount = (part - group) * width % LANES
                turned = pltpu.roll(parts[part], amount, 1) if amount else parts[part]
                tile = jnp.where(lane_group == part, turned, tile)
            tiles[band, group] = tile
    wanted = [tiles[band, group] for band in bands_out for group in range(groups)]
    for n in range(0, len(wanted), 2):
        tile_ref[n * 8 : n * 8 + 16, :] = jnp.concatenate(wanted[n : n + 2], axis=0).astype(jnp.bfloat16)
    copy = pltpu.make_async_copy(tile_ref, out_ref, sem)
    copy.start()
    copy.wait()


def pick(me, offsets, spectra, bands_in, bands_out):
    rows, bands = spectra.shape[0], offsets.shape[0]
    out_rows = len(bands_out) * rows
    vmem = pl.BlockSpec(memory_space=pltpu.VMEM)
    return pl.pallas_call(
        functools.partial(pick_kernel, bands_in, bands_out),
        out_shape=jax.ShapeDtypeStruct((out_rows, LANES), jnp.bfloat16),
        in_specs=[pl.BlockSpec(memory_space=pltpu.SMEM), vmem, vmem],
        out_specs=pl.BlockSpec(memory_space=pl.ANY),
        scratch_shapes=[
            pltpu.VMEM((bands, 4, 8, LANES), jnp.int32),
            pltpu.VMEM((bands, 32, LANES), jnp.float32),
            pltpu.VMEM((out_rows, LANES), jnp.bfloat16),
            pltpu.SemaphoreType.DMA,
        ],
        compiler_params=pltpu.CompilerParams(vmem_limit_bytes=8 * 1024 * 1024),
        cost_estimate=pl.CostEstimate(flops=10_000_000, bytes_accessed=2 * spectra.size, transcendentals=0),
        name="pick",
    )(me, offsets, spectra)


def split(values, count):
    parts = []
    for _ in range(count):
        part = values.astype(jnp.bfloat16)
        parts.append(part)
        values = values - part.astype(jnp.float32)
    return parts


def prepare_kernel(first, run, durations_ref, starts_ref, antenna_ref, fractions_ref, mask_ref, weigh_ref, coef_ref, kernel_ref):
    rows = starts_ref.shape[0]
    count = durations_ref.shape[0]
    sfts = antenna_ref.shape[1]
    sft = iota((rows, sfts), 1)
    sft = jnp.where(sft // run == 0, sft + first * run, jnp.where(sft // run == first, sft - first * run, sft))
    start = starts_ref[:, 0:1]
    after = sft >= start
    for j in range(count):
        inside = after & (sft < start + durations_ref[j])
        mask_ref[pl.ds(j * rows, rows), :] = jnp.where(inside, 1.0, 0.0).astype(jnp.bfloat16)
    antenna = jnp.concatenate([antenna_ref[...], jnp.zeros((4, sfts), jnp.float32)], axis=0)
    place = iota(antenna.shape, 1) // run
    after = pltpu.roll(antenna, sfts - first * run, 1)
    before = pltpu.roll(antenna, first * run, 1)
    antenna = jnp.where(place == 0, after, jnp.where(place == first, before, antenna))
    a1, a2, b1, b2 = (antenna[n : n + 1] for n in range(4))
    terms = jnp.concatenate([a1 * a1 + a2 * a2, b1 * b1 + b2 * b2, a1 * b1 + a2 * b2, jnp.zeros((5, sfts), jnp.float32)], axis=0)
    weights = sum(lax.dot_general(mask_ref[...], part, NT, preferred_element_type=jnp.float32) for part in split(terms, 3))
    wa, wb, wc = (weights[:, n : n + 1] for n in range(3))
    shape = (rows * count, LANES)
    late = iota(shape, 1) >= LANES // 2
    coef_ref[0] = jnp.broadcast_to(1.0 / wa, shape)
    coef_ref[1] = jnp.broadcast_to(wa / (wa * wb - wc * wc), shape)
    coef_ref[2] = jnp.where(late, jnp.broadcast_to(wc / wa, shape), 0.0)
    upright = jnp.transpose(jnp.concatenate([antenna, jnp.zeros((LANES - 8, sfts), jnp.float32)], axis=0))
    shape = (sfts, LANES)
    late = iota(shape, 1) >= LANES // 2
    weigh_ref[0] = jnp.where(late, upright[:, 3:4], upright[:, 0:1])
    weigh_ref[1] = jnp.where(late, upright[:, 2:3], upright[:, 1:2])
    fractions = fractions_ref[...]
    templates = fractions.shape[1]
    blocks = kernel_ref.shape[1] // (4 * LANES)
    bin_id = iota((W, templates), 0)
    distance = fractions + (W // 2 - 1) - bin_id.astype(jnp.float32)
    alternate = 1.0 - 2.0 * (bin_id % 2).astype(jnp.float32)
    values = (alternate * jnp.sin(jnp.pi * fractions) / (jnp.pi * distance)).astype(jnp.bfloat16)
    kernel_ref[...] = jnp.zeros_like(kernel_ref)
    for part in range(2):
        for c in range(4):
            for b in range(blocks):
                row = ((part * 4 + c) * blocks + b) * W
                column = (c * blocks + b) * LANES
                kernel_ref[pl.ds(row, W), pl.ds(column, LANES)] = values[:, b * LANES : (b + 1) * LANES]


def prepare(durations, starts, antenna, fractions, first, run):
    count, rows, sfts = durations.shape[0], starts.shape[0], antenna.shape[0]
    columns = 4 * fractions.shape[0]
    features = 4 * W * (fractions.shape[0] // LANES)
    vmem = pl.BlockSpec(memory_space=pltpu.VMEM)
    return pl.pallas_call(
        functools.partial(prepare_kernel, first, run),
        out_shape=(
            jax.ShapeDtypeStruct((count * rows, sfts), jnp.bfloat16),
            jax.ShapeDtypeStruct((2, sfts, LANES), jnp.float32),
            jax.ShapeDtypeStruct((3, count * rows, LANES), jnp.float32),
            jax.ShapeDtypeStruct((2 * features, columns), jnp.bfloat16),
        ),
        in_specs=[pl.BlockSpec(memory_space=pltpu.SMEM), vmem, vmem, vmem],
        out_specs=(vmem,) * 4,
        compiler_params=pltpu.CompilerParams(vmem_limit_bytes=16 * 1024 * 1024),
        cost_estimate=pl.CostEstimate(flops=100_000_000, bytes_accessed=4_000_000, transcendentals=0),
        name="prepare",
    )(durations, jnp.broadcast_to(starts[:, None], (rows, LANES)), antenna.T, fractions[None, :])


def statistic_kernel(windows_ref, mask_ref, weigh_ref, coef_ref, kernel_ref, map_ref, loudest_ref):
    values = windows_ref[...].astype(jnp.float32)
    half = LANES // 2
    weighted = (weigh_ref[0] * values + weigh_ref[1] * pltpu.roll(values, half, 1)).astype(jnp.bfloat16)
    templates = map_ref.shape[1]
    rows = map_ref.shape[0] // loudest_ref.shape[1]
    copies = loudest_ref.shape[0]
    per_step = LANES // rows
    for step in range(map_ref.shape[0] // LANES):
        here = pl.ds(step * LANES, LANES)
        sums = jnp.dot(mask_ref[here, :], weighted, preferred_element_type=jnp.float32)
        sums = sums - coef_ref[2, here, :] * pltpu.roll(sums, half, 1)
        parts = jnp.concatenate(split(sums, 2), axis=1)
        found = jnp.dot(parts, kernel_ref[...], preferred_element_type=jnp.float32)
        ra, ia, rb, ib = (found[:, c * templates : (c + 1) * templates] for c in range(4))
        power_a, power_b = ra * ra + ia * ia, rb * rb + ib * ib
        best = None
        for b in range(templates // LANES):
            columns = slice(b * LANES, (b + 1) * LANES)
            result = coef_ref[0, here, :] * power_a[:, columns] + coef_ref[1, here, :] * power_b[:, columns]
            map_ref[here, columns] = result
            best = result if best is None else jnp.maximum(best, result)
        best = jnp.max(jnp.transpose(best), axis=0, keepdims=True)
        for n in range(per_step):
            turned = best if n == 0 else pltpu.roll(best, LANES - n * rows, 1)
            for copy in range(copies):
                loudest_ref[copy, pl.ds(step * per_step + n, 1), :] = turned


def statistic(windows, mask, weigh, coef, kernel, rows, copies):
    count = mask.shape[0] // rows
    templates = kernel.shape[1] // 4
    vmem = pl.BlockSpec(memory_space=pltpu.VMEM)
    return pl.pallas_call(
        statistic_kernel,
        out_shape=(
            jax.ShapeDtypeStruct((count * rows, templates), jnp.float32),
            jax.ShapeDtypeStruct((copies, count, LANES), jnp.float32),
        ),
        in_specs=[vmem] * 5,
        out_specs=(vmem, vmem),
        compiler_params=pltpu.CompilerParams(vmem_limit_bytes=16 * 1024 * 1024),
        cost_estimate=pl.CostEstimate(flops=400_000_000, bytes_accessed=4_000_000, transcendentals=0),
        name="statistic",
    )(windows, mask, weigh, coef, kernel)


def exchange(values, axis, members):
    return lax.all_to_all(values, axis, split_axis=0, concat_axis=0, axis_index_groups=[members], tiled=True)


def body(spectra, offsets, fractions, antenna, starts, durations):
    bands, cores = lax.axis_size("tmpl"), lax.axis_size("tm")
    sft_rows = spectra.shape[0]
    grid_size = starts.shape[0]
    my_rows = grid_size // cores
    me = lax.axis_index("tmpl").astype(jnp.int32)[None]
    first = bands // 2 + 1
    by_band = order(bands, first)
    by_run = order(cores * bands, first)
    known = exchange(jnp.broadcast_to(offsets.T[None], (bands,) + offsets.T.shape), "tmpl", by_band)
    my_durations = lax.dynamic_slice_in_dim(durations, lax.axis_index("tm") * my_rows, my_rows, 0)
    windows = pick(me, known, hold(spectra), by_band, [run % bands for run in by_run])
    windows, my_durations = lax.optimization_barrier((windows, my_durations))
    prepared = prepare(my_durations, starts, antenna, fractions, first, sft_rows)
    arrived = exchange(windows.reshape(cores * bands, sft_rows, LANES), ("tm", "tmpl"), by_run)
    fstat_map, loudest = statistic(arrived.reshape(-1, LANES), *prepared, grid_size, bands)
    loudest = jnp.max(exchange(loudest, "tmpl", by_band)[:, :, :grid_size], axis=0)
    return (fstat_map.reshape(my_rows, grid_size, -1), loudest)


def solution(mesh):
    in_specs = (
        P(("grp", "tm", "tmpl"), None, None),
        P(("grp", "tm"), "tmpl"),
        P(("grp", "tmpl")),
        P("grp", None),
        P("grp"),
        P("grp"),
    )
    out_specs = (P("tm", None, ("grp", "tmpl")), P(("grp", "tm"), None))
    return jax.shard_map(body, mesh=mesh, in_specs=in_specs, out_specs=out_specs, check_vma=False)
```

```python
import functools

import jax
import jax.numpy as jnp
from jax import lax
from jax.experimental import pallas as pl
from jax.experimental.pallas import tpu as pltpu
from jax.sharding import PartitionSpec as P

W = 16
LANES = 128
NT = (((1,), (1,)), ((), ()))


def iota(shape, axis):
    return lax.broadcasted_iota(jnp.int32, shape, axis)


def order(size, first):
    members = list(range(size))
    members[0], members[first] = first, 0
    return members


def hold_kernel(spec_ref, out_ref, sem):
    copy = pltpu.make_async_copy(spec_ref, out_ref, sem)
    copy.start()
    copy.wait()


def hold(spectra):
    return pl.pallas_call(
        hold_kernel,
        out_shape=jax.ShapeDtypeStruct(spectra.shape, spectra.dtype),
        in_specs=[pl.BlockSpec(memory_space=pl.ANY)],
        out_specs=pl.BlockSpec(memory_space=pltpu.VMEM),
        scratch_shapes=[pltpu.SemaphoreType.DMA],
        compiler_params=pltpu.CompilerParams(vmem_limit_bytes=8 * 1024 * 1024),
        cost_estimate=pl.CostEstimate(flops=0, bytes_accessed=4 * spectra.size, transcendentals=0),
        name="hold",
    )(spectra)


def pick_kernel(bands_in, bands_out, me_ref, offset_ref, spec_ref, out_ref, place_ref, turn_ref, tile_ref, sem):
    rows, _, bins = spec_ref.shape
    bands, blocks, _ = offset_ref.shape
    band_width = bins // bands
    groups = rows // 8
    chunks = band_width // LANES
    width = blocks * W
    first = me_ref[0] * rows
    columns = pl.ds(pl.multiple_of(first // LANES * LANES, LANES), LANES)
    offsets = jnp.concatenate([offset_ref[bands_in.index(band), :, columns] for band in range(bands)], axis=0).astype(jnp.float32)
    lane = iota(offsets.shape, 1)
    offsets = jnp.take_along_axis(offsets, (lane >> 2) + first & (LANES - 1), axis=1, mode="promise_in_bounds")
    offsets = jnp.concatenate([offsets, jnp.zeros((LANES - bands * blocks, LANES), jnp.float32)], axis=0)
    upright = jnp.transpose(offsets).astype(jnp.int32)
    lane = iota((32, LANES), 1)
    places = upright[0:32]
    for group in range(1, groups):
        turned = pltpu.roll(upright[group * 32 : group * 32 + 32], group * bands * blocks, 1)
        places = jnp.where(lane < group * bands * blocks, places, turned)
    lane = iota((8, LANES), 1)
    lane_group = lane // width
    source = lane_group * (bands * blocks) + lane // W % blocks
    for band in range(bands):
        for pair in range(4):
            place = jnp.take_along_axis(places[pair * 8 : pair * 8 + 8], source + band * blocks, axis=1, mode="promise_in_bounds")
            place_ref[band, pair] = place + ((lane & (W - 1)) + lane_group * band_width)

    def step(band, carry):
        for pair in range(4):
            place = place_ref[band, pair]
            lane_id = place & (LANES - 1)
            chosen = place >> 7
            tile = jnp.zeros((8, LANES), jnp.float32)
            for group in range(groups):
                for chunk in range(chunks):
                    start = pl.multiple_of(band * band_width + chunk * LANES, LANES)
                    values = spec_ref[pl.ds(group * 8 + pair * 2, 2), :, pl.ds(start, LANES)]
                    values = values.astype(jnp.float32).reshape(8, LANES)
                    moved = jnp.take_along_axis(values, lane_id, axis=1, mode="promise_in_bounds")
                    tile = jnp.where(chosen == group * chunks + chunk, moved, tile)
            turn_ref[band, pl.ds(pair * 8, 8), :] = tile
        return carry

    lax.fori_loop(0, bands, step, 0)
    tiles = {}
    for band in range(bands):
        parts = [turn_ref[band, pl.ds(part, 8, stride=4), :] for part in range(4)]
        for group in range(groups):
            tile = jnp.zeros((8, LANES), jnp.float32)
            for part in range(4):
                amount = (part - group) * width % LANES
                turned = pltpu.roll(parts[part], amount, 1) if amount else parts[part]
                tile = jnp.where(lane_group == part, turned, tile)
            tiles[band, group] = tile
    wanted = [tiles[band, group] for band in bands_out for group in range(groups)]
    for n in range(0, len(wanted), 2):
        tile_ref[n * 8 : n * 8 + 16, :] = jnp.concatenate(wanted[n : n + 2], axis=0).astype(jnp.bfloat16)
    copy = pltpu.make_async_copy(tile_ref, out_ref, sem)
    copy.start()
    copy.wait()


def pick(me, offsets, spectra, bands_in, bands_out):
    rows, bands = spectra.shape[0], offsets.shape[0]
    out_rows = len(bands_out) * rows
    vmem = pl.BlockSpec(memory_space=pltpu.VMEM)
    return pl.pallas_call(
        functools.partial(pick_kernel, bands_in, bands_out),
        out_shape=jax.ShapeDtypeStruct((out_rows, LANES), jnp.bfloat16),
        in_specs=[pl.BlockSpec(memory_space=pltpu.SMEM), vmem, vmem],
        out_specs=pl.BlockSpec(memory_space=pl.ANY),
        scratch_shapes=[
            pltpu.VMEM((bands, 4, 8, LANES), jnp.int32),
            pltpu.VMEM((bands, 32, LANES), jnp.float32),
            pltpu.VMEM((out_rows, LANES), jnp.bfloat16),
            pltpu.SemaphoreType.DMA,
        ],
        compiler_params=pltpu.CompilerParams(vmem_limit_bytes=8 * 1024 * 1024),
        cost_estimate=pl.CostEstimate(flops=10_000_000, bytes_accessed=2 * spectra.size, transcendentals=0),
        name="pick",
    )(me, offsets, spectra)


def split(values, count):
    parts = []
    for _ in range(count):
        part = values.astype(jnp.bfloat16)
        parts.append(part)
        values = values - part.astype(jnp.float32)
    return parts


def prepare_kernel(first, run, durations_ref, starts_ref, antenna_ref, fractions_ref, mask_ref, weigh_ref, coef_ref, kernel_ref):
    rows = starts_ref.shape[0]
    count = durations_ref.shape[0]
    sfts = antenna_ref.shape[1]
    sft = iota((rows, sfts), 1)
    sft = jnp.where(sft // run == 0, sft + first * run, jnp.where(sft // run == first, sft - first * run, sft))
    start = starts_ref[:, 0:1]
    after = sft >= start
    for j in range(count):
        inside = after & (sft < start + durations_ref[j])
        mask_ref[pl.ds(j * rows, rows), :] = jnp.where(inside, 1.0, 0.0).astype(jnp.bfloat16)
    antenna = jnp.concatenate([antenna_ref[...], jnp.zeros((4, sfts), jnp.float32)], axis=0)
    place = iota(antenna.shape, 1) // run
    after = pltpu.roll(antenna, sfts - first * run, 1)
    before = pltpu.roll(antenna, first * run, 1)
    antenna = jnp.where(place == 0, after, jnp.where(place == first, before, antenna))
    a1, a2, b1, b2 = (antenna[n : n + 1] for n in range(4))
    terms = jnp.concatenate([a1 * a1 + a2 * a2, b1 * b1 + b2 * b2, a1 * b1 + a2 * b2, jnp.zeros((5, sfts), jnp.float32)], axis=0)
    weights = sum(lax.dot_general(mask_ref[...], part, NT, preferred_element_type=jnp.float32) for part in split(terms, 3))
    wa, wb, wc = (weights[:, n : n + 1] for n in range(3))
    shape = (rows * count, LANES)
    late = iota(shape, 1) >= LANES // 2
    coef_ref[0] = jnp.broadcast_to(1.0 / wa, shape)
    coef_ref[1] = jnp.broadcast_to(wa / (wa * wb - wc * wc), shape)
    coef_ref[2] = jnp.where(late, jnp.broadcast_to(wc / wa, shape), 0.0)
    upright = jnp.transpose(jnp.concatenate([antenna, jnp.zeros((LANES - 8, sfts), jnp.float32)], axis=0))
    shape = (sfts, LANES)
    late = iota(shape, 1) >= LANES // 2
    weigh_ref[0] = jnp.where(late, upright[:, 3:4], upright[:, 0:1])
    weigh_ref[1] = jnp.where(late, upright[:, 2:3], upright[:, 1:2])
    fractions = fractions_ref[...]
    templates = fractions.shape[1]
    blocks = kernel_ref.shape[1] // (4 * LANES)
    bin_id = iota((W, templates), 0)
    distance = fractions + (W // 2 - 1) - bin_id.astype(jnp.float32)
    alternate = 1.0 - 2.0 * (bin_id % 2).astype(jnp.float32)
    values = (alternate * jnp.sin(jnp.pi * fractions) / (jnp.pi * distance)).astype(jnp.bfloat16)
    kernel_ref[...] = jnp.zeros_like(kernel_ref)
    for part in range(2):
        for c in range(4):
            for b in range(blocks):
                row = ((part * 4 + c) * blocks + b) * W
                column = (c * blocks + b) * LANES
                kernel_ref[pl.ds(row, W), pl.ds(column, LANES)] = values[:, b * LANES : (b + 1) * LANES]


def prepare(durations, starts, antenna, fractions, first, run):
    count, rows, sfts = durations.shape[0], starts.shape[0], antenna.shape[0]
    columns = 4 * fractions.shape[0]
    features = 4 * W * (fractions.shape[0] // LANES)
    vmem = pl.BlockSpec(memory_space=pltpu.VMEM)
    return pl.pallas_call(
        functools.partial(prepare_kernel, first, run),
        out_shape=(
            jax.ShapeDtypeStruct((count * rows, sfts), jnp.bfloat16),
            jax.ShapeDtypeStruct((2, sfts, LANES), jnp.float32),
            jax.ShapeDtypeStruct((3, count * rows, LANES), jnp.float32),
            jax.ShapeDtypeStruct((2 * features, columns), jnp.bfloat16),
        ),
        in_specs=[pl.BlockSpec(memory_space=pltpu.SMEM), vmem, vmem, vmem],
        out_specs=(vmem,) * 4,
        compiler_params=pltpu.CompilerParams(vmem_limit_bytes=16 * 1024 * 1024),
        cost_estimate=pl.CostEstimate(flops=100_000_000, bytes_accessed=4_000_000, transcendentals=0),
        name="prepare",
    )(durations, jnp.broadcast_to(starts[:, None], (rows, LANES)), antenna.T, fractions[None, :])


def statistic_kernel(windows_ref, mask_ref, weigh_ref, coef_ref, kernel_ref, map_ref, loudest_ref, found_ref):
    values = windows_ref[...].astype(jnp.float32)
    half = LANES // 2
    weighted = (weigh_ref[0] * values + weigh_ref[1] * pltpu.roll(values, half, 1)).astype(jnp.bfloat16)
    sums = jnp.dot(mask_ref[...], weighted, preferred_element_type=jnp.float32)
    sums = sums - coef_ref[2] * pltpu.roll(sums, half, 1)
    parts = jnp.concatenate(split(sums, 2), axis=1)
    found_ref[...] = jnp.dot(parts, kernel_ref[...], preferred_element_type=jnp.float32)
    templates = map_ref.shape[1]
    rows = map_ref.shape[0] // loudest_ref.shape[1]
    copies = loudest_ref.shape[0]
    per_step = LANES // rows
    for step in range(map_ref.shape[0] // LANES):
        here = pl.ds(step * LANES, LANES)
        best = None
        for b in range(templates // LANES):
            ra, ia, rb, ib = (found_ref[here, pl.ds(c * templates + b * LANES, LANES)] for c in range(4))
            result = coef_ref[0, here, :] * (ra * ra + ia * ia) + coef_ref[1, here, :] * (rb * rb + ib * ib)
            map_ref[here, pl.ds(b * LANES, LANES)] = result
            best = result if best is None else jnp.maximum(best, result)
        best = jnp.max(jnp.transpose(best), axis=0, keepdims=True)
        for n in range(per_step):
            turned = best if n == 0 else pltpu.roll(best, LANES - n * rows, 1)
            for copy in range(copies):
                loudest_ref[copy, pl.ds(step * per_step + n, 1), :] = turned


def statistic(windows, mask, weigh, coef, kernel, rows, copies):
    count = mask.shape[0] // rows
    templates = kernel.shape[1] // 4
    vmem = pl.BlockSpec(memory_space=pltpu.VMEM)
    return pl.pallas_call(
        statistic_kernel,
        out_shape=(
            jax.ShapeDtypeStruct((count * rows, templates), jnp.float32),
            jax.ShapeDtypeStruct((copies, count, LANES), jnp.float32),
        ),
        in_specs=[vmem] * 5,
        out_specs=(vmem, vmem),
        scratch_shapes=[pltpu.VMEM((count * rows, 4 * templates), jnp.float32)],
        compiler_params=pltpu.CompilerParams(vmem_limit_bytes=16 * 1024 * 1024),
        cost_estimate=pl.CostEstimate(flops=400_000_000, bytes_accessed=4_000_000, transcendentals=0),
        name="statistic",
    )(windows, mask, weigh, coef, kernel)


def exchange(values, axis, members):
    return lax.all_to_all(values, axis, split_axis=0, concat_axis=0, axis_index_groups=[members], tiled=True)


def body(spectra, offsets, fractions, antenna, starts, durations):
    bands, cores = lax.axis_size("tmpl"), lax.axis_size("tm")
    sft_rows = spectra.shape[0]
    grid_size = starts.shape[0]
    my_rows = grid_size // cores
    me = lax.axis_index("tmpl").astype(jnp.int32)[None]
    by_band = order(bands, bands // 2 + 1)
    first = (cores - 1) * bands + bands // 2
    by_run = order(cores * bands, first)
    known = exchange(jnp.broadcast_to(offsets.T[None], (bands,) + offsets.T.shape), "tmpl", by_band)
    my_durations = lax.dynamic_slice_in_dim(durations, lax.axis_index("tm") * my_rows, my_rows, 0)
    windows = pick(me, known, hold(spectra), by_band, [run % bands for run in by_run])
    windows, my_durations = lax.optimization_barrier((windows, my_durations))
    prepared = prepare(my_durations, starts, antenna, fractions, first, sft_rows)
    arrived = exchange(windows.reshape(cores * bands, sft_rows, LANES), ("tm", "tmpl"), by_run)
    fstat_map, loudest = statistic(arrived.reshape(-1, LANES), *prepared, grid_size, bands)
    loudest = jnp.max(exchange(loudest, "tmpl", order(bands, bands // 2))[:, :, :grid_size], axis=0)
    return (fstat_map.reshape(my_rows, grid_size, -1), loudest)


def solution(mesh):
    in_specs = (
        P(("grp", "tm", "tmpl"), None, None),
        P(("grp", "tm"), "tmpl"),
        P(("grp", "tmpl")),
        P("grp", None),
        P("grp"),
        P("grp"),
    )
    out_specs = (P("tm", None, ("grp", "tmpl")), P(("grp", "tm"), None))
    return jax.shard_map(body, mesh=mesh, in_specs=in_specs, out_specs=out_specs, check_vma=False)
```

```python
import functools

import jax
import jax.numpy as jnp
from jax import lax
from jax.experimental import pallas as pl
from jax.experimental.pallas import tpu as pltpu
from jax.sharding import PartitionSpec as P

W = 16
LANES = 128
NT = (((1,), (1,)), ((), ()))


def iota(shape, axis):
    return lax.broadcasted_iota(jnp.int32, shape, axis)


def order(size, first):
    members = list(range(size))
    members[0], members[first] = first, 0
    return members


def hold_kernel(spec_ref, out_ref, sem):
    copy = pltpu.make_async_copy(spec_ref, out_ref, sem)
    copy.start()
    copy.wait()


def hold(spectra):
    return pl.pallas_call(
        hold_kernel,
        out_shape=jax.ShapeDtypeStruct(spectra.shape, spectra.dtype),
        in_specs=[pl.BlockSpec(memory_space=pl.ANY)],
        out_specs=pl.BlockSpec(memory_space=pltpu.VMEM),
        scratch_shapes=[pltpu.SemaphoreType.DMA],
        compiler_params=pltpu.CompilerParams(vmem_limit_bytes=8 * 1024 * 1024),
        cost_estimate=pl.CostEstimate(flops=0, bytes_accessed=4 * spectra.size, transcendentals=0),
        name="hold",
    )(spectra)


def pick_kernel(bands_in, bands_out, me_ref, offset_ref, spec_ref, out_ref, place_ref, turn_ref):
    rows, _, bins = spec_ref.shape
    bands, blocks, _ = offset_ref.shape
    band_width = bins // bands
    groups = rows // 8
    chunks = band_width // LANES
    width = blocks * W
    first = me_ref[0] * rows
    columns = pl.ds(pl.multiple_of(first // LANES * LANES, LANES), LANES)
    offsets = jnp.concatenate([offset_ref[bands_in.index(band), :, columns] for band in range(bands)], axis=0).astype(jnp.float32)
    lane = iota(offsets.shape, 1)
    offsets = jnp.take_along_axis(offsets, (lane >> 2) + first & (LANES - 1), axis=1, mode="promise_in_bounds")
    offsets = jnp.concatenate([offsets, jnp.zeros((LANES - bands * blocks, LANES), jnp.float32)], axis=0)
    upright = jnp.transpose(offsets).astype(jnp.int32)
    lane = iota((32, LANES), 1)
    places = upright[0:32]
    for group in range(1, groups):
        turned = pltpu.roll(upright[group * 32 : group * 32 + 32], group * bands * blocks, 1)
        places = jnp.where(lane < group * bands * blocks, places, turned)
    lane = iota((8, LANES), 1)
    lane_group = lane // width
    source = lane_group * (bands * blocks) + lane // W % blocks
    for band in range(bands):
        for pair in range(4):
            place = jnp.take_along_axis(places[pair * 8 : pair * 8 + 8], source + band * blocks, axis=1, mode="promise_in_bounds")
            place_ref[band, pair] = place + ((lane & (W - 1)) + lane_group * band_width)

    def step(band, carry):
        for pair in range(4):
            place = place_ref[band, pair]
            lane_id = place & (LANES - 1)
            chosen = place >> 7
            tile = jnp.zeros((8, LANES), jnp.float32)
            for group in range(groups):
                for chunk in range(chunks):
                    start = pl.multiple_of(band * band_width + chunk * LANES, LANES)
                    values = spec_ref[pl.ds(group * 8 + pair * 2, 2), :, pl.ds(start, LANES)]
                    values = values.astype(jnp.float32).reshape(8, LANES)
                    moved = jnp.take_along_axis(values, lane_id, axis=1, mode="promise_in_bounds")
                    tile = jnp.where(chosen == group * chunks + chunk, moved, tile)
            turn_ref[band, pl.ds(pair * 8, 8), :] = tile
        return carry

    lax.fori_loop(0, bands, step, 0, unroll=2)
    tiles = {}
    for band in range(bands):
        parts = [turn_ref[band, pl.ds(part, 8, stride=4), :] for part in range(4)]
        for group in range(groups):
            tile = jnp.zeros((8, LANES), jnp.float32)
            for part in range(4):
                amount = (part - group) * width % LANES
                turned = pltpu.roll(parts[part], amount, 1) if amount else parts[part]
                tile = jnp.where(lane_group == part, turned, tile)
            tiles[band, group] = tile
    wanted = [tiles[band, group] for band in bands_out for group in range(groups)]
    for n in range(0, len(wanted), 2):
        out_ref[n * 8 : n * 8 + 16, :] = jnp.concatenate(wanted[n : n + 2], axis=0).astype(jnp.bfloat16)


def pick(me, offsets, spectra, bands_in, bands_out):
    rows, bands = spectra.shape[0], offsets.shape[0]
    out_rows = len(bands_out) * rows
    vmem = pl.BlockSpec(memory_space=pltpu.VMEM)
    return pl.pallas_call(
        functools.partial(pick_kernel, bands_in, bands_out),
        out_shape=jax.ShapeDtypeStruct((out_rows, LANES), jnp.bfloat16),
        in_specs=[pl.BlockSpec(memory_space=pltpu.SMEM), vmem, vmem],
        out_specs=vmem,
        scratch_shapes=[
            pltpu.VMEM((bands, 4, 8, LANES), jnp.int32),
            pltpu.VMEM((bands, 32, LANES), jnp.float32),
        ],
        compiler_params=pltpu.CompilerParams(vmem_limit_bytes=8 * 1024 * 1024),
        cost_estimate=pl.CostEstimate(flops=10_000_000, bytes_accessed=2 * spectra.size, transcendentals=0),
        name="pick",
    )(me, offsets, spectra)


def split(values, count):
    parts = []
    for _ in range(count):
        part = values.astype(jnp.bfloat16)
        parts.append(part)
        values = values - part.astype(jnp.float32)
    return parts


def prepare_kernel(first, run, durations_ref, starts_ref, antenna_ref, fractions_ref, mask_ref, weigh_ref, coef_ref, kernel_ref):
    rows = starts_ref.shape[0]
    count = durations_ref.shape[0]
    sfts = antenna_ref.shape[1]
    sft = iota((rows, sfts), 1)
    sft = jnp.where(sft // run == 0, sft + first * run, jnp.where(sft // run == first, sft - first * run, sft))
    start = starts_ref[:, 0:1]
    after = sft >= start
    for j in range(count):
        inside = after & (sft < start + durations_ref[j])
        mask_ref[pl.ds(j * rows, rows), :] = jnp.where(inside, 1.0, 0.0).astype(jnp.bfloat16)
    antenna = jnp.concatenate([antenna_ref[...], jnp.zeros((4, sfts), jnp.float32)], axis=0)
    place = iota(antenna.shape, 1) // run
    after = pltpu.roll(antenna, sfts - first * run, 1)
    before = pltpu.roll(antenna, first * run, 1)
    antenna = jnp.where(place == 0, after, jnp.where(place == first, before, antenna))
    a1, a2, b1, b2 = (antenna[n : n + 1] for n in range(4))
    terms = jnp.concatenate([a1 * a1 + a2 * a2, b1 * b1 + b2 * b2, a1 * b1 + a2 * b2, jnp.zeros((5, sfts), jnp.float32)], axis=0)
    weights = sum(lax.dot_general(mask_ref[...], part, NT, preferred_element_type=jnp.float32) for part in split(terms, 3))
    wa, wb, wc = (weights[:, n : n + 1] for n in range(3))
    shape = (rows * count, LANES)
    late = iota(shape, 1) >= LANES // 2
    coef_ref[0] = jnp.broadcast_to(1.0 / wa, shape)
    coef_ref[1] = jnp.broadcast_to(wa / (wa * wb - wc * wc), shape)
    coef_ref[2] = jnp.where(late, jnp.broadcast_to(wc / wa, shape), 0.0)
    upright = jnp.transpose(jnp.concatenate([antenna, jnp.zeros((LANES - 8, sfts), jnp.float32)], axis=0))
    shape = (sfts, LANES)
    late = iota(shape, 1) >= LANES // 2
    weigh_ref[0] = jnp.where(late, upright[:, 3:4], upright[:, 0:1])
    weigh_ref[1] = jnp.where(late, upright[:, 2:3], upright[:, 1:2])
    fractions = fractions_ref[...]
    templates = fractions.shape[1]
    blocks = kernel_ref.shape[1] // (4 * LANES)
    bin_id = iota((W, templates), 0)
    distance = fractions + (W // 2 - 1) - bin_id.astype(jnp.float32)
    alternate = 1.0 - 2.0 * (bin_id % 2).astype(jnp.float32)
    values = (alternate * jnp.sin(jnp.pi * fractions) / (jnp.pi * distance)).astype(jnp.bfloat16)
    kernel_ref[...] = jnp.zeros_like(kernel_ref)
    for part in range(2):
        for c in range(4):
            for b in range(blocks):
                row = ((part * 4 + c) * blocks + b) * W
                column = (c * blocks + b) * LANES
                kernel_ref[pl.ds(row, W), pl.ds(column, LANES)] = values[:, b * LANES : (b + 1) * LANES]


def prepare(durations, starts, antenna, fractions, first, run):
    count, rows, sfts = durations.shape[0], starts.shape[0], antenna.shape[0]
    columns = 4 * fractions.shape[0]
    features = 4 * W * (fractions.shape[0] // LANES)
    vmem = pl.BlockSpec(memory_space=pltpu.VMEM)
    return pl.pallas_call(
        functools.partial(prepare_kernel, first, run),
        out_shape=(
            jax.ShapeDtypeStruct((count * rows, sfts), jnp.bfloat16),
            jax.ShapeDtypeStruct((2, sfts, LANES), jnp.float32),
            jax.ShapeDtypeStruct((3, count * rows, LANES), jnp.float32),
            jax.ShapeDtypeStruct((2 * features, columns), jnp.bfloat16),
        ),
        in_specs=[pl.BlockSpec(memory_space=pltpu.SMEM), vmem, vmem, vmem],
        out_specs=(vmem,) * 4,
        compiler_params=pltpu.CompilerParams(vmem_limit_bytes=16 * 1024 * 1024),
        cost_estimate=pl.CostEstimate(flops=100_000_000, bytes_accessed=4_000_000, transcendentals=0),
        name="prepare",
    )(durations, jnp.broadcast_to(starts[:, None], (rows, LANES)), antenna.T, fractions[None, :])


def statistic_kernel(windows_ref, mask_ref, weigh_ref, coef_ref, kernel_ref, map_ref, loudest_ref, found_ref):
    values = windows_ref[...].astype(jnp.float32)
    half = LANES // 2
    weighted = (weigh_ref[0] * values + weigh_ref[1] * pltpu.roll(values, half, 1)).astype(jnp.bfloat16)
    sums = jnp.dot(mask_ref[...], weighted, preferred_element_type=jnp.float32)
    sums = sums - coef_ref[2] * pltpu.roll(sums, half, 1)
    parts = jnp.concatenate(split(sums, 2), axis=1)
    found_ref[...] = jnp.dot(parts, kernel_ref[...], preferred_element_type=jnp.float32)
    templates = map_ref.shape[1]
    rows = map_ref.shape[0] // loudest_ref.shape[1]
    copies = loudest_ref.shape[0]
    per_step = LANES // rows
    for step in range(map_ref.shape[0] // LANES):
        here = pl.ds(step * LANES, LANES)
        best = None
        for b in range(templates // LANES):
            ra, ia, rb, ib = (found_ref[here, pl.ds(c * templates + b * LANES, LANES)] for c in range(4))
            result = coef_ref[0, here, :] * (ra * ra + ia * ia) + coef_ref[1, here, :] * (rb * rb + ib * ib)
            map_ref[here, pl.ds(b * LANES, LANES)] = result
            best = result if best is None else jnp.maximum(best, result)
        best = jnp.max(jnp.transpose(best), axis=0, keepdims=True)
        for n in range(per_step):
            turned = best if n == 0 else pltpu.roll(best, LANES - n * rows, 1)
            for copy in range(copies):
                loudest_ref[copy, pl.ds(step * per_step + n, 1), :] = turned


def statistic(windows, mask, weigh, coef, kernel, rows, copies):
    count = mask.shape[0] // rows
    templates = kernel.shape[1] // 4
    vmem = pl.BlockSpec(memory_space=pltpu.VMEM)
    return pl.pallas_call(
        statistic_kernel,
        out_shape=(
            jax.ShapeDtypeStruct((count * rows, templates), jnp.float32),
            jax.ShapeDtypeStruct((copies, count, LANES), jnp.float32),
        ),
        in_specs=[vmem] * 5,
        out_specs=(vmem, vmem),
        scratch_shapes=[pltpu.VMEM((count * rows, 4 * templates), jnp.float32)],
        compiler_params=pltpu.CompilerParams(vmem_limit_bytes=16 * 1024 * 1024),
        cost_estimate=pl.CostEstimate(flops=400_000_000, bytes_accessed=4_000_000, transcendentals=0),
        name="statistic",
    )(windows, mask, weigh, coef, kernel)


def exchange(values, axis, members):
    return lax.all_to_all(values, axis, split_axis=0, concat_axis=0, axis_index_groups=[members], tiled=True)


def body(spectra, offsets, fractions, antenna, starts, durations):
    bands, cores = lax.axis_size("tmpl"), lax.axis_size("tm")
    sft_rows = spectra.shape[0]
    grid_size = starts.shape[0]
    my_rows = grid_size // cores
    me = lax.axis_index("tmpl").astype(jnp.int32)[None]
    by_band = order(bands, bands // 2)
    first = (cores - 1) * bands + bands // 2
    by_run = order(cores * bands, first)
    known = exchange(jnp.broadcast_to(offsets.T[None], (bands,) + offsets.T.shape), "tmpl", by_band)
    my_durations = lax.dynamic_slice_in_dim(durations, lax.axis_index("tm") * my_rows, my_rows, 0)
    prepared = prepare(my_durations, starts, antenna, fractions, first, sft_rows)
    me, prepared = lax.optimization_barrier((me, prepared))
    windows = pick(me, known, hold(spectra), by_band, [run % bands for run in by_run])
    arrived = exchange(windows.reshape(cores * bands, sft_rows, LANES), ("tm", "tmpl"), by_run)
    fstat_map, loudest = statistic(arrived.reshape(-1, LANES), *prepared, grid_size, bands)
    loudest = jnp.max(exchange(loudest, "tmpl", by_band)[:, :, :grid_size], axis=0)
    return (fstat_map.reshape(my_rows, grid_size, -1), loudest)


def solution(mesh):
    in_specs = (
        P(("grp", "tm", "tmpl"), None, None),
        P(("grp", "tm"), "tmpl"),
        P(("grp", "tmpl")),
        P("grp", None),
        P("grp"),
        P("grp"),
    )
    out_specs = (P("tm", None, ("grp", "tmpl")), P(("grp", "tm"), None))
    return jax.shard_map(body, mesh=mesh, in_specs=in_specs, out_specs=out_specs, check_vma=False)
```

```python
import functools

import jax
import jax.numpy as jnp
from jax import lax
from jax.experimental import pallas as pl
from jax.experimental.pallas import tpu as pltpu
from jax.sharding import PartitionSpec as P

W = 16
LANES = 128
NT = (((1,), (1,)), ((), ()))


def iota(shape, axis):
    return lax.broadcasted_iota(jnp.int32, shape, axis)


def order(size, first):
    members = list(range(size))
    members[0], members[first] = first, 0
    return members


def hold_kernel(spec_ref, out_ref, sem):
    copy = pltpu.make_async_copy(spec_ref, out_ref, sem)
    copy.start()
    copy.wait()


def hold(spectra):
    return pl.pallas_call(
        hold_kernel,
        out_shape=jax.ShapeDtypeStruct(spectra.shape, spectra.dtype),
        in_specs=[pl.BlockSpec(memory_space=pl.ANY)],
        out_specs=pl.BlockSpec(memory_space=pltpu.VMEM),
        scratch_shapes=[pltpu.SemaphoreType.DMA],
        compiler_params=pltpu.CompilerParams(vmem_limit_bytes=8 * 1024 * 1024),
        cost_estimate=pl.CostEstimate(flops=0, bytes_accessed=4 * spectra.size, transcendentals=0),
        name="hold",
    )(spectra)


def pick_kernel(bands_in, bands_out, me_ref, offset_ref, spec_ref, out_ref, place_ref, turn_ref):
    rows, _, bins = spec_ref.shape
    bands, blocks, _ = offset_ref.shape
    band_width = bins // bands
    groups = rows // 8
    chunks = band_width // LANES
    width = blocks * W
    first = me_ref[0] * rows
    columns = pl.ds(pl.multiple_of(first // LANES * LANES, LANES), LANES)
    offsets = jnp.concatenate([offset_ref[bands_in.index(band), :, columns] for band in range(bands)], axis=0).astype(jnp.float32)
    lane = iota(offsets.shape, 1)
    offsets = jnp.take_along_axis(offsets, (lane >> 2) + first & (LANES - 1), axis=1, mode="promise_in_bounds")
    offsets = jnp.concatenate([offsets, jnp.zeros((LANES - bands * blocks, LANES), jnp.float32)], axis=0)
    upright = jnp.transpose(offsets).astype(jnp.int32)
    lane = iota((32, LANES), 1)
    places = upright[0:32]
    for group in range(1, groups):
        turned = pltpu.roll(upright[group * 32 : group * 32 + 32], group * bands * blocks, 1)
        places = jnp.where(lane < group * bands * blocks, places, turned)
    lane = iota((8, LANES), 1)
    lane_group = lane // width
    source = lane_group * (bands * blocks) + lane // W % blocks
    for band in range(bands):
        for pair in range(4):
            place = jnp.take_along_axis(places[pair * 8 : pair * 8 + 8], source + band * blocks, axis=1, mode="promise_in_bounds")
            place_ref[band, pair] = place + ((lane & (W - 1)) + lane_group * band_width)

    def step(band, carry):
        for pair in range(4):
            place = place_ref[band, pair]
            lane_id = place & (LANES - 1)
            chosen = place >> 7
            tile = jnp.zeros((8, LANES), jnp.float32)
            for group in range(groups):
                for chunk in range(chunks):
                    start = pl.multiple_of(band * band_width + chunk * LANES, LANES)
                    values = spec_ref[pl.ds(group * 8 + pair * 2, 2), :, pl.ds(start, LANES)]
                    values = values.astype(jnp.float32).reshape(8, LANES)
                    moved = jnp.take_along_axis(values, lane_id, axis=1, mode="promise_in_bounds")
                    tile = jnp.where(chosen == group * chunks + chunk, moved, tile)
            turn_ref[band, pl.ds(pair * 8, 8), :] = tile
        return carry

    lax.fori_loop(0, bands, step, 0, unroll=2)
    tiles = {}
    for band in range(bands):
        parts = [turn_ref[band, pl.ds(part, 8, stride=4), :] for part in range(4)]
        for group in range(groups):
            tile = jnp.zeros((8, LANES), jnp.float32)
            for part in range(4):
                amount = (part - group) * width % LANES
                turned = pltpu.roll(parts[part], amount, 1) if amount else parts[part]
                tile = jnp.where(lane_group == part, turned, tile)
            tiles[band, group] = tile
    wanted = [tiles[band, group] for band in bands_out for group in range(groups)]
    for n in range(0, len(wanted), 2):
        out_ref[n * 8 : n * 8 + 16, :] = jnp.concatenate(wanted[n : n + 2], axis=0).astype(jnp.bfloat16)


def pick(me, offsets, spectra, bands_in, bands_out):
    rows, bands = spectra.shape[0], offsets.shape[0]
    out_rows = len(bands_out) * rows
    vmem = pl.BlockSpec(memory_space=pltpu.VMEM)
    return pl.pallas_call(
        functools.partial(pick_kernel, bands_in, bands_out),
        out_shape=jax.ShapeDtypeStruct((out_rows, LANES), jnp.bfloat16),
        in_specs=[pl.BlockSpec(memory_space=pltpu.SMEM), vmem, vmem],
        out_specs=vmem,
        scratch_shapes=[
            pltpu.VMEM((bands, 4, 8, LANES), jnp.int32),
            pltpu.VMEM((bands, 32, LANES), jnp.float32),
        ],
        compiler_params=pltpu.CompilerParams(vmem_limit_bytes=8 * 1024 * 1024),
        cost_estimate=pl.CostEstimate(flops=10_000_000, bytes_accessed=2 * spectra.size, transcendentals=0),
        name="pick",
    )(me, offsets, spectra)


def split(values, count):
    parts = []
    for _ in range(count):
        part = values.astype(jnp.bfloat16)
        parts.append(part)
        values = values - part.astype(jnp.float32)
    return parts


def prepare_kernel(first, run, durations_ref, starts_ref, antenna_ref, fractions_ref, mask_ref, weigh_ref, coef_ref, kernel_ref):
    rows = starts_ref.shape[0]
    count = durations_ref.shape[0]
    sfts = antenna_ref.shape[1]
    sft = iota((rows, sfts), 1)
    sft = jnp.where(sft // run == 0, sft + first * run, jnp.where(sft // run == first, sft - first * run, sft))
    start = starts_ref[:, 0:1]
    after = sft >= start
    for j in range(count):
        inside = after & (sft < start + durations_ref[j])
        mask_ref[pl.ds(j * rows, rows), :] = jnp.where(inside, 1.0, 0.0).astype(jnp.bfloat16)
    antenna = jnp.concatenate([antenna_ref[...], jnp.zeros((4, sfts), jnp.float32)], axis=0)
    place = iota(antenna.shape, 1) // run
    after = pltpu.roll(antenna, sfts - first * run, 1)
    before = pltpu.roll(antenna, first * run, 1)
    antenna = jnp.where(place == 0, after, jnp.where(place == first, before, antenna))
    a1, a2, b1, b2 = (antenna[n : n + 1] for n in range(4))
    terms = jnp.concatenate([a1 * a1 + a2 * a2, b1 * b1 + b2 * b2, a1 * b1 + a2 * b2, jnp.zeros((5, sfts), jnp.float32)], axis=0)
    weights = sum(lax.dot_general(mask_ref[...], part, NT, preferred_element_type=jnp.float32) for part in split(terms, 3))
    wa, wb, wc = (weights[:, n : n + 1] for n in range(3))
    shape = (rows * count, LANES)
    coef_ref[0] = jnp.where(iota(shape, 1) < LANES // 2, 1.0 / wa, wc / wa)
    coef_ref[1] = jnp.broadcast_to(wa / (wa * wb - wc * wc), shape)
    upright = jnp.transpose(jnp.concatenate([antenna, jnp.zeros((LANES - 8, sfts), jnp.float32)], axis=0))
    quarter = iota((sfts, LANES), 1) // (LANES // 4)
    early = jnp.where(quarter == 0, upright[:, 0:1], upright[:, 1:2])
    weigh_ref[...] = jnp.where(quarter < 2, early, jnp.where(quarter == 2, upright[:, 3:4], upright[:, 2:3]))
    fractions = fractions_ref[...]
    templates = fractions.shape[1]
    blocks = kernel_ref.shape[1] // (4 * LANES)
    bin_id = iota((W, templates), 0)
    distance = fractions + (W // 2 - 1) - bin_id.astype(jnp.float32)
    alternate = 1.0 - 2.0 * (bin_id % 2).astype(jnp.float32)
    values = (alternate * jnp.sin(jnp.pi * fractions) / (jnp.pi * distance)).astype(jnp.bfloat16)
    kernel_ref[...] = jnp.zeros_like(kernel_ref)
    for c in range(4):
        for b in range(blocks):
            row, column = (c * blocks + b) * W, (c * blocks + b) * LANES
            kernel_ref[pl.ds(row, W), pl.ds(column, LANES)] = values[:, b * LANES : (b + 1) * LANES]


def prepare(durations, starts, antenna, fractions, first, run):
    count, rows, sfts = durations.shape[0], starts.shape[0], antenna.shape[0]
    columns = 4 * fractions.shape[0]
    features = 4 * W * (fractions.shape[0] // LANES)
    vmem = pl.BlockSpec(memory_space=pltpu.VMEM)
    return pl.pallas_call(
        functools.partial(prepare_kernel, first, run),
        out_shape=(
            jax.ShapeDtypeStruct((count * rows, sfts), jnp.bfloat16),
            jax.ShapeDtypeStruct((sfts, LANES), jnp.float32),
            jax.ShapeDtypeStruct((2, count * rows, LANES), jnp.float32),
            jax.ShapeDtypeStruct((features, columns), jnp.bfloat16),
        ),
        in_specs=[pl.BlockSpec(memory_space=pltpu.SMEM), vmem, vmem, vmem],
        out_specs=(vmem,) * 4,
        compiler_params=pltpu.CompilerParams(vmem_limit_bytes=16 * 1024 * 1024),
        cost_estimate=pl.CostEstimate(flops=100_000_000, bytes_accessed=7_000_000, transcendentals=0),
        name="prepare",
    )(durations, jnp.broadcast_to(starts[:, None], (rows, LANES)), antenna.T, fractions[None, :])


def statistic_kernel(windows_ref, mask_ref, weigh_ref, coef_ref, kernel_ref, map_ref, loudest_ref, found_ref):
    values = windows_ref[...].astype(jnp.float32)
    half, quarter = LANES // 2, LANES // 4
    weigh = weigh_ref[...]
    even = iota(weigh.shape, 1) // quarter % 2 == 0
    own = jnp.where(even, weigh, pltpu.roll(weigh, quarter, 1))
    other = jnp.where(even, pltpu.roll(weigh, LANES - quarter, 1), weigh)
    weighted = (own * values + other * pltpu.roll(values, half, 1)).astype(jnp.bfloat16)
    sums = jnp.dot(mask_ref[...], weighted, preferred_element_type=jnp.float32)
    early = iota(sums.shape, 1) < half
    sums = sums - jnp.where(early, 0.0, coef_ref[0]) * pltpu.roll(sums, half, 1)
    parts = jnp.concatenate(split(sums, 2), axis=1)
    kernel = jnp.concatenate([kernel_ref[...]] * 2, axis=0)
    found_ref[...] = jnp.dot(parts, kernel, preferred_element_type=jnp.float32)
    templates = map_ref.shape[1]
    rows = map_ref.shape[0] // loudest_ref.shape[1]
    copies = loudest_ref.shape[0]
    per_step = LANES // rows
    for step in range(map_ref.shape[0] // LANES):
        here = pl.ds(step * LANES, LANES)
        scale_a = jnp.where(iota((LANES, LANES), 1) < half, coef_ref[0, here, :], pltpu.roll(coef_ref[0, here, :], half, 1))
        best = None
        for b in range(templates // LANES):
            ra, ia, rb, ib = (found_ref[here, pl.ds(c * templates + b * LANES, LANES)] for c in range(4))
            result = scale_a * (ra * ra + ia * ia) + coef_ref[1, here, :] * (rb * rb + ib * ib)
            map_ref[here, pl.ds(b * LANES, LANES)] = result
            best = result if best is None else jnp.maximum(best, result)
        best = jnp.max(jnp.transpose(best), axis=0, keepdims=True)
        for n in range(per_step):
            turned = best if n == 0 else pltpu.roll(best, LANES - n * rows, 1)
            for copy in range(copies):
                loudest_ref[copy, pl.ds(step * per_step + n, 1), :] = turned


def statistic(windows, mask, weigh, coef, kernel, rows, copies):
    count = mask.shape[0] // rows
    templates = kernel.shape[1] // 4
    vmem = pl.BlockSpec(memory_space=pltpu.VMEM)
    return pl.pallas_call(
        statistic_kernel,
        out_shape=(
            jax.ShapeDtypeStruct((count * rows, templates), jnp.float32),
            jax.ShapeDtypeStruct((copies, count, LANES), jnp.float32),
        ),
        in_specs=[vmem] * 5,
        out_specs=(vmem, vmem),
        scratch_shapes=[pltpu.VMEM((count * rows, 4 * templates), jnp.float32)],
        compiler_params=pltpu.CompilerParams(vmem_limit_bytes=16 * 1024 * 1024),
        cost_estimate=pl.CostEstimate(flops=400_000_000, bytes_accessed=4_000_000, transcendentals=0),
        name="statistic",
    )(windows, mask, weigh, coef, kernel)


def exchange(values, axis, members):
    return lax.all_to_all(values, axis, split_axis=0, concat_axis=0, axis_index_groups=[members], tiled=True)


def body(spectra, offsets, fractions, antenna, starts, durations):
    bands, cores = lax.axis_size("tmpl"), lax.axis_size("tm")
    sft_rows = spectra.shape[0]
    grid_size = starts.shape[0]
    my_rows = grid_size // cores
    me = lax.axis_index("tmpl").astype(jnp.int32)[None]
    by_band = order(bands, bands // 2)
    first = (cores - 1) * bands + bands // 2
    by_run = order(cores * bands, first)
    known = exchange(jnp.broadcast_to(offsets.T[None], (bands,) + offsets.T.shape), "tmpl", by_band)
    my_durations = lax.dynamic_slice_in_dim(durations, lax.axis_index("tm") * my_rows, my_rows, 0)
    prepared = prepare(my_durations, starts, antenna, fractions, first, sft_rows)
    spectra, prepared = lax.optimization_barrier((spectra, prepared))
    windows = pick(me, known, hold(spectra), by_band, [run % bands for run in by_run])
    arrived = exchange(windows.reshape(cores * bands, sft_rows, LANES), ("tm", "tmpl"), by_run)
    fstat_map, loudest = statistic(arrived.reshape(-1, LANES), *prepared, grid_size, bands)
    loudest = jnp.max(exchange(loudest, "tmpl", by_band)[:, :, :grid_size], axis=0)
    return (fstat_map.reshape(my_rows, grid_size, -1), loudest)


def solution(mesh):
    in_specs = (
        P(("grp", "tm", "tmpl"), None, None),
        P(("grp", "tm"), "tmpl"),
        P(("grp", "tmpl")),
        P("grp", None),
        P("grp"),
        P("grp"),
    )
    out_specs = (P("tm", None, ("grp", "tmpl")), P(("grp", "tm"), None))
    return jax.shard_map(body, mesh=mesh, in_specs=in_specs, out_specs=out_specs, check_vma=False)
```

```python
import functools

import jax
import jax.numpy as jnp
from jax import lax
from jax.experimental import pallas as pl
from jax.experimental.pallas import tpu as pltpu
from jax.sharding import PartitionSpec as P

W = 16
LANES = 128
NT = (((1,), (1,)), ((), ()))


def iota(shape, axis):
    return lax.broadcasted_iota(jnp.int32, shape, axis)


def order(size, first):
    members = list(range(size))
    members[0], members[first] = first, 0
    return members


def repeat_kernel(in_ref, out_ref, sems):
    copies = [pltpu.make_async_copy(in_ref, out_ref.at[n], sems.at[n]) for n in range(out_ref.shape[0])]
    for copy in copies:
        copy.start()
    for copy in copies:
        copy.wait()


def repeat(values, count):
    return pl.pallas_call(
        repeat_kernel,
        out_shape=jax.ShapeDtypeStruct((count,) + values.shape, values.dtype),
        in_specs=[pl.BlockSpec(memory_space=pl.ANY)],
        out_specs=pl.BlockSpec(memory_space=pl.ANY),
        scratch_shapes=[pltpu.SemaphoreType.DMA((count,))],
        name="repeat",
    )(values)


def hold_kernel(spec_ref, out_ref, sem):
    copy = pltpu.make_async_copy(spec_ref, out_ref, sem)
    copy.start()
    copy.wait()


def hold(spectra):
    return pl.pallas_call(
        hold_kernel,
        out_shape=jax.ShapeDtypeStruct(spectra.shape, spectra.dtype),
        in_specs=[pl.BlockSpec(memory_space=pl.ANY)],
        out_specs=pl.BlockSpec(memory_space=pltpu.VMEM),
        scratch_shapes=[pltpu.SemaphoreType.DMA],
        compiler_params=pltpu.CompilerParams(vmem_limit_bytes=8 * 1024 * 1024),
        cost_estimate=pl.CostEstimate(flops=0, bytes_accessed=4 * spectra.size, transcendentals=0),
        name="hold",
    )(spectra)


def pick_kernel(bands_in, bands_out, me_ref, offset_ref, spec_ref, out_ref, place_ref, turn_ref, tile_ref, sems):
    rows, _, bins = spec_ref.shape
    bands, blocks, _ = offset_ref.shape
    band_width = bins // bands
    groups = rows // 8
    chunks = band_width // LANES
    width = blocks * W
    first = me_ref[0] * rows
    columns = pl.ds(pl.multiple_of(first // LANES * LANES, LANES), LANES)
    offsets = jnp.concatenate([offset_ref[bands_in.index(band), :, columns] for band in range(bands)], axis=0).astype(jnp.float32)
    lane = iota(offsets.shape, 1)
    offsets = jnp.take_along_axis(offsets, (lane >> 2) + first & (LANES - 1), axis=1, mode="promise_in_bounds")
    offsets = jnp.concatenate([offsets, jnp.zeros((LANES - bands * blocks, LANES), jnp.float32)], axis=0)
    upright = jnp.transpose(offsets).astype(jnp.int32)
    lane = iota((32, LANES), 1)
    places = upright[0:32]
    for group in range(1, groups):
        turned = pltpu.roll(upright[group * 32 : group * 32 + 32], group * bands * blocks, 1)
        places = jnp.where(lane < group * bands * blocks, places, turned)
    lane = iota((8, LANES), 1)
    lane_group = lane // width
    source = lane_group * (bands * blocks) + lane // W % blocks
    for band in range(bands):
        for pair in range(4):
            place = jnp.take_along_axis(places[pair * 8 : pair * 8 + 8], source + band * blocks, axis=1, mode="promise_in_bounds")
            place_ref[band, pair] = place + ((lane & (W - 1)) + lane_group * band_width)

    def gather(band):
        for pair in range(4):
            place = place_ref[band, pair]
            lane_id = place & (LANES - 1)
            chosen = place >> 7
            tile = jnp.zeros((8, LANES), jnp.float32)
            for group in range(groups):
                for chunk in range(chunks):
                    columns = pl.ds(band * band_width + chunk * LANES, LANES)
                    values = spec_ref[pl.ds(group * 8 + pair * 2, 2), :, columns]
                    values = values.astype(jnp.float32).reshape(8, LANES)
                    moved = jnp.take_along_axis(values, lane_id, axis=1, mode="promise_in_bounds")
                    tile = jnp.where(chosen == group * chunks + chunk, moved, tile)
            turn_ref[band, pl.ds(pair * 8, 8), :] = tile

    def turn(band):
        parts = [turn_ref[band, pl.ds(part, 8, stride=4), :] for part in range(4)]
        tiles = []
        for group in range(groups):
            tile = jnp.zeros((8, LANES), jnp.float32)
            for part in range(4):
                amount = (part - group) * width % LANES
                turned = pltpu.roll(parts[part], amount, 1) if amount else parts[part]
                tile = jnp.where(lane_group == part, turned, tile)
            tiles.append(tile)
        return tiles

    tiles, copies = {}, []
    for band in range(bands):
        gather(band)
        tiles[band] = turn(band)
        if rows % 16 == 0:
            here = pl.ds(band * rows, rows)
            tile_ref[here, :] = jnp.concatenate(tiles[band], axis=0).astype(jnp.bfloat16)
            for slot in range(len(bands_out)):
                if bands_out[slot] == band:
                    there = out_ref.at[pl.ds(slot * rows, rows), :]
                    copies.append(pltpu.make_async_copy(tile_ref.at[here, :], there, sems.at[slot]))
                    copies[-1].start()
    if rows % 16:
        wanted = [tile for band in bands_out for tile in tiles[band]]
        for n in range(0, len(wanted), 2):
            tile_ref[n * 8 : n * 8 + 16, :] = jnp.concatenate(wanted[n : n + 2], axis=0).astype(jnp.bfloat16)
        copies.append(pltpu.make_async_copy(tile_ref, out_ref, sems.at[0]))
        copies[-1].start()
    for copy in copies:
        copy.wait()


def pick(me, offsets, spectra, bands_in, bands_out):
    rows, bands = spectra.shape[0], offsets.shape[0]
    out_rows = len(bands_out) * rows
    vmem = pl.BlockSpec(memory_space=pltpu.VMEM)
    return pl.pallas_call(
        functools.partial(pick_kernel, bands_in, bands_out),
        out_shape=jax.ShapeDtypeStruct((out_rows, LANES), jnp.bfloat16),
        in_specs=[pl.BlockSpec(memory_space=pltpu.SMEM), vmem, vmem],
        out_specs=pl.BlockSpec(memory_space=pl.ANY),
        scratch_shapes=[
            pltpu.VMEM((bands, 4, 8, LANES), jnp.int32),
            pltpu.VMEM((bands, 32, LANES), jnp.float32),
            pltpu.VMEM((out_rows, LANES), jnp.bfloat16),
            pltpu.SemaphoreType.DMA((len(bands_out),)),
        ],
        compiler_params=pltpu.CompilerParams(vmem_limit_bytes=8 * 1024 * 1024),
        cost_estimate=pl.CostEstimate(flops=10_000_000, bytes_accessed=2 * spectra.size, transcendentals=0),
        name="pick",
    )(me, offsets, spectra)


def split(values, count):
    parts = []
    for _ in range(count):
        part = values.astype(jnp.bfloat16)
        parts.append(part)
        values = values - part.astype(jnp.float32)
    return parts


def prepare_kernel(first, run, durations_ref, starts_ref, antenna_ref, fractions_ref, mask_ref, weigh_ref, coef_ref, kernel_ref):
    rows = starts_ref.shape[0]
    count = durations_ref.shape[0]
    sfts = antenna_ref.shape[1]
    sft = iota((rows, sfts), 1)
    sft = jnp.where(sft // run == 0, sft + first * run, jnp.where(sft // run == first, sft - first * run, sft))
    start = starts_ref[:, 0:1]
    after = sft >= start
    for j in range(count):
        inside = after & (sft < start + durations_ref[j])
        mask_ref[pl.ds(j * rows, rows), :] = jnp.where(inside, 1.0, 0.0).astype(jnp.bfloat16)
    antenna = jnp.concatenate([antenna_ref[...], jnp.zeros((4, sfts), jnp.float32)], axis=0)
    place = iota(antenna.shape, 1) // run
    after = pltpu.roll(antenna, sfts - first * run, 1)
    before = pltpu.roll(antenna, first * run, 1)
    antenna = jnp.where(place == 0, after, jnp.where(place == first, before, antenna))
    a1, a2, b1, b2 = (antenna[n : n + 1] for n in range(4))
    terms = jnp.concatenate([a1 * a1 + a2 * a2, b1 * b1 + b2 * b2, a1 * b1 + a2 * b2, jnp.zeros((5, sfts), jnp.float32)], axis=0)
    weights = sum(lax.dot_general(mask_ref[...], part, NT, preferred_element_type=jnp.float32) for part in split(terms, 3))
    wa, wb, wc = (weights[:, n : n + 1] for n in range(3))
    shape = (rows * count, LANES)
    late = iota(shape, 1) >= LANES // 2
    coef_ref[0] = jnp.broadcast_to(1.0 / wa, shape)
    coef_ref[1] = jnp.broadcast_to(wa / (wa * wb - wc * wc), shape)
    coef_ref[2] = jnp.where(late, jnp.broadcast_to(wc / wa, shape), 0.0)
    upright = jnp.transpose(jnp.concatenate([antenna, jnp.zeros((LANES - 8, sfts), jnp.float32)], axis=0))
    shape = (sfts, LANES)
    late = iota(shape, 1) >= LANES // 2
    weigh_ref[0] = jnp.where(late, upright[:, 3:4], upright[:, 0:1])
    weigh_ref[1] = jnp.where(late, upright[:, 2:3], upright[:, 1:2])
    fractions = fractions_ref[...]
    templates = fractions.shape[1]
    blocks = kernel_ref.shape[1] // (4 * LANES)
    bin_id = iota((W, templates), 0)
    distance = fractions + (W // 2 - 1) - bin_id.astype(jnp.float32)
    alternate = 1.0 - 2.0 * (bin_id % 2).astype(jnp.float32)
    values = (alternate * jnp.sin(jnp.pi * fractions) / (jnp.pi * distance)).astype(jnp.bfloat16)
    kernel_ref[...] = jnp.zeros_like(kernel_ref)
    for part in range(2):
        for c in range(4):
            for b in range(blocks):
                row = ((part * 4 + c) * blocks + b) * W
                column = (c * blocks + b) * LANES
                kernel_ref[pl.ds(row, W), pl.ds(column, LANES)] = values[:, b * LANES : (b + 1) * LANES]


def prepare(durations, starts, antenna, fractions, first, run):
    count, rows, sfts = durations.shape[0], starts.shape[0], antenna.shape[0]
    columns = 4 * fractions.shape[0]
    features = 4 * W * (fractions.shape[0] // LANES)
    vmem = pl.BlockSpec(memory_space=pltpu.VMEM)
    return pl.pallas_call(
        functools.partial(prepare_kernel, first, run),
        out_shape=(
            jax.ShapeDtypeStruct((count * rows, sfts), jnp.bfloat16),
            jax.ShapeDtypeStruct((2, sfts, LANES), jnp.float32),
            jax.ShapeDtypeStruct((3, count * rows, LANES), jnp.float32),
            jax.ShapeDtypeStruct((2 * features, columns), jnp.bfloat16),
        ),
        in_specs=[pl.BlockSpec(memory_space=pltpu.SMEM), vmem, vmem, vmem],
        out_specs=(vmem,) * 4,
        compiler_params=pltpu.CompilerParams(vmem_limit_bytes=16 * 1024 * 1024),
        cost_estimate=pl.CostEstimate(flops=100_000_000, bytes_accessed=4_000_000, transcendentals=0),
        name="prepare",
    )(durations, jnp.broadcast_to(starts[:, None], (rows, LANES)), antenna.T, fractions[None, :])


def statistic_kernel(windows_ref, mask_ref, weigh_ref, coef_ref, kernel_ref, map_ref, loudest_ref, found_ref):
    values = windows_ref[...].astype(jnp.float32)
    half = LANES // 2
    weighted = (weigh_ref[0] * values + weigh_ref[1] * pltpu.roll(values, half, 1)).astype(jnp.bfloat16)
    sums = jnp.dot(mask_ref[...], weighted, preferred_element_type=jnp.float32)
    sums = sums - coef_ref[2] * pltpu.roll(sums, half, 1)
    parts = jnp.concatenate(split(sums, 2), axis=1)
    found_ref[...] = jnp.dot(parts, kernel_ref[...], preferred_element_type=jnp.float32)
    templates = map_ref.shape[1]
    rows = map_ref.shape[0] // loudest_ref.shape[1]
    copies = loudest_ref.shape[0]
    per_step = LANES // rows
    for step in range(map_ref.shape[0] // LANES):
        here = pl.ds(step * LANES, LANES)
        best = None
        for b in range(templates // LANES):
            ra, ia, rb, ib = (found_ref[here, pl.ds(c * templates + b * LANES, LANES)] for c in range(4))
            result = coef_ref[0, here, :] * (ra * ra + ia * ia) + coef_ref[1, here, :] * (rb * rb + ib * ib)
            map_ref[here, pl.ds(b * LANES, LANES)] = result
            best = result if best is None else jnp.maximum(best, result)
        best = jnp.max(jnp.transpose(best), axis=0, keepdims=True)
        for n in range(per_step):
            turned = best if n == 0 else pltpu.roll(best, LANES - n * rows, 1)
            for copy in range(copies):
                loudest_ref[copy, pl.ds(step * per_step + n, 1), :] = turned


def statistic(windows, mask, weigh, coef, kernel, rows, copies):
    count = mask.shape[0] // rows
    templates = kernel.shape[1] // 4
    vmem = pl.BlockSpec(memory_space=pltpu.VMEM)
    return pl.pallas_call(
        statistic_kernel,
        out_shape=(
            jax.ShapeDtypeStruct((count * rows, templates), jnp.float32),
            jax.ShapeDtypeStruct((copies, count, LANES), jnp.float32),
        ),
        in_specs=[vmem] * 5,
        out_specs=(vmem, vmem),
        scratch_shapes=[pltpu.VMEM((count * rows, 4 * templates), jnp.float32)],
        compiler_params=pltpu.CompilerParams(vmem_limit_bytes=16 * 1024 * 1024),
        cost_estimate=pl.CostEstimate(flops=400_000_000, bytes_accessed=4_000_000, transcendentals=0),
        name="statistic",
    )(windows, mask, weigh, coef, kernel)


def exchange(values, axis, members):
    return lax.all_to_all(values, axis, split_axis=0, concat_axis=0, axis_index_groups=[members], tiled=True)


def body(spectra, offsets, fractions, antenna, starts, durations):
    bands, cores = lax.axis_size("tmpl"), lax.axis_size("tm")
    sft_rows = spectra.shape[0]
    grid_size = starts.shape[0]
    my_rows = grid_size // cores
    me = lax.axis_index("tmpl").astype(jnp.int32)[None]
    by_band = order(bands, bands // 2)
    first = (cores - 1) * bands + bands // 2
    by_run = order(cores * bands, first)
    known = exchange(repeat(offsets.T, bands), "tmpl", by_band)
    my_durations = lax.dynamic_slice_in_dim(durations, lax.axis_index("tm") * my_rows, my_rows, 0)
    windows = pick(me, known, hold(spectra), by_band, [run % bands for run in by_run])
    windows, my_durations = lax.optimization_barrier((windows, my_durations))
    prepared = prepare(my_durations, starts, antenna, fractions, first, sft_rows)
    arrived = exchange(windows.reshape(cores * bands, sft_rows, LANES), ("tm", "tmpl"), by_run)
    fstat_map, loudest = statistic(arrived.reshape(-1, LANES), *prepared, grid_size, bands)
    loudest = jnp.max(exchange(loudest, "tmpl", by_band)[:, :, :grid_size], axis=0)
    return (fstat_map.reshape(my_rows, grid_size, -1), loudest)


def solution(mesh):
    in_specs = (
        P(("grp", "tm", "tmpl"), None, None),
        P(("grp", "tm"), "tmpl"),
        P(("grp", "tmpl")),
        P("grp", None),
        P("grp"),
        P("grp"),
    )
    out_specs = (P("tm", None, ("grp", "tmpl")), P(("grp", "tm"), None))
    return jax.shard_map(body, mesh=mesh, in_specs=in_specs, out_specs=out_specs, check_vma=False)
```

```python
import functools

import jax
import jax.numpy as jnp
from jax import lax
from jax.experimental import pallas as pl
from jax.experimental.pallas import tpu as pltpu
from jax.sharding import PartitionSpec as P

W = 16
LANES = 128
NT = (((1,), (1,)), ((), ()))


def iota(shape, axis):
    return lax.broadcasted_iota(jnp.int32, shape, axis)


def order(size, first):
    members = list(range(size))
    members[0], members[first] = first, 0
    return members


def pick_kernel(bands_in, bands_out, me_ref, offset_ref, spec_ref, out_ref, place_ref, turn_ref, tile_ref, sems):
    rows, _, bins = spec_ref.shape
    bands, blocks, _ = offset_ref.shape
    band_width = bins // bands
    groups = rows // 8
    chunks = band_width // LANES
    width = blocks * W
    first = me_ref[0] * rows
    columns = pl.ds(pl.multiple_of(first // LANES * LANES, LANES), LANES)
    offsets = jnp.concatenate([offset_ref[bands_in.index(band), :, columns] for band in range(bands)], axis=0).astype(jnp.float32)
    lane = iota(offsets.shape, 1)
    offsets = jnp.take_along_axis(offsets, (lane >> 2) + first & (LANES - 1), axis=1, mode="promise_in_bounds")
    offsets = jnp.concatenate([offsets, jnp.zeros((LANES - bands * blocks, LANES), jnp.float32)], axis=0)
    upright = jnp.transpose(offsets).astype(jnp.int32)
    lane = iota((32, LANES), 1)
    places = upright[0:32]
    for group in range(1, groups):
        turned = pltpu.roll(upright[group * 32 : group * 32 + 32], group * bands * blocks, 1)
        places = jnp.where(lane < group * bands * blocks, places, turned)
    lane = iota((8, LANES), 1)
    lane_group = lane // width
    source = lane_group * (bands * blocks) + lane // W % blocks
    for band in range(bands):
        for pair in range(4):
            place = jnp.take_along_axis(places[pair * 8 : pair * 8 + 8], source + band * blocks, axis=1, mode="promise_in_bounds")
            place_ref[band, pair] = place + ((lane & (W - 1)) + lane_group * band_width)

    def gather(band):
        for pair in range(4):
            place = place_ref[band, pair]
            lane_id = place & (LANES - 1)
            chosen = place >> 7
            tile = jnp.zeros((8, LANES), jnp.float32)
            for group in range(groups):
                for chunk in range(chunks):
                    columns = pl.ds(band * band_width + chunk * LANES, LANES)
                    values = spec_ref[pl.ds(group * 8 + pair * 2, 2), :, columns]
                    values = values.astype(jnp.float32).reshape(8, LANES)
                    moved = jnp.take_along_axis(values, lane_id, axis=1, mode="promise_in_bounds")
                    tile = jnp.where(chosen == group * chunks + chunk, moved, tile)
            turn_ref[band, pl.ds(pair * 8, 8), :] = tile

    def turn(band):
        parts = [turn_ref[band, pl.ds(part, 8, stride=4), :] for part in range(4)]
        tiles = []
        for group in range(groups):
            tile = jnp.zeros((8, LANES), jnp.float32)
            for part in range(4):
                amount = (part - group) * width % LANES
                turned = pltpu.roll(parts[part], amount, 1) if amount else parts[part]
                tile = jnp.where(lane_group == part, turned, tile)
            tiles.append(tile)
        return tiles

    tiles, copies = {}, []
    for band in range(bands):
        gather(band)
        tiles[band] = turn(band)
        if rows % 16 == 0:
            here = pl.ds(band * rows, rows)
            tile_ref[here, :] = jnp.concatenate(tiles[band], axis=0).astype(jnp.bfloat16)
            for slot in range(len(bands_out)):
                if bands_out[slot] == band:
                    there = out_ref.at[pl.ds(slot * rows, rows), :]
                    copies.append(pltpu.make_async_copy(tile_ref.at[here, :], there, sems.at[slot]))
                    copies[-1].start()
    if rows % 16:
        wanted = [tile for band in bands_out for tile in tiles[band]]
        for n in range(0, len(wanted), 2):
            tile_ref[n * 8 : n * 8 + 16, :] = jnp.concatenate(wanted[n : n + 2], axis=0).astype(jnp.bfloat16)
        copies.append(pltpu.make_async_copy(tile_ref, out_ref, sems.at[0]))
        copies[-1].start()
    for copy in copies:
        copy.wait()


def pick(me, offsets, spectra, bands_in, bands_out):
    rows, bands = spectra.shape[0], offsets.shape[0]
    out_rows = len(bands_out) * rows
    vmem = pl.BlockSpec(memory_space=pltpu.VMEM)
    return pl.pallas_call(
        functools.partial(pick_kernel, bands_in, bands_out),
        out_shape=jax.ShapeDtypeStruct((out_rows, LANES), jnp.bfloat16),
        in_specs=[pl.BlockSpec(memory_space=pltpu.SMEM), vmem, vmem],
        out_specs=pl.BlockSpec(memory_space=pl.ANY),
        scratch_shapes=[
            pltpu.VMEM((bands, 4, 8, LANES), jnp.int32),
            pltpu.VMEM((bands, 32, LANES), jnp.float32),
            pltpu.VMEM((out_rows, LANES), jnp.bfloat16),
            pltpu.SemaphoreType.DMA((len(bands_out),)),
        ],
        compiler_params=pltpu.CompilerParams(vmem_limit_bytes=8 * 1024 * 1024),
        cost_estimate=pl.CostEstimate(flops=10_000_000, bytes_accessed=2 * spectra.size, transcendentals=0),
        name="pick",
    )(me, offsets, spectra)


def split(values, count):
    parts = []
    for _ in range(count):
        part = values.astype(jnp.bfloat16)
        parts.append(part)
        values = values - part.astype(jnp.float32)
    return parts


def prepare_kernel(first, run, durations_ref, starts_ref, antenna_ref, fractions_ref, mask_ref, weigh_ref, coef_ref, kernel_ref):
    rows = starts_ref.shape[0]
    count = durations_ref.shape[0]
    sfts = antenna_ref.shape[1]
    sft = iota((rows, sfts), 1)
    sft = jnp.where(sft // run == 0, sft + first * run, jnp.where(sft // run == first, sft - first * run, sft))
    start = starts_ref[:, 0:1]
    after = sft >= start
    for j in range(count):
        inside = after & (sft < start + durations_ref[j])
        mask_ref[pl.ds(j * rows, rows), :] = jnp.where(inside, 1.0, 0.0).astype(jnp.bfloat16)
    antenna = jnp.concatenate([antenna_ref[...], jnp.zeros((4, sfts), jnp.float32)], axis=0)
    place = iota(antenna.shape, 1) // run
    after = pltpu.roll(antenna, sfts - first * run, 1)
    before = pltpu.roll(antenna, first * run, 1)
    antenna = jnp.where(place == 0, after, jnp.where(place == first, before, antenna))
    a1, a2, b1, b2 = (antenna[n : n + 1] for n in range(4))
    terms = jnp.concatenate([a1 * a1 + a2 * a2, b1 * b1 + b2 * b2, a1 * b1 + a2 * b2, jnp.zeros((5, sfts), jnp.float32)], axis=0)
    weights = sum(lax.dot_general(mask_ref[...], part, NT, preferred_element_type=jnp.float32) for part in split(terms, 3))
    wa, wb, wc = (weights[:, n : n + 1] for n in range(3))
    shape = (rows * count, LANES)
    late = iota(shape, 1) >= LANES // 2
    coef_ref[0] = jnp.broadcast_to(1.0 / wa, shape)
    coef_ref[1] = jnp.broadcast_to(wa / (wa * wb - wc * wc), shape)
    coef_ref[2] = jnp.where(late, jnp.broadcast_to(wc / wa, shape), 0.0)
    upright = jnp.transpose(jnp.concatenate([antenna, jnp.zeros((LANES - 8, sfts), jnp.float32)], axis=0))
    shape = (sfts, LANES)
    late = iota(shape, 1) >= LANES // 2
    weigh_ref[0] = jnp.where(late, upright[:, 3:4], upright[:, 0:1])
    weigh_ref[1] = jnp.where(late, upright[:, 2:3], upright[:, 1:2])
    fractions = fractions_ref[...]
    templates = fractions.shape[1]
    blocks = kernel_ref.shape[1] // (4 * LANES)
    bin_id = iota((W, templates), 0)
    distance = fractions + (W // 2 - 1) - bin_id.astype(jnp.float32)
    alternate = 1.0 - 2.0 * (bin_id % 2).astype(jnp.float32)
    values = (alternate * jnp.sin(jnp.pi * fractions) / (jnp.pi * distance)).astype(jnp.bfloat16)
    kernel_ref[...] = jnp.zeros_like(kernel_ref)
    for part in range(2):
        for c in range(4):
            for b in range(blocks):
                row = ((part * 4 + c) * blocks + b) * W
                column = (c * blocks + b) * LANES
                kernel_ref[pl.ds(row, W), pl.ds(column, LANES)] = values[:, b * LANES : (b + 1) * LANES]


def prepare(durations, starts, antenna, fractions, first, run):
    count, rows, sfts = durations.shape[0], starts.shape[0], antenna.shape[0]
    columns = 4 * fractions.shape[0]
    features = 4 * W * (fractions.shape[0] // LANES)
    vmem = pl.BlockSpec(memory_space=pltpu.VMEM)
    return pl.pallas_call(
        functools.partial(prepare_kernel, first, run),
        out_shape=(
            jax.ShapeDtypeStruct((count * rows, sfts), jnp.bfloat16),
            jax.ShapeDtypeStruct((2, sfts, LANES), jnp.float32),
            jax.ShapeDtypeStruct((3, count * rows, LANES), jnp.float32),
            jax.ShapeDtypeStruct((2 * features, columns), jnp.bfloat16),
        ),
        in_specs=[pl.BlockSpec(memory_space=pltpu.SMEM), vmem, vmem, vmem],
        out_specs=(vmem,) * 4,
        compiler_params=pltpu.CompilerParams(vmem_limit_bytes=16 * 1024 * 1024),
        cost_estimate=pl.CostEstimate(flops=100_000_000, bytes_accessed=4_000_000, transcendentals=0),
        name="prepare",
    )(durations, jnp.broadcast_to(starts[:, None], (rows, LANES)), antenna.T, fractions[None, :])


def statistic_kernel(windows_ref, mask_ref, weigh_ref, coef_ref, kernel_ref, map_ref, loudest_ref, found_ref):
    values = windows_ref[...].astype(jnp.float32)
    half = LANES // 2
    weighted = (weigh_ref[0] * values + weigh_ref[1] * pltpu.roll(values, half, 1)).astype(jnp.bfloat16)
    sums = jnp.dot(mask_ref[...], weighted, preferred_element_type=jnp.float32)
    sums = sums - coef_ref[2] * pltpu.roll(sums, half, 1)
    parts = jnp.concatenate(split(sums, 2), axis=1)
    found_ref[...] = jnp.dot(parts, kernel_ref[...], preferred_element_type=jnp.float32)
    templates = map_ref.shape[1]
    rows = map_ref.shape[0] // loudest_ref.shape[1]
    copies = loudest_ref.shape[0]
    per_step = LANES // rows
    for step in range(map_ref.shape[0] // LANES):
        here = pl.ds(step * LANES, LANES)
        best = None
        for b in range(templates // LANES):
            ra, ia, rb, ib = (found_ref[here, pl.ds(c * templates + b * LANES, LANES)] for c in range(4))
            result = coef_ref[0, here, :] * (ra * ra + ia * ia) + coef_ref[1, here, :] * (rb * rb + ib * ib)
            map_ref[here, pl.ds(b * LANES, LANES)] = result
            best = result if best is None else jnp.maximum(best, result)
        best = jnp.max(jnp.transpose(best), axis=0, keepdims=True)
        for n in range(per_step):
            turned = best if n == 0 else pltpu.roll(best, LANES - n * rows, 1)
            for copy in range(copies):
                loudest_ref[copy, pl.ds(step * per_step + n, 1), :] = turned


def statistic(windows, mask, weigh, coef, kernel, rows, copies):
    count = mask.shape[0] // rows
    templates = kernel.shape[1] // 4
    vmem = pl.BlockSpec(memory_space=pltpu.VMEM)
    return pl.pallas_call(
        statistic_kernel,
        out_shape=(
            jax.ShapeDtypeStruct((count * rows, templates), jnp.float32),
            jax.ShapeDtypeStruct((copies, count, LANES), jnp.float32),
        ),
        in_specs=[vmem] * 5,
        out_specs=(vmem, vmem),
        scratch_shapes=[pltpu.VMEM((count * rows, 4 * templates), jnp.float32)],
        compiler_params=pltpu.CompilerParams(vmem_limit_bytes=16 * 1024 * 1024),
        cost_estimate=pl.CostEstimate(flops=400_000_000, bytes_accessed=4_000_000, transcendentals=0),
        name="statistic",
    )(windows, mask, weigh, coef, kernel)


def exchange(values, axis, members):
    return lax.all_to_all(values, axis, split_axis=0, concat_axis=0, axis_index_groups=[members], tiled=True)


def body(spectra, offsets, fractions, antenna, starts, durations):
    bands, cores = lax.axis_size("tmpl"), lax.axis_size("tm")
    sft_rows = spectra.shape[0]
    grid_size = starts.shape[0]
    my_rows = grid_size // cores
    me = lax.axis_index("tmpl").astype(jnp.int32)[None]
    by_band = order(bands, bands // 2)
    first = (cores - 1) * bands + bands // 2
    by_run = order(cores * bands, first)
    known = exchange(jnp.broadcast_to(offsets.T[None], (bands,) + offsets.T.shape), "tmpl", by_band)
    windows = pick(me, known, spectra, by_band, [run % bands for run in by_run])
    windows, *late = lax.optimization_barrier((windows, durations, starts, antenna, fractions))
    durations, starts, antenna, fractions = late
    my_durations = lax.dynamic_slice_in_dim(durations, lax.axis_index("tm") * my_rows, my_rows, 0)
    prepared = prepare(my_durations, starts, antenna, fractions, first, sft_rows)
    arrived = exchange(windows.reshape(cores * bands, sft_rows, LANES), ("tm", "tmpl"), by_run)
    fstat_map, loudest = statistic(arrived.reshape(-1, LANES), *prepared, grid_size, bands)
    loudest = jnp.max(exchange(loudest, "tmpl", by_band)[:, :, :grid_size], axis=0)
    return (fstat_map.reshape(my_rows, grid_size, -1), loudest)


def solution(mesh):
    in_specs = (
        P(("grp", "tm", "tmpl"), None, None),
        P(("grp", "tm"), "tmpl"),
        P(("grp", "tmpl")),
        P("grp", None),
        P("grp"),
        P("grp"),
    )
    out_specs = (P("tm", None, ("grp", "tmpl")), P(("grp", "tm"), None))
    return jax.shard_map(body, mesh=mesh, in_specs=in_specs, out_specs=out_specs, check_vma=False)
```

```python
import functools

import jax
import jax.numpy as jnp
from jax import lax
from jax.experimental import pallas as pl
from jax.experimental.pallas import tpu as pltpu
from jax.sharding import PartitionSpec as P

W = 16
LANES = 128
NT = (((1,), (1,)), ((), ()))


def iota(shape, axis):
    return lax.broadcasted_iota(jnp.int32, shape, axis)


def order(size, first):
    members = list(range(size))
    members[0], members[first] = first, 0
    return members


def pick_kernel(bands_in, bands_out, offset_ref, spec_ref, out_ref, place_ref, turn_ref, tile_ref, sems):
    rows, _, bins = spec_ref.shape
    bands, blocks, _ = offset_ref.shape
    band_width = bins // bands
    groups = rows // 8
    chunks = band_width // LANES
    width = blocks * W
    first = lax.axis_index("tmpl").astype(jnp.int32) * rows
    columns = pl.ds(pl.multiple_of(first // LANES * LANES, LANES), LANES)
    offsets = jnp.concatenate([offset_ref[bands_in.index(band), :, columns] for band in range(bands)], axis=0).astype(jnp.float32)
    lane = iota(offsets.shape, 1)
    offsets = jnp.take_along_axis(offsets, (lane >> 2) + first & (LANES - 1), axis=1, mode="promise_in_bounds")
    offsets = jnp.concatenate([offsets, jnp.zeros((LANES - bands * blocks, LANES), jnp.float32)], axis=0)
    upright = jnp.transpose(offsets).astype(jnp.int32)
    lane = iota((32, LANES), 1)
    places = upright[0:32]
    for group in range(1, groups):
        turned = pltpu.roll(upright[group * 32 : group * 32 + 32], group * bands * blocks, 1)
        places = jnp.where(lane < group * bands * blocks, places, turned)
    lane = iota((8, LANES), 1)
    lane_group = lane // width
    source = lane_group * (bands * blocks) + lane // W % blocks
    for band in range(bands):
        for pair in range(4):
            place = jnp.take_along_axis(places[pair * 8 : pair * 8 + 8], source + band * blocks, axis=1, mode="promise_in_bounds")
            place_ref[band, pair] = place + ((lane & (W - 1)) + lane_group * band_width)

    def gather(band):
        for pair in range(4):
            place = place_ref[band, pair]
            lane_id = place & (LANES - 1)
            chosen = place >> 7
            tile = jnp.zeros((8, LANES), jnp.float32)
            for group in range(groups):
                for chunk in range(chunks):
                    columns = pl.ds(band * band_width + chunk * LANES, LANES)
                    values = spec_ref[pl.ds(group * 8 + pair * 2, 2), :, columns]
                    values = values.astype(jnp.float32).reshape(8, LANES)
                    moved = jnp.take_along_axis(values, lane_id, axis=1, mode="promise_in_bounds")
                    tile = jnp.where(chosen == group * chunks + chunk, moved, tile)
            turn_ref[band, pl.ds(pair * 8, 8), :] = tile

    def turn(band):
        parts = [turn_ref[band, pl.ds(part, 8, stride=4), :] for part in range(4)]
        tiles = []
        for group in range(groups):
            tile = jnp.zeros((8, LANES), jnp.float32)
            for part in range(4):
                amount = (part - group) * width % LANES
                turned = pltpu.roll(parts[part], amount, 1) if amount else parts[part]
                tile = jnp.where(lane_group == part, turned, tile)
            tiles.append(tile)
        return tiles

    tiles, copies = {}, []
    for band in range(bands):
        gather(band)
        tiles[band] = turn(band)
        if rows % 16 == 0:
            here = pl.ds(band * rows, rows)
            tile_ref[here, :] = jnp.concatenate(tiles[band], axis=0).astype(jnp.bfloat16)
            for slot in range(len(bands_out)):
                if bands_out[slot] == band:
                    there = out_ref.at[pl.ds(slot * rows, rows), :]
                    copies.append(pltpu.make_async_copy(tile_ref.at[here, :], there, sems.at[slot]))
                    copies[-1].start()
    if rows % 16:
        wanted = [tile for band in bands_out for tile in tiles[band]]
        for n in range(0, len(wanted), 2):
            tile_ref[n * 8 : n * 8 + 16, :] = jnp.concatenate(wanted[n : n + 2], axis=0).astype(jnp.bfloat16)
        copies.append(pltpu.make_async_copy(tile_ref, out_ref, sems.at[0]))
        copies[-1].start()
    for copy in copies:
        copy.wait()


def pick(offsets, spectra, bands_in, bands_out):
    rows, bands = spectra.shape[0], offsets.shape[0]
    out_rows = len(bands_out) * rows
    vmem = pl.BlockSpec(memory_space=pltpu.VMEM)
    return pl.pallas_call(
        functools.partial(pick_kernel, bands_in, bands_out),
        out_shape=jax.ShapeDtypeStruct((out_rows, LANES), jnp.bfloat16),
        in_specs=[vmem, vmem],
        out_specs=pl.BlockSpec(memory_space=pl.ANY),
        scratch_shapes=[
            pltpu.VMEM((bands, 4, 8, LANES), jnp.int32),
            pltpu.VMEM((bands, 32, LANES), jnp.float32),
            pltpu.VMEM((out_rows, LANES), jnp.bfloat16),
            pltpu.SemaphoreType.DMA((len(bands_out),)),
        ],
        compiler_params=pltpu.CompilerParams(vmem_limit_bytes=8 * 1024 * 1024),
        cost_estimate=pl.CostEstimate(flops=10_000_000, bytes_accessed=2 * spectra.size, transcendentals=0),
        name="pick",
    )(offsets, spectra)


def split(values, count):
    parts = []
    for _ in range(count):
        part = values.astype(jnp.bfloat16)
        parts.append(part)
        values = values - part.astype(jnp.float32)
    return parts


def prepare_kernel(first, run, durations_ref, starts_ref, antenna_ref, fractions_ref, mask_ref, weigh_ref, coef_ref, kernel_ref):
    rows = starts_ref.shape[0]
    count = mask_ref.shape[0] // rows
    mine = lax.axis_index("tm").astype(jnp.int32) * count
    sfts = antenna_ref.shape[1]
    sft = iota((rows, sfts), 1)
    sft = jnp.where(sft // run == 0, sft + first * run, jnp.where(sft // run == first, sft - first * run, sft))
    start = starts_ref[:, 0:1]
    after = sft >= start
    for j in range(count):
        inside = after & (sft < start + durations_ref[mine + j])
        mask_ref[pl.ds(j * rows, rows), :] = jnp.where(inside, 1.0, 0.0).astype(jnp.bfloat16)
    antenna = jnp.concatenate([antenna_ref[...], jnp.zeros((4, sfts), jnp.float32)], axis=0)
    place = iota(antenna.shape, 1) // run
    after = pltpu.roll(antenna, sfts - first * run, 1)
    before = pltpu.roll(antenna, first * run, 1)
    antenna = jnp.where(place == 0, after, jnp.where(place == first, before, antenna))
    a1, a2, b1, b2 = (antenna[n : n + 1] for n in range(4))
    terms = jnp.concatenate([a1 * a1 + a2 * a2, b1 * b1 + b2 * b2, a1 * b1 + a2 * b2, jnp.zeros((5, sfts), jnp.float32)], axis=0)
    weights = sum(lax.dot_general(mask_ref[...], part, NT, preferred_element_type=jnp.float32) for part in split(terms, 3))
    wa, wb, wc = (weights[:, n : n + 1] for n in range(3))
    shape = (rows * count, LANES)
    late = iota(shape, 1) >= LANES // 2
    coef_ref[0] = jnp.broadcast_to(1.0 / wa, shape)
    coef_ref[1] = jnp.broadcast_to(wa / (wa * wb - wc * wc), shape)
    coef_ref[2] = jnp.where(late, jnp.broadcast_to(wc / wa, shape), 0.0)
    upright = jnp.transpose(jnp.concatenate([antenna, jnp.zeros((LANES - 8, sfts), jnp.float32)], axis=0))
    shape = (sfts, LANES)
    late = iota(shape, 1) >= LANES // 2
    weigh_ref[0] = jnp.where(late, upright[:, 3:4], upright[:, 0:1])
    weigh_ref[1] = jnp.where(late, upright[:, 2:3], upright[:, 1:2])
    fractions = fractions_ref[...]
    templates = fractions.shape[1]
    blocks = kernel_ref.shape[1] // (4 * LANES)
    bin_id = iota((W, templates), 0)
    distance = fractions + (W // 2 - 1) - bin_id.astype(jnp.float32)
    alternate = 1.0 - 2.0 * (bin_id % 2).astype(jnp.float32)
    values = (alternate * jnp.sin(jnp.pi * fractions) / (jnp.pi * distance)).astype(jnp.bfloat16)
    kernel_ref[...] = jnp.zeros_like(kernel_ref)
    for part in range(2):
        for c in range(4):
            for b in range(blocks):
                row = ((part * 4 + c) * blocks + b) * W
                column = (c * blocks + b) * LANES
                kernel_ref[pl.ds(row, W), pl.ds(column, LANES)] = values[:, b * LANES : (b + 1) * LANES]


def prepare(durations, starts, antenna, fractions, first, run, cores):
    count, rows, sfts = durations.shape[0] // cores, starts.shape[0], antenna.shape[0]
    columns = 4 * fractions.shape[0]
    features = 4 * W * (fractions.shape[0] // LANES)
    vmem = pl.BlockSpec(memory_space=pltpu.VMEM)
    return pl.pallas_call(
        functools.partial(prepare_kernel, first, run),
        out_shape=(
            jax.ShapeDtypeStruct((count * rows, sfts), jnp.bfloat16),
            jax.ShapeDtypeStruct((2, sfts, LANES), jnp.float32),
            jax.ShapeDtypeStruct((3, count * rows, LANES), jnp.float32),
            jax.ShapeDtypeStruct((2 * features, columns), jnp.bfloat16),
        ),
        in_specs=[pl.BlockSpec(memory_space=pltpu.SMEM), vmem, vmem, vmem],
        out_specs=(vmem,) * 4,
        compiler_params=pltpu.CompilerParams(vmem_limit_bytes=16 * 1024 * 1024),
        cost_estimate=pl.CostEstimate(flops=100_000_000, bytes_accessed=4_000_000, transcendentals=0),
        name="prepare",
    )(durations, jnp.broadcast_to(starts[:, None], (rows, LANES)), antenna.T, fractions[None, :])


def statistic_kernel(windows_ref, mask_ref, weigh_ref, coef_ref, kernel_ref, map_ref, loudest_ref, found_ref):
    values = windows_ref[...].astype(jnp.float32)
    half = LANES // 2
    weighted = (weigh_ref[0] * values + weigh_ref[1] * pltpu.roll(values, half, 1)).astype(jnp.bfloat16)
    sums = jnp.dot(mask_ref[...], weighted, preferred_element_type=jnp.float32)
    sums = sums - coef_ref[2] * pltpu.roll(sums, half, 1)
    parts = jnp.concatenate(split(sums, 2), axis=1)
    found_ref[...] = jnp.dot(parts, kernel_ref[...], preferred_element_type=jnp.float32)
    templates = map_ref.shape[1]
    rows = map_ref.shape[0] // loudest_ref.shape[1]
    copies = loudest_ref.shape[0]
    per_step = LANES // rows
    for step in range(map_ref.shape[0] // LANES):
        here = pl.ds(step * LANES, LANES)
        best = None
        for b in range(templates // LANES):
            ra, ia, rb, ib = (found_ref[here, pl.ds(c * templates + b * LANES, LANES)] for c in range(4))
            result = coef_ref[0, here, :] * (ra * ra + ia * ia) + coef_ref[1, here, :] * (rb * rb + ib * ib)
            map_ref[here, pl.ds(b * LANES, LANES)] = result
            best = result if best is None else jnp.maximum(best, result)
        best = jnp.max(jnp.transpose(best), axis=0, keepdims=True)
        for n in range(per_step):
            turned = best if n == 0 else pltpu.roll(best, LANES - n * rows, 1)
            for copy in range(copies):
                loudest_ref[copy, pl.ds(step * per_step + n, 1), :] = turned


def statistic(windows, mask, weigh, coef, kernel, rows, copies):
    count = mask.shape[0] // rows
    templates = kernel.shape[1] // 4
    vmem = pl.BlockSpec(memory_space=pltpu.VMEM)
    return pl.pallas_call(
        statistic_kernel,
        out_shape=(
            jax.ShapeDtypeStruct((count * rows, templates), jnp.float32),
            jax.ShapeDtypeStruct((copies, count, LANES), jnp.float32),
        ),
        in_specs=[vmem] * 5,
        out_specs=(vmem, vmem),
        scratch_shapes=[pltpu.VMEM((count * rows, 4 * templates), jnp.float32)],
        compiler_params=pltpu.CompilerParams(vmem_limit_bytes=16 * 1024 * 1024),
        cost_estimate=pl.CostEstimate(flops=400_000_000, bytes_accessed=4_000_000, transcendentals=0),
        name="statistic",
    )(windows, mask, weigh, coef, kernel)


def exchange(values, axis, members):
    return lax.all_to_all(values, axis, split_axis=0, concat_axis=0, axis_index_groups=[members], tiled=True)


def body(spectra, offsets, fractions, antenna, starts, durations):
    bands, cores = lax.axis_size("tmpl"), lax.axis_size("tm")
    sft_rows = spectra.shape[0]
    grid_size = starts.shape[0]
    my_rows = grid_size // cores
    by_band = order(bands, bands // 2)
    first = (cores - 1) * bands + bands // 2
    by_run = order(cores * bands, first)
    known = exchange(jnp.broadcast_to(offsets.T[None], (bands,) + offsets.T.shape), "tmpl", by_band)
    windows = pick(known, spectra, by_band, [run % bands for run in by_run])
    windows, *late = lax.optimization_barrier((windows, durations, starts, antenna, fractions))
    durations, starts, antenna, fractions = late
    prepared = prepare(durations, starts, antenna, fractions, first, sft_rows, cores)
    arrived = exchange(windows.reshape(cores * bands, sft_rows, LANES), ("tm", "tmpl"), by_run)
    fstat_map, loudest = statistic(arrived.reshape(-1, LANES), *prepared, grid_size, bands)
    loudest = jnp.max(exchange(loudest, "tmpl", by_band)[:, :, :grid_size], axis=0)
    return (fstat_map.reshape(my_rows, grid_size, -1), loudest)


def solution(mesh):
    in_specs = (
        P(("grp", "tm", "tmpl"), None, None),
        P(("grp", "tm"), "tmpl"),
        P(("grp", "tmpl")),
        P("grp", None),
        P("grp"),
        P("grp"),
    )
    out_specs = (P("tm", None, ("grp", "tmpl")), P(("grp", "tm"), None))
    return jax.shard_map(body, mesh=mesh, in_specs=in_specs, out_specs=out_specs, check_vma=False)
```

```python
import functools

import jax
import jax.numpy as jnp
from jax import lax
from jax.experimental import pallas as pl
from jax.experimental.pallas import tpu as pltpu
from jax.sharding import PartitionSpec as P

W = 16
LANES = 128
NT = (((1,), (1,)), ((), ()))


def iota(shape, axis):
    return lax.broadcasted_iota(jnp.int32, shape, axis)


def order(size, first):
    members = list(range(size))
    members[0], members[first] = first, 0
    return members


def repeat_kernel(in_ref, out_ref, sems):
    copies = [pltpu.make_async_copy(in_ref, out_ref.at[n], sems.at[n]) for n in range(out_ref.shape[0])]
    for copy in copies:
        copy.start()
    for copy in copies:
        copy.wait()


def repeat(values, count):
    return pl.pallas_call(
        repeat_kernel,
        out_shape=jax.ShapeDtypeStruct((count,) + values.shape, values.dtype),
        in_specs=[pl.BlockSpec(memory_space=pl.ANY)],
        out_specs=pl.BlockSpec(memory_space=pltpu.VMEM),
        scratch_shapes=[pltpu.SemaphoreType.DMA((count,))],
        compiler_params=pltpu.CompilerParams(vmem_limit_bytes=8 * 1024 * 1024),
        cost_estimate=pl.CostEstimate(flops=0, bytes_accessed=32_000_000, transcendentals=0),
        name="repeat",
    )(values)


def pick_kernel(bands_in, bands_out, offset_ref, spec_ref, out_ref, place_ref, turn_ref, tile_ref, sems):
    rows, _, bins = spec_ref.shape
    bands, blocks, _ = offset_ref.shape
    band_width = bins // bands
    groups = rows // 8
    chunks = band_width // LANES
    width = blocks * W
    first = lax.axis_index("tmpl").astype(jnp.int32) * rows
    columns = pl.ds(pl.multiple_of(first // LANES * LANES, LANES), LANES)
    offsets = jnp.concatenate([offset_ref[bands_in.index(band), :, columns] for band in range(bands)], axis=0).astype(jnp.float32)
    lane = iota(offsets.shape, 1)
    offsets = jnp.take_along_axis(offsets, (lane >> 2) + first & (LANES - 1), axis=1, mode="promise_in_bounds")
    offsets = jnp.concatenate([offsets, jnp.zeros((LANES - bands * blocks, LANES), jnp.float32)], axis=0)
    upright = jnp.transpose(offsets).astype(jnp.int32)
    lane = iota((32, LANES), 1)
    places = upright[0:32]
    for group in range(1, groups):
        turned = pltpu.roll(upright[group * 32 : group * 32 + 32], group * bands * blocks, 1)
        places = jnp.where(lane < group * bands * blocks, places, turned)
    lane = iota((8, LANES), 1)
    lane_group = lane // width
    source = lane_group * (bands * blocks) + lane // W % blocks
    for band in range(bands):
        for pair in range(4):
            place = jnp.take_along_axis(places[pair * 8 : pair * 8 + 8], source + band * blocks, axis=1, mode="promise_in_bounds")
            place_ref[band, pair] = place + ((lane & (W - 1)) + lane_group * band_width)

    def gather(band):
        for pair in range(4):
            place = place_ref[band, pair]
            lane_id = place & (LANES - 1)
            chosen = place >> 7
            tile = jnp.zeros((8, LANES), jnp.float32)
            for group in range(groups):
                for chunk in range(chunks):
                    columns = pl.ds(band * band_width + chunk * LANES, LANES)
                    values = spec_ref[pl.ds(group * 8 + pair * 2, 2), :, columns]
                    values = values.astype(jnp.float32).reshape(8, LANES)
                    moved = jnp.take_along_axis(values, lane_id, axis=1, mode="promise_in_bounds")
                    tile = jnp.where(chosen == group * chunks + chunk, moved, tile)
            turn_ref[band, pl.ds(pair * 8, 8), :] = tile

    def turn(band):
        parts = [turn_ref[band, pl.ds(part, 8, stride=4), :] for part in range(4)]
        tiles = []
        for group in range(groups):
            tile = jnp.zeros((8, LANES), jnp.float32)
            for part in range(4):
                amount = (part - group) * width % LANES
                turned = pltpu.roll(parts[part], amount, 1) if amount else parts[part]
                tile = jnp.where(lane_group == part, turned, tile)
            tiles.append(tile)
        return tiles

    tiles, copies = {}, []
    for band in range(bands):
        gather(band)
        tiles[band] = turn(band)
        if rows % 16 == 0:
            here = pl.ds(band * rows, rows)
            tile_ref[here, :] = jnp.concatenate(tiles[band], axis=0).astype(jnp.bfloat16)
            for slot in range(len(bands_out)):
                if bands_out[slot] == band:
                    there = out_ref.at[pl.ds(slot * rows, rows), :]
                    copies.append(pltpu.make_async_copy(tile_ref.at[here, :], there, sems.at[slot]))
                    copies[-1].start()
    if rows % 16:
        wanted = [tile for band in bands_out for tile in tiles[band]]
        for n in range(0, len(wanted), 2):
            tile_ref[n * 8 : n * 8 + 16, :] = jnp.concatenate(wanted[n : n + 2], axis=0).astype(jnp.bfloat16)
        copies.append(pltpu.make_async_copy(tile_ref, out_ref, sems.at[0]))
        copies[-1].start()
    for copy in copies:
        copy.wait()


def pick(offsets, spectra, bands_in, bands_out):
    rows, bands = spectra.shape[0], offsets.shape[0]
    out_rows = len(bands_out) * rows
    vmem = pl.BlockSpec(memory_space=pltpu.VMEM)
    return pl.pallas_call(
        functools.partial(pick_kernel, bands_in, bands_out),
        out_shape=jax.ShapeDtypeStruct((out_rows, LANES), jnp.bfloat16),
        in_specs=[vmem, vmem],
        out_specs=pl.BlockSpec(memory_space=pl.ANY),
        scratch_shapes=[
            pltpu.VMEM((bands, 4, 8, LANES), jnp.int32),
            pltpu.VMEM((bands, 32, LANES), jnp.float32),
            pltpu.VMEM((out_rows, LANES), jnp.bfloat16),
            pltpu.SemaphoreType.DMA((len(bands_out),)),
        ],
        compiler_params=pltpu.CompilerParams(vmem_limit_bytes=8 * 1024 * 1024),
        cost_estimate=pl.CostEstimate(flops=10_000_000, bytes_accessed=2 * spectra.size, transcendentals=0),
        name="pick",
    )(offsets, spectra)


def split(values, count):
    parts = []
    for _ in range(count):
        part = values.astype(jnp.bfloat16)
        parts.append(part)
        values = values - part.astype(jnp.float32)
    return parts


def prepare_kernel(first, run, durations_ref, starts_ref, antenna_ref, fractions_ref, mask_ref, weigh_ref, coef_ref, kernel_ref):
    rows = starts_ref.shape[0]
    count = mask_ref.shape[0] // rows
    mine = lax.axis_index("tm").astype(jnp.int32) * count
    sfts = antenna_ref.shape[1]
    sft = iota((rows, sfts), 1)
    sft = jnp.where(sft // run == 0, sft + first * run, jnp.where(sft // run == first, sft - first * run, sft))
    start = starts_ref[:, 0:1]
    after = sft >= start
    for j in range(count):
        inside = after & (sft < start + durations_ref[mine + j])
        mask_ref[pl.ds(j * rows, rows), :] = jnp.where(inside, 1.0, 0.0).astype(jnp.bfloat16)
    antenna = jnp.concatenate([antenna_ref[...], jnp.zeros((4, sfts), jnp.float32)], axis=0)
    place = iota(antenna.shape, 1) // run
    after = pltpu.roll(antenna, sfts - first * run, 1)
    before = pltpu.roll(antenna, first * run, 1)
    antenna = jnp.where(place == 0, after, jnp.where(place == first, before, antenna))
    a1, a2, b1, b2 = (antenna[n : n + 1] for n in range(4))
    terms = jnp.concatenate([a1 * a1 + a2 * a2, b1 * b1 + b2 * b2, a1 * b1 + a2 * b2, jnp.zeros((5, sfts), jnp.float32)], axis=0)
    weights = sum(lax.dot_general(mask_ref[...], part, NT, preferred_element_type=jnp.float32) for part in split(terms, 3))
    wa, wb, wc = (weights[:, n : n + 1] for n in range(3))
    shape = (rows * count, LANES)
    late = iota(shape, 1) >= LANES // 2
    coef_ref[0] = jnp.broadcast_to(1.0 / wa, shape)
    coef_ref[1] = jnp.broadcast_to(wa / (wa * wb - wc * wc), shape)
    coef_ref[2] = jnp.where(late, jnp.broadcast_to(wc / wa, shape), 0.0)
    upright = jnp.transpose(jnp.concatenate([antenna, jnp.zeros((LANES - 8, sfts), jnp.float32)], axis=0))
    shape = (sfts, LANES)
    late = iota(shape, 1) >= LANES // 2
    weigh_ref[0] = jnp.where(late, upright[:, 3:4], upright[:, 0:1])
    weigh_ref[1] = jnp.where(late, upright[:, 2:3], upright[:, 1:2])
    fractions = fractions_ref[...]
    templates = fractions.shape[1]
    blocks = kernel_ref.shape[1] // (4 * LANES)
    bin_id = iota((W, templates), 0)
    distance = fractions + (W // 2 - 1) - bin_id.astype(jnp.float32)
    alternate = 1.0 - 2.0 * (bin_id % 2).astype(jnp.float32)
    values = (alternate * jnp.sin(jnp.pi * fractions) / (jnp.pi * distance)).astype(jnp.bfloat16)
    kernel_ref[...] = jnp.zeros_like(kernel_ref)
    for part in range(2):
        for c in range(4):
            for b in range(blocks):
                row = ((part * 4 + c) * blocks + b) * W
                column = (c * blocks + b) * LANES
                kernel_ref[pl.ds(row, W), pl.ds(column, LANES)] = values[:, b * LANES : (b + 1) * LANES]


def prepare(durations, starts, antenna, fractions, first, run, cores):
    count, rows, sfts = durations.shape[0] // cores, starts.shape[0], antenna.shape[0]
    columns = 4 * fractions.shape[0]
    features = 4 * W * (fractions.shape[0] // LANES)
    vmem = pl.BlockSpec(memory_space=pltpu.VMEM)
    return pl.pallas_call(
        functools.partial(prepare_kernel, first, run),
        out_shape=(
            jax.ShapeDtypeStruct((count * rows, sfts), jnp.bfloat16),
            jax.ShapeDtypeStruct((2, sfts, LANES), jnp.float32),
            jax.ShapeDtypeStruct((3, count * rows, LANES), jnp.float32),
            jax.ShapeDtypeStruct((2 * features, columns), jnp.bfloat16),
        ),
        in_specs=[pl.BlockSpec(memory_space=pltpu.SMEM), vmem, vmem, vmem],
        out_specs=(vmem,) * 4,
        compiler_params=pltpu.CompilerParams(vmem_limit_bytes=16 * 1024 * 1024),
        cost_estimate=pl.CostEstimate(flops=100_000_000, bytes_accessed=4_000_000, transcendentals=0),
        name="prepare",
    )(durations, jnp.broadcast_to(starts[:, None], (rows, LANES)), antenna.T, fractions[None, :])


def statistic_kernel(windows_ref, mask_ref, weigh_ref, coef_ref, kernel_ref, map_ref, loudest_ref, found_ref):
    values = windows_ref[...].astype(jnp.float32)
    half = LANES // 2
    weighted = (weigh_ref[0] * values + weigh_ref[1] * pltpu.roll(values, half, 1)).astype(jnp.bfloat16)
    sums = jnp.dot(mask_ref[...], weighted, preferred_element_type=jnp.float32)
    sums = sums - coef_ref[2] * pltpu.roll(sums, half, 1)
    parts = jnp.concatenate(split(sums, 2), axis=1)
    found_ref[...] = jnp.dot(parts, kernel_ref[...], preferred_element_type=jnp.float32)
    templates = map_ref.shape[1]
    rows = map_ref.shape[0] // loudest_ref.shape[1]
    copies = loudest_ref.shape[0]
    per_step = LANES // rows
    for step in range(map_ref.shape[0] // LANES):
        here = pl.ds(step * LANES, LANES)
        best = None
        for b in range(templates // LANES):
            ra, ia, rb, ib = (found_ref[here, pl.ds(c * templates + b * LANES, LANES)] for c in range(4))
            result = coef_ref[0, here, :] * (ra * ra + ia * ia) + coef_ref[1, here, :] * (rb * rb + ib * ib)
            map_ref[here, pl.ds(b * LANES, LANES)] = result
            best = result if best is None else jnp.maximum(best, result)
        best = jnp.max(jnp.transpose(best), axis=0, keepdims=True)
        for n in range(per_step):
            turned = best if n == 0 else pltpu.roll(best, LANES - n * rows, 1)
            for copy in range(copies):
                loudest_ref[copy, pl.ds(step * per_step + n, 1), :] = turned


def statistic(windows, mask, weigh, coef, kernel, rows, copies):
    count = mask.shape[0] // rows
    templates = kernel.shape[1] // 4
    vmem = pl.BlockSpec(memory_space=pltpu.VMEM)
    return pl.pallas_call(
        statistic_kernel,
        out_shape=(
            jax.ShapeDtypeStruct((count * rows, templates), jnp.float32),
            jax.ShapeDtypeStruct((copies, count, LANES), jnp.float32),
        ),
        in_specs=[vmem] * 5,
        out_specs=(vmem, vmem),
        scratch_shapes=[pltpu.VMEM((count * rows, 4 * templates), jnp.float32)],
        compiler_params=pltpu.CompilerParams(vmem_limit_bytes=16 * 1024 * 1024),
        cost_estimate=pl.CostEstimate(flops=400_000_000, bytes_accessed=4_000_000, transcendentals=0),
        name="statistic",
    )(windows, mask, weigh, coef, kernel)


def exchange(values, axis, members):
    return lax.all_to_all(values, axis, split_axis=0, concat_axis=0, axis_index_groups=[members], tiled=True)


def body(spectra, offsets, fractions, antenna, starts, durations):
    bands, cores = lax.axis_size("tmpl"), lax.axis_size("tm")
    sft_rows = spectra.shape[0]
    grid_size = starts.shape[0]
    my_rows = grid_size // cores
    by_band = order(bands, bands // 2)
    first = (cores - 1) * bands + bands // 2
    by_run = order(cores * bands, first)
    known = exchange(repeat(offsets.T, bands), "tmpl", by_band)
    windows = pick(known, spectra, by_band, [run % bands for run in by_run])
    windows, *late = lax.optimization_barrier((windows, durations, starts, antenna, fractions))
    durations, starts, antenna, fractions = late
    prepared = prepare(durations, starts, antenna, fractions, first, sft_rows, cores)
    arrived = exchange(windows.reshape(cores * bands, sft_rows, LANES), ("tm", "tmpl"), by_run)
    fstat_map, loudest = statistic(arrived.reshape(-1, LANES), *prepared, grid_size, bands)
    loudest = jnp.max(exchange(loudest, "tmpl", by_band)[:, :, :grid_size], axis=0)
    return (fstat_map.reshape(my_rows, grid_size, -1), loudest)


def solution(mesh):
    in_specs = (
        P(("grp", "tm", "tmpl"), None, None),
        P(("grp", "tm"), "tmpl"),
        P(("grp", "tmpl")),
        P("grp", None),
        P("grp"),
        P("grp"),
    )
    out_specs = (P("tm", None, ("grp", "tmpl")), P(("grp", "tm"), None))
    return jax.shard_map(body, mesh=mesh, in_specs=in_specs, out_specs=out_specs, check_vma=False)
```

```python
import functools

import jax
import jax.numpy as jnp
from jax import lax
from jax.experimental import pallas as pl
from jax.experimental.pallas import tpu as pltpu
from jax.sharding import PartitionSpec as P

W = 16
LANES = 128
NT = (((1,), (1,)), ((), ()))


def iota(shape, axis):
    return lax.broadcasted_iota(jnp.int32, shape, axis)


def order(size, first):
    members = list(range(size))
    members[0], members[first] = first, 0
    return members


def pick_kernel(bands_in, bands_out, offset_ref, spec_ref, out_ref, held_ref, place_ref, turn_ref, tile_ref, in_sems, sems):
    rows, _, bins = spec_ref.shape
    bands, blocks, _ = offset_ref.shape
    band_width = bins // bands
    groups = rows // 8
    chunks = band_width // LANES
    width = blocks * W
    arrivals = []
    for band in range(bands):
        columns = pl.ds(band * band_width, band_width)
        arrivals.append(pltpu.make_async_copy(spec_ref.at[:, :, columns], held_ref.at[:, :, columns], in_sems.at[band]))
        arrivals[-1].start()
    first = lax.axis_index("tmpl").astype(jnp.int32) * rows
    columns = pl.ds(pl.multiple_of(first // LANES * LANES, LANES), LANES)
    offsets = jnp.concatenate([offset_ref[bands_in.index(band), :, columns] for band in range(bands)], axis=0).astype(jnp.float32)
    lane = iota(offsets.shape, 1)
    offsets = jnp.take_along_axis(offsets, (lane >> 2) + first & (LANES - 1), axis=1, mode="promise_in_bounds")
    offsets = jnp.concatenate([offsets, jnp.zeros((LANES - bands * blocks, LANES), jnp.float32)], axis=0)
    upright = jnp.transpose(offsets).astype(jnp.int32)
    lane = iota((32, LANES), 1)
    places = upright[0:32]
    for group in range(1, groups):
        turned = pltpu.roll(upright[group * 32 : group * 32 + 32], group * bands * blocks, 1)
        places = jnp.where(lane < group * bands * blocks, places, turned)
    lane = iota((8, LANES), 1)
    lane_group = lane // width
    source = lane_group * (bands * blocks) + lane // W % blocks
    for band in range(bands):
        for pair in range(4):
            place = jnp.take_along_axis(places[pair * 8 : pair * 8 + 8], source + band * blocks, axis=1, mode="promise_in_bounds")
            place_ref[band, pair] = place + ((lane & (W - 1)) + lane_group * band_width)

    def gather(band):
        for pair in range(4):
            place = place_ref[band, pair]
            lane_id = place & (LANES - 1)
            chosen = place >> 7
            tile = jnp.zeros((8, LANES), jnp.float32)
            for group in range(groups):
                for chunk in range(chunks):
                    columns = pl.ds(band * band_width + chunk * LANES, LANES)
                    values = held_ref[pl.ds(group * 8 + pair * 2, 2), :, columns]
                    values = values.astype(jnp.float32).reshape(8, LANES)
                    moved = jnp.take_along_axis(values, lane_id, axis=1, mode="promise_in_bounds")
                    tile = jnp.where(chosen == group * chunks + chunk, moved, tile)
            turn_ref[band, pl.ds(pair * 8, 8), :] = tile

    def turn(band):
        parts = [turn_ref[band, pl.ds(part, 8, stride=4), :] for part in range(4)]
        tiles = []
        for group in range(groups):
            tile = jnp.zeros((8, LANES), jnp.float32)
            for part in range(4):
                amount = (part - group) * width % LANES
                turned = pltpu.roll(parts[part], amount, 1) if amount else parts[part]
                tile = jnp.where(lane_group == part, turned, tile)
            tiles.append(tile)
        return tiles

    tiles, copies = {}, []
    for band in range(bands):
        arrivals[band].wait()
        gather(band)
        tiles[band] = turn(band)
        if rows % 16 == 0:
            here = pl.ds(band * rows, rows)
            tile_ref[here, :] = jnp.concatenate(tiles[band], axis=0).astype(jnp.bfloat16)
            for slot in range(len(bands_out)):
                if bands_out[slot] == band:
                    there = out_ref.at[pl.ds(slot * rows, rows), :]
                    copies.append(pltpu.make_async_copy(tile_ref.at[here, :], there, sems.at[slot]))
                    copies[-1].start()
    if rows % 16:
        wanted = [tile for band in bands_out for tile in tiles[band]]
        for n in range(0, len(wanted), 2):
            tile_ref[n * 8 : n * 8 + 16, :] = jnp.concatenate(wanted[n : n + 2], axis=0).astype(jnp.bfloat16)
        copies.append(pltpu.make_async_copy(tile_ref, out_ref, sems.at[0]))
        copies[-1].start()
    for copy in copies:
        copy.wait()


def pick(offsets, spectra, bands_in, bands_out):
    rows, bands = spectra.shape[0], offsets.shape[0]
    out_rows = len(bands_out) * rows
    vmem = pl.BlockSpec(memory_space=pltpu.VMEM)
    return pl.pallas_call(
        functools.partial(pick_kernel, bands_in, bands_out),
        out_shape=jax.ShapeDtypeStruct((out_rows, LANES), jnp.bfloat16),
        in_specs=[vmem, pl.BlockSpec(memory_space=pl.ANY)],
        out_specs=pl.BlockSpec(memory_space=pl.ANY),
        scratch_shapes=[
            pltpu.VMEM(spectra.shape, spectra.dtype),
            pltpu.VMEM((bands, 4, 8, LANES), jnp.int32),
            pltpu.VMEM((bands, 32, LANES), jnp.float32),
            pltpu.VMEM((out_rows, LANES), jnp.bfloat16),
            pltpu.SemaphoreType.DMA((bands,)),
            pltpu.SemaphoreType.DMA((len(bands_out),)),
        ],
        compiler_params=pltpu.CompilerParams(vmem_limit_bytes=52 * 1024 * 1024),
        cost_estimate=pl.CostEstimate(flops=10_000_000, bytes_accessed=2 * spectra.size, transcendentals=0),
        name="pick",
    )(offsets, spectra)


def split(values, count):
    parts = []
    for _ in range(count):
        part = values.astype(jnp.bfloat16)
        parts.append(part)
        values = values - part.astype(jnp.float32)
    return parts


def prepare_kernel(first, run, durations_ref, starts_ref, antenna_ref, fractions_ref, mask_ref, weigh_ref, coef_ref, kernel_ref):
    rows = starts_ref.shape[0]
    count = mask_ref.shape[0] // rows
    mine = lax.axis_index("tm").astype(jnp.int32) * count
    sfts = antenna_ref.shape[1]
    sft = iota((rows, sfts), 1)
    sft = jnp.where(sft // run == 0, sft + first * run, jnp.where(sft // run == first, sft - first * run, sft))
    start = starts_ref[:, 0:1]
    after = sft >= start
    for j in range(count):
        inside = after & (sft < start + durations_ref[mine + j])
        mask_ref[pl.ds(j * rows, rows), :] = jnp.where(inside, 1.0, 0.0).astype(jnp.bfloat16)
    antenna = jnp.concatenate([antenna_ref[...], jnp.zeros((4, sfts), jnp.float32)], axis=0)
    place = iota(antenna.shape, 1) // run
    after = pltpu.roll(antenna, sfts - first * run, 1)
    before = pltpu.roll(antenna, first * run, 1)
    antenna = jnp.where(place == 0, after, jnp.where(place == first, before, antenna))
    a1, a2, b1, b2 = (antenna[n : n + 1] for n in range(4))
    terms = jnp.concatenate([a1 * a1 + a2 * a2, b1 * b1 + b2 * b2, a1 * b1 + a2 * b2, jnp.zeros((5, sfts), jnp.float32)], axis=0)
    weights = sum(lax.dot_general(mask_ref[...], part, NT, preferred_element_type=jnp.float32) for part in split(terms, 3))
    wa, wb, wc = (weights[:, n : n + 1] for n in range(3))
    shape = (rows * count, LANES)
    late = iota(shape, 1) >= LANES // 2
    coef_ref[0] = jnp.broadcast_to(1.0 / wa, shape)
    coef_ref[1] = jnp.broadcast_to(wa / (wa * wb - wc * wc), shape)
    coef_ref[2] = jnp.where(late, jnp.broadcast_to(wc / wa, shape), 0.0)
    upright = jnp.transpose(jnp.concatenate([antenna, jnp.zeros((LANES - 8, sfts), jnp.float32)], axis=0))
    shape = (sfts, LANES)
    late = iota(shape, 1) >= LANES // 2
    weigh_ref[0] = jnp.where(late, upright[:, 3:4], upright[:, 0:1])
    weigh_ref[1] = jnp.where(late, upright[:, 2:3], upright[:, 1:2])
    fractions = fractions_ref[...]
    templates = fractions.shape[1]
    blocks = kernel_ref.shape[1] // (4 * LANES)
    bin_id = iota((W, templates), 0)
    distance = fractions + (W // 2 - 1) - bin_id.astype(jnp.float32)
    alternate = 1.0 - 2.0 * (bin_id % 2).astype(jnp.float32)
    values = (alternate * jnp.sin(jnp.pi * fractions) / (jnp.pi * distance)).astype(jnp.bfloat16)
    kernel_ref[...] = jnp.zeros_like(kernel_ref)
    for part in range(2):
        for c in range(4):
            for b in range(blocks):
                row = ((part * 4 + c) * blocks + b) * W
                column = (c * blocks + b) * LANES
                kernel_ref[pl.ds(row, W), pl.ds(column, LANES)] = values[:, b * LANES : (b + 1) * LANES]


def prepare(durations, starts, antenna, fractions, first, run, cores):
    count, rows, sfts = durations.shape[0] // cores, starts.shape[0], antenna.shape[0]
    columns = 4 * fractions.shape[0]
    features = 4 * W * (fractions.shape[0] // LANES)
    vmem = pl.BlockSpec(memory_space=pltpu.VMEM)
    return pl.pallas_call(
        functools.partial(prepare_kernel, first, run),
        out_shape=(
            jax.ShapeDtypeStruct((count * rows, sfts), jnp.bfloat16),
            jax.ShapeDtypeStruct((2, sfts, LANES), jnp.float32),
            jax.ShapeDtypeStruct((3, count * rows, LANES), jnp.float32),
            jax.ShapeDtypeStruct((2 * features, columns), jnp.bfloat16),
        ),
        in_specs=[pl.BlockSpec(memory_space=pltpu.SMEM), vmem, vmem, vmem],
        out_specs=(vmem,) * 4,
        compiler_params=pltpu.CompilerParams(vmem_limit_bytes=16 * 1024 * 1024),
        cost_estimate=pl.CostEstimate(flops=100_000_000, bytes_accessed=4_000_000, transcendentals=0),
        name="prepare",
    )(durations, jnp.broadcast_to(starts[:, None], (rows, LANES)), antenna.T, fractions[None, :])


def statistic_kernel(windows_ref, mask_ref, weigh_ref, coef_ref, kernel_ref, map_ref, loudest_ref, found_ref):
    values = windows_ref[...].astype(jnp.float32)
    half = LANES // 2
    weighted = (weigh_ref[0] * values + weigh_ref[1] * pltpu.roll(values, half, 1)).astype(jnp.bfloat16)
    sums = jnp.dot(mask_ref[...], weighted, preferred_element_type=jnp.float32)
    sums = sums - coef_ref[2] * pltpu.roll(sums, half, 1)
    parts = jnp.concatenate(split(sums, 2), axis=1)
    found_ref[...] = jnp.dot(parts, kernel_ref[...], preferred_element_type=jnp.float32)
    templates = map_ref.shape[1]
    rows = map_ref.shape[0] // loudest_ref.shape[1]
    copies = loudest_ref.shape[0]
    per_step = LANES // rows
    for step in range(map_ref.shape[0] // LANES):
        here = pl.ds(step * LANES, LANES)
        best = None
        for b in range(templates // LANES):
            ra, ia, rb, ib = (found_ref[here, pl.ds(c * templates + b * LANES, LANES)] for c in range(4))
            result = coef_ref[0, here, :] * (ra * ra + ia * ia) + coef_ref[1, here, :] * (rb * rb + ib * ib)
            map_ref[here, pl.ds(b * LANES, LANES)] = result
            best = result if best is None else jnp.maximum(best, result)
        best = jnp.max(jnp.transpose(best), axis=0, keepdims=True)
        for n in range(per_step):
            turned = best if n == 0 else pltpu.roll(best, LANES - n * rows, 1)
            for copy in range(copies):
                loudest_ref[copy, pl.ds(step * per_step + n, 1), :] = turned


def statistic(windows, mask, weigh, coef, kernel, rows, copies):
    count = mask.shape[0] // rows
    templates = kernel.shape[1] // 4
    vmem = pl.BlockSpec(memory_space=pltpu.VMEM)
    return pl.pallas_call(
        statistic_kernel,
        out_shape=(
            jax.ShapeDtypeStruct((count * rows, templates), jnp.float32),
            jax.ShapeDtypeStruct((copies, count, LANES), jnp.float32),
        ),
        in_specs=[vmem] * 5,
        out_specs=(vmem, vmem),
        scratch_shapes=[pltpu.VMEM((count * rows, 4 * templates), jnp.float32)],
        compiler_params=pltpu.CompilerParams(vmem_limit_bytes=16 * 1024 * 1024),
        cost_estimate=pl.CostEstimate(flops=400_000_000, bytes_accessed=4_000_000, transcendentals=0),
        name="statistic",
    )(windows, mask, weigh, coef, kernel)


def exchange(values, axis, members):
    return lax.all_to_all(values, axis, split_axis=0, concat_axis=0, axis_index_groups=[members], tiled=True)


def body(spectra, offsets, fractions, antenna, starts, durations):
    bands, cores = lax.axis_size("tmpl"), lax.axis_size("tm")
    sft_rows = spectra.shape[0]
    grid_size = starts.shape[0]
    my_rows = grid_size // cores
    by_band = order(bands, bands // 2)
    first = (cores - 1) * bands + bands // 2
    by_run = order(cores * bands, first)
    known = exchange(jnp.broadcast_to(offsets.T[None], (bands,) + offsets.T.shape), "tmpl", by_band)
    windows = pick(known, spectra, by_band, [run % bands for run in by_run])
    windows, *late = lax.optimization_barrier((windows, durations, starts, antenna, fractions))
    durations, starts, antenna, fractions = late
    prepared = prepare(durations, starts, antenna, fractions, first, sft_rows, cores)
    arrived = exchange(windows.reshape(cores * bands, sft_rows, LANES), ("tm", "tmpl"), by_run)
    fstat_map, loudest = statistic(arrived.reshape(-1, LANES), *prepared, grid_size, bands)
    loudest = jnp.max(exchange(loudest, "tmpl", by_band)[:, :, :grid_size], axis=0)
    return (fstat_map.reshape(my_rows, grid_size, -1), loudest)


def solution(mesh):
    in_specs = (
        P(("grp", "tm", "tmpl"), None, None),
        P(("grp", "tm"), "tmpl"),
        P(("grp", "tmpl")),
        P("grp", None),
        P("grp"),
        P("grp"),
    )
    out_specs = (P("tm", None, ("grp", "tmpl")), P(("grp", "tm"), None))
    return jax.shard_map(body, mesh=mesh, in_specs=in_specs, out_specs=out_specs, check_vma=False)
```

```python
import functools

import jax
import jax.numpy as jnp
from jax import lax
from jax.experimental import pallas as pl
from jax.experimental.pallas import tpu as pltpu
from jax.sharding import PartitionSpec as P

W = 16
LANES = 128
NT = (((1,), (1,)), ((), ()))


def iota(shape, axis):
    return lax.broadcasted_iota(jnp.int32, shape, axis)


def order(size, first):
    members = list(range(size))
    members[0], members[first] = first, 0
    return members


def hold_kernel(spec_ref, out_ref, sem):
    copy = pltpu.make_async_copy(spec_ref, out_ref, sem)
    copy.start()
    copy.wait()


def hold(spectra):
    return pl.pallas_call(
        hold_kernel,
        out_shape=jax.ShapeDtypeStruct(spectra.shape, spectra.dtype),
        in_specs=[pl.BlockSpec(memory_space=pl.ANY)],
        out_specs=pl.BlockSpec(memory_space=pltpu.VMEM),
        scratch_shapes=[pltpu.SemaphoreType.DMA],
        compiler_params=pltpu.CompilerParams(vmem_limit_bytes=8 * 1024 * 1024),
        cost_estimate=pl.CostEstimate(flops=0, bytes_accessed=4 * spectra.size, transcendentals=0),
        name="hold",
    )(spectra)


def pick_kernel(bands_in, bands_out, offset_ref, spec_ref, out_ref, place_ref, turn_ref, tile_ref, sems):
    rows, _, bins = spec_ref.shape
    bands, blocks, _ = offset_ref.shape
    band_width = bins // bands
    groups = rows // 8
    chunks = band_width // LANES
    width = blocks * W
    first = lax.axis_index("tmpl").astype(jnp.int32) * rows
    columns = pl.ds(pl.multiple_of(first // LANES * LANES, LANES), LANES)
    offsets = jnp.concatenate([offset_ref[bands_in.index(band), :, columns] for band in range(bands)], axis=0).astype(jnp.float32)
    lane = iota(offsets.shape, 1)
    offsets = jnp.take_along_axis(offsets, (lane >> 2) + first & (LANES - 1), axis=1, mode="promise_in_bounds")
    offsets = jnp.concatenate([offsets, jnp.zeros((LANES - bands * blocks, LANES), jnp.float32)], axis=0)
    upright = jnp.transpose(offsets).astype(jnp.int32)
    lane = iota((32, LANES), 1)
    places = upright[0:32]
    for group in range(1, groups):
        turned = pltpu.roll(upright[group * 32 : group * 32 + 32], group * bands * blocks, 1)
        places = jnp.where(lane < group * bands * blocks, places, turned)
    lane = iota((8, LANES), 1)
    lane_group = lane // width
    source = lane_group * (bands * blocks) + lane // W % blocks
    for band in range(bands):
        for pair in range(4):
            place = jnp.take_along_axis(places[pair * 8 : pair * 8 + 8], source + band * blocks, axis=1, mode="promise_in_bounds")
            place_ref[band, pair] = place + ((lane & (W - 1)) + lane_group * band_width)

    def gather(band):
        for pair in range(4):
            place = place_ref[band, pair]
            lane_id = place & (LANES - 1)
            chosen = place >> 7
            tile = jnp.zeros((8, LANES), jnp.float32)
            for group in range(groups):
                for chunk in range(chunks):
                    columns = pl.ds(band * band_width + chunk * LANES, LANES)
                    values = spec_ref[pl.ds(group * 8 + pair * 2, 2), :, columns]
                    values = values.astype(jnp.float32).reshape(8, LANES)
                    moved = jnp.take_along_axis(values, lane_id, axis=1, mode="promise_in_bounds")
                    tile = jnp.where(chosen == group * chunks + chunk, moved, tile)
            turn_ref[band, pl.ds(pair * 8, 8), :] = tile

    def turn(band):
        parts = [turn_ref[band, pl.ds(part, 8, stride=4), :] for part in range(4)]
        tiles = []
        for group in range(groups):
            tile = jnp.zeros((8, LANES), jnp.float32)
            for part in range(4):
                amount = (part - group) * width % LANES
                turned = pltpu.roll(parts[part], amount, 1) if amount else parts[part]
                tile = jnp.where(lane_group == part, turned, tile)
            tiles.append(tile)
        return tiles

    tiles, copies = {}, []
    for band in range(bands):
        gather(band)
        tiles[band] = turn(band)
        if rows % 16 == 0:
            here = pl.ds(band * rows, rows)
            tile_ref[here, :] = jnp.concatenate(tiles[band], axis=0).astype(jnp.bfloat16)
            for slot in range(len(bands_out)):
                if bands_out[slot] == band:
                    there = out_ref.at[pl.ds(slot * rows, rows), :]
                    copies.append(pltpu.make_async_copy(tile_ref.at[here, :], there, sems.at[slot]))
                    copies[-1].start()
    if rows % 16:
        wanted = [tile for band in bands_out for tile in tiles[band]]
        for n in range(0, len(wanted), 2):
            tile_ref[n * 8 : n * 8 + 16, :] = jnp.concatenate(wanted[n : n + 2], axis=0).astype(jnp.bfloat16)
        copies.append(pltpu.make_async_copy(tile_ref, out_ref, sems.at[0]))
        copies[-1].start()
    for copy in copies:
        copy.wait()


def pick(offsets, spectra, bands_in, bands_out):
    rows, bands = spectra.shape[0], offsets.shape[0]
    out_rows = len(bands_out) * rows
    vmem = pl.BlockSpec(memory_space=pltpu.VMEM)
    return pl.pallas_call(
        functools.partial(pick_kernel, bands_in, bands_out),
        out_shape=jax.ShapeDtypeStruct((out_rows, LANES), jnp.bfloat16),
        in_specs=[vmem, vmem],
        out_specs=pl.BlockSpec(memory_space=pl.ANY),
        scratch_shapes=[
            pltpu.VMEM((bands, 4, 8, LANES), jnp.int32),
            pltpu.VMEM((bands, 32, LANES), jnp.float32),
            pltpu.VMEM((out_rows, LANES), jnp.bfloat16),
            pltpu.SemaphoreType.DMA((len(bands_out),)),
        ],
        compiler_params=pltpu.CompilerParams(vmem_limit_bytes=8 * 1024 * 1024),
        cost_estimate=pl.CostEstimate(flops=10_000_000, bytes_accessed=2 * spectra.size, transcendentals=0),
        name="pick",
    )(offsets, spectra)


def split(values, count):
    parts = []
    for _ in range(count):
        part = values.astype(jnp.bfloat16)
        parts.append(part)
        values = values - part.astype(jnp.float32)
    return parts


def prepare_kernel(first, run, durations_ref, starts_ref, antenna_ref, fractions_ref, mask_ref, weigh_ref, coef_ref, kernel_ref):
    rows = starts_ref.shape[0]
    count = mask_ref.shape[0] // rows
    mine = lax.axis_index("tm").astype(jnp.int32) * count
    sfts = antenna_ref.shape[1]
    sft = iota((rows, sfts), 1)
    sft = jnp.where(sft // run == 0, sft + first * run, jnp.where(sft // run == first, sft - first * run, sft))
    start = starts_ref[:, 0:1]
    after = sft >= start
    for j in range(count):
        inside = after & (sft < start + durations_ref[mine + j])
        mask_ref[pl.ds(j * rows, rows), :] = jnp.where(inside, 1.0, 0.0).astype(jnp.bfloat16)
    antenna = jnp.concatenate([antenna_ref[...], jnp.zeros((4, sfts), jnp.float32)], axis=0)
    place = iota(antenna.shape, 1) // run
    after = pltpu.roll(antenna, sfts - first * run, 1)
    before = pltpu.roll(antenna, first * run, 1)
    antenna = jnp.where(place == 0, after, jnp.where(place == first, before, antenna))
    a1, a2, b1, b2 = (antenna[n : n + 1] for n in range(4))
    terms = jnp.concatenate([a1 * a1 + a2 * a2, b1 * b1 + b2 * b2, a1 * b1 + a2 * b2, jnp.zeros((5, sfts), jnp.float32)], axis=0)
    weights = sum(lax.dot_general(mask_ref[...], part, NT, preferred_element_type=jnp.float32) for part in split(terms, 3))
    wa, wb, wc = (weights[:, n : n + 1] for n in range(3))
    shape = (rows * count, LANES)
    late = iota(shape, 1) >= LANES // 2
    coef_ref[0] = jnp.broadcast_to(1.0 / wa, shape)
    coef_ref[1] = jnp.broadcast_to(wa / (wa * wb - wc * wc), shape)
    coef_ref[2] = jnp.where(late, jnp.broadcast_to(wc / wa, shape), 0.0)
    upright = jnp.transpose(jnp.concatenate([antenna, jnp.zeros((LANES - 8, sfts), jnp.float32)], axis=0))
    shape = (sfts, LANES)
    late = iota(shape, 1) >= LANES // 2
    weigh_ref[0] = jnp.where(late, upright[:, 3:4], upright[:, 0:1])
    weigh_ref[1] = jnp.where(late, upright[:, 2:3], upright[:, 1:2])
    fractions = fractions_ref[...]
    templates = fractions.shape[1]
    blocks = kernel_ref.shape[1] // (4 * LANES)
    bin_id = iota((W, templates), 0)
    distance = fractions + (W // 2 - 1) - bin_id.astype(jnp.float32)
    alternate = 1.0 - 2.0 * (bin_id % 2).astype(jnp.float32)
    values = (alternate * jnp.sin(jnp.pi * fractions) / (jnp.pi * distance)).astype(jnp.bfloat16)
    kernel_ref[...] = jnp.zeros_like(kernel_ref)
    for part in range(2):
        for c in range(4):
            for b in range(blocks):
                row = ((part * 4 + c) * blocks + b) * W
                column = (c * blocks + b) * LANES
                kernel_ref[pl.ds(row, W), pl.ds(column, LANES)] = values[:, b * LANES : (b + 1) * LANES]


def prepare(durations, starts, antenna, fractions, first, run, cores):
    count, rows, sfts = durations.shape[0] // cores, starts.shape[0], antenna.shape[0]
    columns = 4 * fractions.shape[0]
    features = 4 * W * (fractions.shape[0] // LANES)
    vmem = pl.BlockSpec(memory_space=pltpu.VMEM)
    return pl.pallas_call(
        functools.partial(prepare_kernel, first, run),
        out_shape=(
            jax.ShapeDtypeStruct((count * rows, sfts), jnp.bfloat16),
            jax.ShapeDtypeStruct((2, sfts, LANES), jnp.float32),
            jax.ShapeDtypeStruct((3, count * rows, LANES), jnp.float32),
            jax.ShapeDtypeStruct((2 * features, columns), jnp.bfloat16),
        ),
        in_specs=[pl.BlockSpec(memory_space=pltpu.SMEM), vmem, vmem, vmem],
        out_specs=(vmem,) * 4,
        compiler_params=pltpu.CompilerParams(vmem_limit_bytes=16 * 1024 * 1024),
        cost_estimate=pl.CostEstimate(flops=100_000_000, bytes_accessed=4_000_000, transcendentals=0),
        name="prepare",
    )(durations, jnp.broadcast_to(starts[:, None], (rows, LANES)), antenna.T, fractions[None, :])


def statistic_kernel(windows_ref, mask_ref, weigh_ref, coef_ref, kernel_ref, map_ref, loudest_ref, found_ref):
    values = windows_ref[...].astype(jnp.float32)
    half = LANES // 2
    weighted = (weigh_ref[0] * values + weigh_ref[1] * pltpu.roll(values, half, 1)).astype(jnp.bfloat16)
    sums = jnp.dot(mask_ref[...], weighted, preferred_element_type=jnp.float32)
    sums = sums - coef_ref[2] * pltpu.roll(sums, half, 1)
    parts = jnp.concatenate(split(sums, 2), axis=1)
    found_ref[...] = jnp.dot(parts, kernel_ref[...], preferred_element_type=jnp.float32)
    templates = map_ref.shape[1]
    rows = map_ref.shape[0] // loudest_ref.shape[1]
    copies = loudest_ref.shape[0]
    per_step = LANES // rows
    for step in range(map_ref.shape[0] // LANES):
        here = pl.ds(step * LANES, LANES)
        best = None
        for b in range(templates // LANES):
            ra, ia, rb, ib = (found_ref[here, pl.ds(c * templates + b * LANES, LANES)] for c in range(4))
            result = coef_ref[0, here, :] * (ra * ra + ia * ia) + coef_ref[1, here, :] * (rb * rb + ib * ib)
            map_ref[here, pl.ds(b * LANES, LANES)] = result
            best = result if best is None else jnp.maximum(best, result)
        best = jnp.max(jnp.transpose(best), axis=0, keepdims=True)
        for n in range(per_step):
            turned = best if n == 0 else pltpu.roll(best, LANES - n * rows, 1)
            for copy in range(copies):
                loudest_ref[copy, pl.ds(step * per_step + n, 1), :] = turned


def statistic(windows, mask, weigh, coef, kernel, rows, copies):
    count = mask.shape[0] // rows
    templates = kernel.shape[1] // 4
    vmem = pl.BlockSpec(memory_space=pltpu.VMEM)
    return pl.pallas_call(
        statistic_kernel,
        out_shape=(
            jax.ShapeDtypeStruct((count * rows, templates), jnp.float32),
            jax.ShapeDtypeStruct((copies, count, LANES), jnp.float32),
        ),
        in_specs=[vmem] * 5,
        out_specs=(vmem, vmem),
        scratch_shapes=[pltpu.VMEM((count * rows, 4 * templates), jnp.float32)],
        compiler_params=pltpu.CompilerParams(vmem_limit_bytes=16 * 1024 * 1024),
        cost_estimate=pl.CostEstimate(flops=400_000_000, bytes_accessed=4_000_000, transcendentals=0),
        name="statistic",
    )(windows, mask, weigh, coef, kernel)


def exchange(values, axis, members):
    return lax.all_to_all(values, axis, split_axis=0, concat_axis=0, axis_index_groups=[members], tiled=True)


def body(spectra, offsets, fractions, antenna, starts, durations):
    bands, cores = lax.axis_size("tmpl"), lax.axis_size("tm")
    sft_rows = spectra.shape[0]
    grid_size = starts.shape[0]
    my_rows = grid_size // cores
    by_band = order(bands, bands // 2)
    first = (cores - 1) * bands + bands // 2
    by_run = order(cores * bands, first)
    known = exchange(jnp.broadcast_to(offsets.T[None], (bands,) + offsets.T.shape), "tmpl", by_band)
    windows = pick(known, hold(spectra), by_band, [run % bands for run in by_run])
    windows, *late = lax.optimization_barrier((windows, durations, starts, antenna, fractions))
    durations, starts, antenna, fractions = late
    prepared = prepare(durations, starts, antenna, fractions, first, sft_rows, cores)
    arrived = exchange(windows.reshape(cores * bands, sft_rows, LANES), ("tm", "tmpl"), by_run)
    fstat_map, loudest = statistic(arrived.reshape(-1, LANES), *prepared, grid_size, bands)
    loudest = jnp.max(exchange(loudest, "tmpl", by_band)[:, :, :grid_size], axis=0)
    return (fstat_map.reshape(my_rows, grid_size, -1), loudest)


def solution(mesh):
    in_specs = (
        P(("grp", "tm", "tmpl"), None, None),
        P(("grp", "tm"), "tmpl"),
        P(("grp", "tmpl")),
        P("grp", None),
        P("grp"),
        P("grp"),
    )
    out_specs = (P("tm", None, ("grp", "tmpl")), P(("grp", "tm"), None))
    return jax.shard_map(body, mesh=mesh, in_specs=in_specs, out_specs=out_specs, check_vma=False)
```

```python
import functools

import jax
import jax.numpy as jnp
from jax import lax
from jax.experimental import pallas as pl
from jax.experimental.pallas import tpu as pltpu
from jax.sharding import PartitionSpec as P

W = 16
LANES = 128
NT = (((1,), (1,)), ((), ()))


def iota(shape, axis):
    return lax.broadcasted_iota(jnp.int32, shape, axis)


def order(size, first):
    members = list(range(size))
    members[0], members[first] = first, 0
    return members


def hold_kernel(spec_ref, out_ref, sem):
    copy = pltpu.make_async_copy(spec_ref, out_ref, sem)
    copy.start()
    copy.wait()


def hold(spectra):
    return pl.pallas_call(
        hold_kernel,
        out_shape=jax.ShapeDtypeStruct(spectra.shape, spectra.dtype),
        in_specs=[pl.BlockSpec(memory_space=pl.ANY)],
        out_specs=pl.BlockSpec(memory_space=pltpu.VMEM),
        scratch_shapes=[pltpu.SemaphoreType.DMA],
        compiler_params=pltpu.CompilerParams(vmem_limit_bytes=8 * 1024 * 1024),
        cost_estimate=pl.CostEstimate(flops=0, bytes_accessed=4 * spectra.size, transcendentals=0),
        name="hold",
    )(spectra)


def pick_kernel(bands_in, bands_out, offset_ref, spec_ref, out_ref, place_ref, turn_ref):
    rows, _, bins = spec_ref.shape
    bands, blocks, _ = offset_ref.shape
    band_width = bins // bands
    groups = rows // 8
    chunks = band_width // LANES
    width = blocks * W
    first = lax.axis_index("tmpl").astype(jnp.int32) * rows
    columns = pl.ds(pl.multiple_of(first // LANES * LANES, LANES), LANES)
    offsets = jnp.concatenate([offset_ref[bands_in.index(band), :, columns] for band in range(bands)], axis=0).astype(jnp.float32)
    lane = iota(offsets.shape, 1)
    offsets = jnp.take_along_axis(offsets, (lane >> 2) + first & (LANES - 1), axis=1, mode="promise_in_bounds")
    offsets = jnp.concatenate([offsets, jnp.zeros((LANES - bands * blocks, LANES), jnp.float32)], axis=0)
    upright = jnp.transpose(offsets).astype(jnp.int32)
    lane = iota((32, LANES), 1)
    places = upright[0:32]
    for group in range(1, groups):
        turned = pltpu.roll(upright[group * 32 : group * 32 + 32], group * bands * blocks, 1)
        places = jnp.where(lane < group * bands * blocks, places, turned)
    lane = iota((8, LANES), 1)
    lane_group = lane // width
    source = lane_group * (bands * blocks) + lane // W % blocks
    for band in range(bands):
        for pair in range(4):
            place = jnp.take_along_axis(places[pair * 8 : pair * 8 + 8], source + band * blocks, axis=1, mode="promise_in_bounds")
            place_ref[band, pair] = place + ((lane & (W - 1)) + lane_group * band_width)

    def gather(band):
        for pair in range(4):
            place = place_ref[band, pair]
            lane_id = place & (LANES - 1)
            chosen = place >> 7
            tile = jnp.zeros((8, LANES), jnp.float32)
            for group in range(groups):
                for chunk in range(chunks):
                    columns = pl.ds(band * band_width + chunk * LANES, LANES)
                    values = spec_ref[pl.ds(group * 8 + pair * 2, 2), :, columns]
                    values = values.astype(jnp.float32).reshape(8, LANES)
                    moved = jnp.take_along_axis(values, lane_id, axis=1, mode="promise_in_bounds")
                    tile = jnp.where(chosen == group * chunks + chunk, moved, tile)
            turn_ref[band, pl.ds(pair * 8, 8), :] = tile

    def turn(band):
        parts = [turn_ref[band, pl.ds(part, 8, stride=4), :] for part in range(4)]
        tiles = []
        for group in range(groups):
            tile = jnp.zeros((8, LANES), jnp.float32)
            for part in range(4):
                amount = (part - group) * width % LANES
                turned = pltpu.roll(parts[part], amount, 1) if amount else parts[part]
                tile = jnp.where(lane_group == part, turned, tile)
            tiles.append(tile)
        return tiles

    tiles = {}
    for band in range(bands):
        gather(band)
        tiles[band] = turn(band)
    wanted = [tile for band in bands_out for tile in tiles[band]]
    for n in range(0, len(wanted), 2):
        out_ref[n * 8 : n * 8 + 16, :] = jnp.concatenate(wanted[n : n + 2], axis=0).astype(jnp.bfloat16)


def pick(offsets, spectra, bands_in, bands_out):
    rows, bands = spectra.shape[0], offsets.shape[0]
    out_rows = len(bands_out) * rows
    vmem = pl.BlockSpec(memory_space=pltpu.VMEM)
    return pl.pallas_call(
        functools.partial(pick_kernel, bands_in, bands_out),
        out_shape=jax.ShapeDtypeStruct((out_rows, LANES), jnp.bfloat16),
        in_specs=[vmem, vmem],
        out_specs=vmem,
        scratch_shapes=[
            pltpu.VMEM((bands, 4, 8, LANES), jnp.int32),
            pltpu.VMEM((bands, 32, LANES), jnp.float32),
        ],
        compiler_params=pltpu.CompilerParams(vmem_limit_bytes=8 * 1024 * 1024),
        cost_estimate=pl.CostEstimate(flops=10_000_000, bytes_accessed=2 * spectra.size, transcendentals=0),
        name="pick",
    )(offsets, spectra)


def split(values, count):
    parts = []
    for _ in range(count):
        part = values.astype(jnp.bfloat16)
        parts.append(part)
        values = values - part.astype(jnp.float32)
    return parts


def prepare_kernel(first, run, durations_ref, starts_ref, antenna_ref, fractions_ref, mask_ref, weigh_ref, coef_ref, kernel_ref):
    rows = starts_ref.shape[0]
    count = mask_ref.shape[0] // rows
    mine = lax.axis_index("tm").astype(jnp.int32) * count
    sfts = antenna_ref.shape[1]
    sft = iota((rows, sfts), 1)
    sft = jnp.where(sft // run == 0, sft + first * run, jnp.where(sft // run == first, sft - first * run, sft))
    start = starts_ref[:, 0:1]
    after = sft >= start
    for j in range(count):
        inside = after & (sft < start + durations_ref[mine + j])
        mask_ref[pl.ds(j * rows, rows), :] = jnp.where(inside, 1.0, 0.0).astype(jnp.bfloat16)
    antenna = jnp.concatenate([antenna_ref[...], jnp.zeros((4, sfts), jnp.float32)], axis=0)
    place = iota(antenna.shape, 1) // run
    after = pltpu.roll(antenna, sfts - first * run, 1)
    before = pltpu.roll(antenna, first * run, 1)
    antenna = jnp.where(place == 0, after, jnp.where(place == first, before, antenna))
    a1, a2, b1, b2 = (antenna[n : n + 1] for n in range(4))
    terms = jnp.concatenate([a1 * a1 + a2 * a2, b1 * b1 + b2 * b2, a1 * b1 + a2 * b2, jnp.zeros((5, sfts), jnp.float32)], axis=0)
    weights = sum(lax.dot_general(mask_ref[...], part, NT, preferred_element_type=jnp.float32) for part in split(terms, 3))
    wa, wb, wc = (weights[:, n : n + 1] for n in range(3))
    quarter = iota((rows * count, LANES), 1) // (LANES // 4)
    coef_ref[...] = jnp.where(quarter == 0, 1.0 / wa, jnp.where(quarter == 1, wa / (wa * wb - wc * wc), wc / wa))
    upright = jnp.transpose(jnp.concatenate([antenna, jnp.zeros((LANES - 8, sfts), jnp.float32)], axis=0))
    quarter = iota((sfts, LANES), 1) // (LANES // 4)
    early = jnp.where(quarter == 0, upright[:, 0:1], upright[:, 1:2])
    weigh_ref[...] = jnp.where(quarter < 2, early, jnp.where(quarter == 2, upright[:, 3:4], upright[:, 2:3]))
    fractions = fractions_ref[...]
    bin_id = iota((W, fractions.shape[1]), 0)
    distance = fractions + (W // 2 - 1) - bin_id.astype(jnp.float32)
    alternate = 1.0 - 2.0 * (bin_id % 2).astype(jnp.float32)
    kernel_ref[...] = (alternate * jnp.sin(jnp.pi * fractions) / (jnp.pi * distance)).astype(jnp.bfloat16)


def prepare(durations, starts, antenna, fractions, first, run, cores):
    count, rows, sfts = durations.shape[0] // cores, starts.shape[0], antenna.shape[0]
    vmem = pl.BlockSpec(memory_space=pltpu.VMEM)
    return pl.pallas_call(
        functools.partial(prepare_kernel, first, run),
        out_shape=(
            jax.ShapeDtypeStruct((count * rows, sfts), jnp.bfloat16),
            jax.ShapeDtypeStruct((sfts, LANES), jnp.float32),
            jax.ShapeDtypeStruct((count * rows, LANES), jnp.float32),
            jax.ShapeDtypeStruct((W, fractions.shape[0]), jnp.bfloat16),
        ),
        in_specs=[pl.BlockSpec(memory_space=pltpu.SMEM), vmem, vmem, vmem],
        out_specs=(vmem,) * 4,
        compiler_params=pltpu.CompilerParams(vmem_limit_bytes=16 * 1024 * 1024),
        cost_estimate=pl.CostEstimate(flops=100_000_000, bytes_accessed=4_000_000, transcendentals=0),
        name="prepare",
    )(durations, jnp.broadcast_to(starts[:, None], (rows, LANES)), antenna.T, fractions[None, :])


def statistic_kernel(windows_ref, mask_ref, weigh_ref, coef_ref, kernel_ref, map_ref, loudest_ref, block_ref, found_ref):
    templates = map_ref.shape[1]
    blocks = templates // LANES
    block_ref[...] = jnp.zeros_like(block_ref)
    for part in range(2):
        for c in range(4):
            for b in range(blocks):
                row, column = ((part * 4 + c) * blocks + b) * W, (c * blocks + b) * LANES
                block_ref[pl.ds(row, W), pl.ds(column, LANES)] = kernel_ref[:, b * LANES : (b + 1) * LANES]
    values = windows_ref[...].astype(jnp.float32)
    half, quarter = LANES // 2, LANES // 4
    weigh = weigh_ref[...]
    even = iota(weigh.shape, 1) // quarter % 2 == 0
    own = jnp.where(even, weigh, pltpu.roll(weigh, quarter, 1))
    other = jnp.where(even, pltpu.roll(weigh, LANES - quarter, 1), weigh)
    weighted = (own * values + other * pltpu.roll(values, half, 1)).astype(jnp.bfloat16)
    sums = jnp.dot(mask_ref[...], weighted, preferred_element_type=jnp.float32)
    sums = sums - jnp.where(iota(sums.shape, 1) < half, 0.0, coef_ref[...]) * pltpu.roll(sums, half, 1)
    parts = jnp.concatenate(split(sums, 2), axis=1)
    found_ref[...] = jnp.dot(parts, block_ref[...], preferred_element_type=jnp.float32)
    rows = map_ref.shape[0] // loudest_ref.shape[1]
    copies = loudest_ref.shape[0]
    per_step = LANES // rows
    for step in range(map_ref.shape[0] // LANES):
        here = pl.ds(step * LANES, LANES)
        scale_a = jnp.broadcast_to(coef_ref[here, 0:1], (LANES, LANES))
        scale_b = jnp.broadcast_to(coef_ref[here, quarter : quarter + 1], (LANES, LANES))
        best = None
        for b in range(blocks):
            ra, ia, rb, ib = (found_ref[here, pl.ds(c * templates + b * LANES, LANES)] for c in range(4))
            result = scale_a * (ra * ra + ia * ia) + scale_b * (rb * rb + ib * ib)
            map_ref[here, pl.ds(b * LANES, LANES)] = result
            best = result if best is None else jnp.maximum(best, result)
        best = jnp.max(jnp.transpose(best), axis=0, keepdims=True)
        for n in range(per_step):
            turned = best if n == 0 else pltpu.roll(best, LANES - n * rows, 1)
            for copy in range(copies):
                loudest_ref[copy, pl.ds(step * per_step + n, 1), :] = turned


def statistic(windows, mask, weigh, coef, kernel, rows, copies):
    count = mask.shape[0] // rows
    templates = kernel.shape[1]
    features = 4 * W * (templates // LANES)
    vmem = pl.BlockSpec(memory_space=pltpu.VMEM)
    return pl.pallas_call(
        statistic_kernel,
        out_shape=(
            jax.ShapeDtypeStruct((count * rows, templates), jnp.float32),
            jax.ShapeDtypeStruct((copies, count, LANES), jnp.float32),
        ),
        in_specs=[vmem] * 5,
        out_specs=(vmem, vmem),
        scratch_shapes=[
            pltpu.VMEM((2 * features, 4 * templates), jnp.bfloat16),
            pltpu.VMEM((count * rows, 4 * templates), jnp.float32),
        ],
        compiler_params=pltpu.CompilerParams(vmem_limit_bytes=16 * 1024 * 1024),
        cost_estimate=pl.CostEstimate(flops=400_000_000, bytes_accessed=4_000_000, transcendentals=0),
        name="statistic",
    )(windows, mask, weigh, coef, kernel)


def exchange(values, axis, members):
    return lax.all_to_all(values, axis, split_axis=0, concat_axis=0, axis_index_groups=[members], tiled=True)


def body(spectra, offsets, fractions, antenna, starts, durations):
    bands, cores = lax.axis_size("tmpl"), lax.axis_size("tm")
    sft_rows = spectra.shape[0]
    grid_size = starts.shape[0]
    my_rows = grid_size // cores
    by_band = order(bands, bands // 2)
    first = (cores - 1) * bands + bands // 2
    by_run = order(cores * bands, first)
    known = exchange(jnp.broadcast_to(offsets.T[None], (bands,) + offsets.T.shape), "tmpl", by_band)
    held, *late = lax.optimization_barrier((hold(spectra), durations, starts, antenna, fractions))
    prepared = prepare(*late, first, sft_rows, cores)
    held, *prepared = lax.optimization_barrier((held, *prepared))
    windows = pick(known, held, by_band, [run % bands for run in by_run])
    arrived = exchange(windows.reshape(cores * bands, sft_rows, LANES), ("tm", "tmpl"), by_run)
    fstat_map, loudest = statistic(arrived.reshape(-1, LANES), *prepared, grid_size, bands)
    loudest = jnp.max(exchange(loudest, "tmpl", by_band)[:, :, :grid_size], axis=0)
    return (fstat_map.reshape(my_rows, grid_size, -1), loudest)


def solution(mesh):
    in_specs = (
        P(("grp", "tm", "tmpl"), None, None),
        P(("grp", "tm"), "tmpl"),
        P(("grp", "tmpl")),
        P("grp", None),
        P("grp"),
        P("grp"),
    )
    out_specs = (P("tm", None, ("grp", "tmpl")), P(("grp", "tm"), None))
    return jax.shard_map(body, mesh=mesh, in_specs=in_specs, out_specs=out_specs, check_vma=False)
```

```python
import functools

import jax
import jax.numpy as jnp
from jax import lax
from jax.experimental import pallas as pl
from jax.experimental.pallas import tpu as pltpu
from jax.sharding import PartitionSpec as P

W = 16
LANES = 128
NT = (((1,), (1,)), ((), ()))


def iota(shape, axis):
    return lax.broadcasted_iota(jnp.int32, shape, axis)


def order(size, first):
    members = list(range(size))
    members[0], members[first] = first, 0
    return members


def hold_kernel(spec_ref, out_ref, sem):
    copy = pltpu.make_async_copy(spec_ref, out_ref, sem)
    copy.start()
    copy.wait()


def hold(spectra):
    return pl.pallas_call(
        hold_kernel,
        out_shape=jax.ShapeDtypeStruct(spectra.shape, spectra.dtype),
        in_specs=[pl.BlockSpec(memory_space=pl.ANY)],
        out_specs=pl.BlockSpec(memory_space=pltpu.VMEM),
        scratch_shapes=[pltpu.SemaphoreType.DMA],
        compiler_params=pltpu.CompilerParams(vmem_limit_bytes=8 * 1024 * 1024),
        cost_estimate=pl.CostEstimate(flops=0, bytes_accessed=4 * spectra.size, transcendentals=0),
        name="hold",
    )(spectra)


def pick_kernel(bands_in, bands_out, offset_ref, spec_ref, out_ref, place_ref, turn_ref):
    rows, _, bins = spec_ref.shape
    bands, blocks, _ = offset_ref.shape
    band_width = bins // bands
    groups = rows // 8
    chunks = band_width // LANES
    width = blocks * W
    first = lax.axis_index("tmpl").astype(jnp.int32) * rows
    columns = pl.ds(pl.multiple_of(first // LANES * LANES, LANES), LANES)
    offsets = jnp.concatenate([offset_ref[bands_in.index(band), :, columns] for band in range(bands)], axis=0).astype(jnp.float32)
    lane = iota(offsets.shape, 1)
    offsets = jnp.take_along_axis(offsets, (lane >> 2) + first & (LANES - 1), axis=1, mode="promise_in_bounds")
    offsets = jnp.concatenate([offsets, jnp.zeros((LANES - bands * blocks, LANES), jnp.float32)], axis=0)
    upright = jnp.transpose(offsets).astype(jnp.int32)
    lane = iota((32, LANES), 1)
    places = upright[0:32]
    for group in range(1, groups):
        turned = pltpu.roll(upright[group * 32 : group * 32 + 32], group * bands * blocks, 1)
        places = jnp.where(lane < group * bands * blocks, places, turned)
    lane = iota((8, LANES), 1)
    lane_group = lane // width
    source = lane_group * (bands * blocks) + lane // W % blocks
    for band in range(bands):
        for pair in range(4):
            place = jnp.take_along_axis(places[pair * 8 : pair * 8 + 8], source + band * blocks, axis=1, mode="promise_in_bounds")
            place_ref[band, pair] = place + ((lane & (W - 1)) + lane_group * band_width)

    def gather(band):
        for pair in range(4):
            place = place_ref[band, pair]
            lane_id = place & (LANES - 1)
            chosen = place >> 7
            tile = jnp.zeros((8, LANES), jnp.float32)
            for group in range(groups):
                for chunk in range(chunks):
                    columns = pl.ds(band * band_width + chunk * LANES, LANES)
                    values = spec_ref[pl.ds(group * 8 + pair * 2, 2), :, columns]
                    values = values.astype(jnp.float32).reshape(8, LANES)
                    moved = jnp.take_along_axis(values, lane_id, axis=1, mode="promise_in_bounds")
                    tile = jnp.where(chosen == group * chunks + chunk, moved, tile)
            turn_ref[band, pl.ds(pair * 8, 8), :] = tile

    def turn(band):
        parts = [turn_ref[band, pl.ds(part, 8, stride=4), :] for part in range(4)]
        tiles = []
        for group in range(groups):
            tile = jnp.zeros((8, LANES), jnp.float32)
            for part in range(4):
                amount = (part - group) * width % LANES
                turned = pltpu.roll(parts[part], amount, 1) if amount else parts[part]
                tile = jnp.where(lane_group == part, turned, tile)
            tiles.append(tile)
        return tiles

    tiles = {}
    for band in range(bands):
        gather(band)
        tiles[band] = turn(band)
    wanted = [tile for band in bands_out for tile in tiles[band]]
    for n in range(0, len(wanted), 2):
        out_ref[n * 8 : n * 8 + 16, :] = jnp.concatenate(wanted[n : n + 2], axis=0).astype(jnp.bfloat16)


def pick(offsets, spectra, bands_in, bands_out):
    rows, bands = spectra.shape[0], offsets.shape[0]
    out_rows = len(bands_out) * rows
    vmem = pl.BlockSpec(memory_space=pltpu.VMEM)
    return pl.pallas_call(
        functools.partial(pick_kernel, bands_in, bands_out),
        out_shape=jax.ShapeDtypeStruct((out_rows, LANES), jnp.bfloat16),
        in_specs=[vmem, vmem],
        out_specs=vmem,
        scratch_shapes=[
            pltpu.VMEM((bands, 4, 8, LANES), jnp.int32),
            pltpu.VMEM((bands, 32, LANES), jnp.float32),
        ],
        compiler_params=pltpu.CompilerParams(vmem_limit_bytes=8 * 1024 * 1024),
        cost_estimate=pl.CostEstimate(flops=10_000_000, bytes_accessed=2 * spectra.size, transcendentals=0),
        name="pick",
    )(offsets, spectra)


def split(values, count):
    parts = []
    for _ in range(count):
        part = values.astype(jnp.bfloat16)
        parts.append(part)
        values = values - part.astype(jnp.float32)
    return parts


def prepare_kernel(first, run, durations_ref, starts_ref, antenna_ref, fractions_ref, mask_ref, weigh_ref, coef_ref, kernel_ref):
    rows = starts_ref.shape[0]
    count = mask_ref.shape[0] // rows
    mine = lax.axis_index("tm").astype(jnp.int32) * count
    sfts = antenna_ref.shape[1]
    sft = iota((rows, sfts), 1)
    sft = jnp.where(sft // run == 0, sft + first * run, jnp.where(sft // run == first, sft - first * run, sft))
    start = starts_ref[:, 0:1]
    after = sft >= start
    for j in range(count):
        inside = after & (sft < start + durations_ref[mine + j])
        mask_ref[pl.ds(j * rows, rows), :] = jnp.where(inside, 1.0, 0.0).astype(jnp.bfloat16)
    antenna = jnp.concatenate([antenna_ref[...], jnp.zeros((4, sfts), jnp.float32)], axis=0)
    place = iota(antenna.shape, 1) // run
    after = pltpu.roll(antenna, sfts - first * run, 1)
    before = pltpu.roll(antenna, first * run, 1)
    antenna = jnp.where(place == 0, after, jnp.where(place == first, before, antenna))
    a1, a2, b1, b2 = (antenna[n : n + 1] for n in range(4))
    terms = jnp.concatenate([a1 * a1 + a2 * a2, b1 * b1 + b2 * b2, a1 * b1 + a2 * b2, jnp.zeros((5, sfts), jnp.float32)], axis=0)
    parts = jnp.concatenate(split(terms, 3) + [jnp.zeros((LANES - 24, sfts), jnp.bfloat16)], axis=0)
    weights = lax.dot_general(mask_ref[...], parts, NT, preferred_element_type=jnp.float32)
    weights = weights + pltpu.roll(weights, LANES - 8, 1) + pltpu.roll(weights, LANES - 16, 1)
    wa, wb, wc = (weights[:, n : n + 1] for n in range(3))
    quarter = iota((rows * count, LANES), 1) // (LANES // 4)
    coef_ref[...] = jnp.where(quarter == 0, 1.0 / wa, jnp.where(quarter == 1, wa / (wa * wb - wc * wc), wc / wa))
    upright = jnp.transpose(jnp.concatenate([antenna, jnp.zeros((LANES - 8, sfts), jnp.float32)], axis=0))
    quarter = iota((sfts, LANES), 1) // (LANES // 4)
    early = jnp.where(quarter == 0, upright[:, 0:1], upright[:, 1:2])
    weigh_ref[...] = jnp.where(quarter < 2, early, jnp.where(quarter == 2, upright[:, 3:4], upright[:, 2:3]))
    fractions = fractions_ref[...]
    bin_id = iota((W, fractions.shape[1]), 0)
    distance = fractions + (W // 2 - 1) - bin_id.astype(jnp.float32)
    alternate = 1.0 - 2.0 * (bin_id % 2).astype(jnp.float32)
    kernel_ref[...] = (alternate * jnp.sin(jnp.pi * fractions) / (jnp.pi * distance)).astype(jnp.bfloat16)


def prepare(durations, starts, antenna, fractions, first, run, cores):
    count, rows, sfts = durations.shape[0] // cores, starts.shape[0], antenna.shape[0]
    vmem = pl.BlockSpec(memory_space=pltpu.VMEM)
    return pl.pallas_call(
        functools.partial(prepare_kernel, first, run),
        out_shape=(
            jax.ShapeDtypeStruct((count * rows, sfts), jnp.bfloat16),
            jax.ShapeDtypeStruct((sfts, LANES), jnp.float32),
            jax.ShapeDtypeStruct((count * rows, LANES), jnp.float32),
            jax.ShapeDtypeStruct((W, fractions.shape[0]), jnp.bfloat16),
        ),
        in_specs=[pl.BlockSpec(memory_space=pltpu.SMEM), vmem, vmem, vmem],
        out_specs=(vmem,) * 4,
        compiler_params=pltpu.CompilerParams(vmem_limit_bytes=16 * 1024 * 1024),
        cost_estimate=pl.CostEstimate(flops=100_000_000, bytes_accessed=4_000_000, transcendentals=0),
        name="prepare",
    )(durations, jnp.broadcast_to(starts[:, None], (rows, LANES)), antenna.T, fractions[None, :])


def statistic_kernel(windows_ref, mask_ref, weigh_ref, coef_ref, kernel_ref, map_ref, loudest_ref, block_ref, found_ref):
    templates = map_ref.shape[1]
    blocks = templates // LANES
    block_ref[...] = jnp.zeros_like(block_ref)
    for part in range(2):
        for c in range(4):
            for b in range(blocks):
                row, column = ((part * 4 + c) * blocks + b) * W, (c * blocks + b) * LANES
                block_ref[pl.ds(row, W), pl.ds(column, LANES)] = kernel_ref[:, b * LANES : (b + 1) * LANES]
    values = windows_ref[...].astype(jnp.float32)
    half, quarter = LANES // 2, LANES // 4
    weigh = weigh_ref[...]
    even = iota(weigh.shape, 1) // quarter % 2 == 0
    own = jnp.where(even, weigh, pltpu.roll(weigh, quarter, 1))
    other = jnp.where(even, pltpu.roll(weigh, LANES - quarter, 1), weigh)
    weighted = (own * values + other * pltpu.roll(values, half, 1)).astype(jnp.bfloat16)
    sums = jnp.dot(mask_ref[...], weighted, preferred_element_type=jnp.float32)
    sums = sums - jnp.where(iota(sums.shape, 1) < half, 0.0, coef_ref[...]) * pltpu.roll(sums, half, 1)
    parts = jnp.concatenate(split(sums, 2), axis=1)
    found_ref[...] = jnp.dot(parts, block_ref[...], preferred_element_type=jnp.float32)
    rows = map_ref.shape[0] // loudest_ref.shape[1]
    copies = loudest_ref.shape[0]
    per_step = LANES // rows
    for step in range(map_ref.shape[0] // LANES):
        here = pl.ds(step * LANES, LANES)
        scale_a = jnp.broadcast_to(coef_ref[here, 0:1], (LANES, LANES))
        scale_b = jnp.broadcast_to(coef_ref[here, quarter : quarter + 1], (LANES, LANES))
        best = None
        for b in range(blocks):
            ra, ia, rb, ib = (found_ref[here, pl.ds(c * templates + b * LANES, LANES)] for c in range(4))
            result = scale_a * (ra * ra + ia * ia) + scale_b * (rb * rb + ib * ib)
            map_ref[here, pl.ds(b * LANES, LANES)] = result
            best = result if best is None else jnp.maximum(best, result)
        best = jnp.max(jnp.transpose(best), axis=0, keepdims=True)
        for n in range(per_step):
            turned = best if n == 0 else pltpu.roll(best, LANES - n * rows, 1)
            for copy in range(copies):
                loudest_ref[copy, pl.ds(step * per_step + n, 1), :] = turned


def statistic(windows, mask, weigh, coef, kernel, rows, copies):
    count = mask.shape[0] // rows
    templates = kernel.shape[1]
    features = 4 * W * (templates // LANES)
    vmem = pl.BlockSpec(memory_space=pltpu.VMEM)
    return pl.pallas_call(
        statistic_kernel,
        out_shape=(
            jax.ShapeDtypeStruct((count * rows, templates), jnp.float32),
            jax.ShapeDtypeStruct((copies, count, LANES), jnp.float32),
        ),
        in_specs=[vmem] * 5,
        out_specs=(vmem, vmem),
        scratch_shapes=[
            pltpu.VMEM((2 * features, 4 * templates), jnp.bfloat16),
            pltpu.VMEM((count * rows, 4 * templates), jnp.float32),
        ],
        compiler_params=pltpu.CompilerParams(vmem_limit_bytes=16 * 1024 * 1024),
        cost_estimate=pl.CostEstimate(flops=400_000_000, bytes_accessed=4_000_000, transcendentals=0),
        name="statistic",
    )(windows, mask, weigh, coef, kernel)


def exchange(values, axis, members):
    return lax.all_to_all(values, axis, split_axis=0, concat_axis=0, axis_index_groups=[members], tiled=True)


def body(spectra, offsets, fractions, antenna, starts, durations):
    bands, cores = lax.axis_size("tmpl"), lax.axis_size("tm")
    sft_rows = spectra.shape[0]
    grid_size = starts.shape[0]
    my_rows = grid_size // cores
    by_band = order(bands, bands // 2)
    first = (cores - 1) * bands + bands // 2
    by_run = order(cores * bands, first)
    known = exchange(jnp.broadcast_to(offsets.T[None], (bands,) + offsets.T.shape), "tmpl", by_band)
    held, *late = lax.optimization_barrier((hold(spectra), durations, starts, antenna, fractions))
    prepared = prepare(*late, first, sft_rows, cores)
    held, *prepared = lax.optimization_barrier((held, *prepared))
    windows = pick(known, held, by_band, [run % bands for run in by_run])
    arrived = exchange(windows.reshape(cores * bands, sft_rows, LANES), ("tm", "tmpl"), by_run)
    fstat_map, loudest = statistic(arrived.reshape(-1, LANES), *prepared, grid_size, bands)
    loudest = jnp.max(exchange(loudest, "tmpl", by_band)[:, :, :grid_size], axis=0)
    return (fstat_map.reshape(my_rows, grid_size, -1), loudest)


def solution(mesh):
    in_specs = (
        P(("grp", "tm", "tmpl"), None, None),
        P(("grp", "tm"), "tmpl"),
        P(("grp", "tmpl")),
        P("grp", None),
        P("grp"),
        P("grp"),
    )
    out_specs = (P("tm", None, ("grp", "tmpl")), P(("grp", "tm"), None))
    return jax.shard_map(body, mesh=mesh, in_specs=in_specs, out_specs=out_specs, check_vma=False)
```

```python
import functools

import jax
import jax.numpy as jnp
from jax import lax
from jax.experimental import pallas as pl
from jax.experimental.pallas import tpu as pltpu
from jax.sharding import PartitionSpec as P

W = 16
LANES = 128
NT = (((1,), (1,)), ((), ()))


def iota(shape, axis):
    return lax.broadcasted_iota(jnp.int32, shape, axis)


def order(size, first):
    members = list(range(size))
    members[0], members[first] = first, 0
    return members


def hold_kernel(spec_ref, out_ref, sem):
    copy = pltpu.make_async_copy(spec_ref, out_ref, sem)
    copy.start()
    copy.wait()


def hold(spectra):
    return pl.pallas_call(
        hold_kernel,
        out_shape=jax.ShapeDtypeStruct(spectra.shape, spectra.dtype),
        in_specs=[pl.BlockSpec(memory_space=pl.ANY)],
        out_specs=pl.BlockSpec(memory_space=pltpu.VMEM),
        scratch_shapes=[pltpu.SemaphoreType.DMA],
        compiler_params=pltpu.CompilerParams(vmem_limit_bytes=8 * 1024 * 1024),
        cost_estimate=pl.CostEstimate(flops=0, bytes_accessed=4 * spectra.size, transcendentals=0),
        name="hold",
    )(spectra)


def pick_kernel(bands_in, bands_out, offset_ref, spec_ref, out_ref, place_ref, turn_ref):
    rows, _, bins = spec_ref.shape
    bands, blocks, _ = offset_ref.shape
    band_width = bins // bands
    groups = rows // 8
    chunks = band_width // LANES
    width = blocks * W
    first = lax.axis_index("tmpl").astype(jnp.int32) * rows
    columns = pl.ds(pl.multiple_of(first // LANES * LANES, LANES), LANES)
    offsets = jnp.concatenate([offset_ref[bands_in.index(band), :, columns] for band in range(bands)], axis=0).astype(jnp.float32)
    lane = iota(offsets.shape, 1)
    offsets = jnp.take_along_axis(offsets, (lane >> 2) + first & (LANES - 1), axis=1, mode="promise_in_bounds")
    offsets = jnp.concatenate([offsets, jnp.zeros((LANES - bands * blocks, LANES), jnp.float32)], axis=0)
    upright = jnp.transpose(offsets).astype(jnp.int32)
    lane = iota((32, LANES), 1)
    places = upright[0:32]
    for group in range(1, groups):
        turned = pltpu.roll(upright[group * 32 : group * 32 + 32], group * bands * blocks, 1)
        places = jnp.where(lane < group * bands * blocks, places, turned)
    lane = iota((8, LANES), 1)
    lane_group = lane // width
    source = lane_group * (bands * blocks) + lane // W % blocks
    for band in range(bands):
        for pair in range(4):
            place = jnp.take_along_axis(places[pair * 8 : pair * 8 + 8], source + band * blocks, axis=1, mode="promise_in_bounds")
            place_ref[band, pair] = place + ((lane & (W - 1)) + lane_group * band_width)

    def gather(band):
        for pair in range(4):
            place = place_ref[band, pair]
            lane_id = place & (LANES - 1)
            chosen = place >> 7
            tile = jnp.zeros((8, LANES), jnp.float32)
            for group in range(groups):
                for chunk in range(chunks):
                    columns = pl.ds(band * band_width + chunk * LANES, LANES)
                    values = spec_ref[pl.ds(group * 8 + pair * 2, 2), :, columns]
                    values = values.astype(jnp.float32).reshape(8, LANES)
                    moved = jnp.take_along_axis(values, lane_id, axis=1, mode="promise_in_bounds")
                    tile = jnp.where(chosen == group * chunks + chunk, moved, tile)
            turn_ref[band, pl.ds(pair * 8, 8), :] = tile

    def turn(band):
        parts = [turn_ref[band, pl.ds(part, 8, stride=4), :] for part in range(4)]
        tiles = []
        for group in range(groups):
            tile = jnp.zeros((8, LANES), jnp.float32)
            for part in range(4):
                amount = (part - group) * width % LANES
                turned = pltpu.roll(parts[part], amount, 1) if amount else parts[part]
                tile = jnp.where(lane_group == part, turned, tile)
            tiles.append(tile)
        return tiles

    tiles = {}
    for band in range(bands):
        gather(band)
        tiles[band] = turn(band)
    wanted = [tile for band in bands_out for tile in tiles[band]]
    for n in range(0, len(wanted), 2):
        out_ref[n * 8 : n * 8 + 16, :] = jnp.concatenate(wanted[n : n + 2], axis=0).astype(jnp.bfloat16)


def pick(offsets, spectra, bands_in, bands_out):
    rows, bands = spectra.shape[0], offsets.shape[0]
    out_rows = len(bands_out) * rows
    vmem = pl.BlockSpec(memory_space=pltpu.VMEM)
    return pl.pallas_call(
        functools.partial(pick_kernel, bands_in, bands_out),
        out_shape=jax.ShapeDtypeStruct((out_rows, LANES), jnp.bfloat16),
        in_specs=[vmem, vmem],
        out_specs=vmem,
        scratch_shapes=[
            pltpu.VMEM((bands, 4, 8, LANES), jnp.int32),
            pltpu.VMEM((bands, 32, LANES), jnp.float32),
        ],
        compiler_params=pltpu.CompilerParams(vmem_limit_bytes=8 * 1024 * 1024),
        cost_estimate=pl.CostEstimate(flops=10_000_000, bytes_accessed=2 * spectra.size, transcendentals=0),
        name="pick",
    )(offsets, spectra)


def split(values, count):
    parts = []
    for _ in range(count):
        part = values.astype(jnp.bfloat16)
        parts.append(part)
        values = values - part.astype(jnp.float32)
    return parts


def prepare_kernel(first, run, durations_ref, starts_ref, antenna_ref, fractions_ref, mask_ref, weigh_ref, coef_ref, kernel_ref):
    rows = starts_ref.shape[0]
    count = mask_ref.shape[0] // rows
    mine = lax.axis_index("tm").astype(jnp.int32) * count
    sfts = antenna_ref.shape[1]
    sft = iota((rows, sfts), 1)
    sft = jnp.where(sft // run == 0, sft + first * run, jnp.where(sft // run == first, sft - first * run, sft))
    start = starts_ref[:, 0:1]
    after = sft >= start
    for j in range(count):
        inside = after & (sft < start + durations_ref[mine + j])
        mask_ref[pl.ds(j * rows, rows), :] = jnp.where(inside, 1.0, 0.0).astype(jnp.bfloat16)
    antenna = jnp.concatenate([antenna_ref[...], jnp.zeros((4, sfts), jnp.float32)], axis=0)
    place = iota(antenna.shape, 1) // run
    after = pltpu.roll(antenna, sfts - first * run, 1)
    before = pltpu.roll(antenna, first * run, 1)
    antenna = jnp.where(place == 0, after, jnp.where(place == first, before, antenna))
    a1, a2, b1, b2 = (antenna[n : n + 1] for n in range(4))
    terms = jnp.concatenate([a1 * a1 + a2 * a2, b1 * b1 + b2 * b2, a1 * b1 + a2 * b2, jnp.zeros((5, sfts), jnp.float32)], axis=0)
    sums = lax.dot_general(jnp.concatenate(split(terms, 3), axis=0), mask_ref[...], NT, preferred_element_type=jnp.float32)
    sums = sums[0:8] + sums[8:16] + sums[16:24]
    wa, wb, wc = (sums[n : n + 1] for n in range(3))

    def quarters(*factors):
        shape = (LANES // 4, factors[0].shape[1])
        return jnp.transpose(jnp.concatenate([jnp.broadcast_to(factor, shape) for factor in factors], axis=0))

    coef_ref[...] = quarters(1.0 / wa, wa / (wa * wb - wc * wc), wc / wa, wc / wa)
    weigh_ref[...] = quarters(a1, a2, b2, b1)
    fractions = fractions_ref[...]
    bin_id = iota((W, fractions.shape[1]), 0)
    distance = fractions + (W // 2 - 1) - bin_id.astype(jnp.float32)
    alternate = 1.0 - 2.0 * (bin_id % 2).astype(jnp.float32)
    kernel_ref[...] = (alternate * jnp.sin(jnp.pi * fractions) / (jnp.pi * distance)).astype(jnp.bfloat16)


def prepare(durations, starts, antenna, fractions, first, run, cores):
    count, rows, sfts = durations.shape[0] // cores, starts.shape[0], antenna.shape[0]
    vmem = pl.BlockSpec(memory_space=pltpu.VMEM)
    return pl.pallas_call(
        functools.partial(prepare_kernel, first, run),
        out_shape=(
            jax.ShapeDtypeStruct((count * rows, sfts), jnp.bfloat16),
            jax.ShapeDtypeStruct((sfts, LANES), jnp.float32),
            jax.ShapeDtypeStruct((count * rows, LANES), jnp.float32),
            jax.ShapeDtypeStruct((W, fractions.shape[0]), jnp.bfloat16),
        ),
        in_specs=[pl.BlockSpec(memory_space=pltpu.SMEM), vmem, vmem, vmem],
        out_specs=(vmem,) * 4,
        compiler_params=pltpu.CompilerParams(vmem_limit_bytes=16 * 1024 * 1024),
        cost_estimate=pl.CostEstimate(flops=100_000_000, bytes_accessed=4_000_000, transcendentals=0),
        name="prepare",
    )(durations, jnp.broadcast_to(starts[:, None], (rows, LANES)), antenna.T, fractions[None, :])


def statistic_kernel(windows_ref, mask_ref, weigh_ref, coef_ref, kernel_ref, map_ref, loudest_ref, block_ref, found_ref):
    templates = map_ref.shape[1]
    blocks = templates // LANES
    block_ref[...] = jnp.zeros_like(block_ref)
    for part in range(2):
        for c in range(4):
            for b in range(blocks):
                row, column = ((part * 4 + c) * blocks + b) * W, (c * blocks + b) * LANES
                block_ref[pl.ds(row, W), pl.ds(column, LANES)] = kernel_ref[:, b * LANES : (b + 1) * LANES]
    values = windows_ref[...].astype(jnp.float32)
    half, quarter = LANES // 2, LANES // 4
    weigh = weigh_ref[...]
    even = iota(weigh.shape, 1) // quarter % 2 == 0
    own = jnp.where(even, weigh, pltpu.roll(weigh, quarter, 1))
    other = jnp.where(even, pltpu.roll(weigh, LANES - quarter, 1), weigh)
    weighted = (own * values + other * pltpu.roll(values, half, 1)).astype(jnp.bfloat16)
    sums = jnp.dot(mask_ref[...], weighted, preferred_element_type=jnp.float32)
    sums = sums - jnp.where(iota(sums.shape, 1) < half, 0.0, coef_ref[...]) * pltpu.roll(sums, half, 1)
    parts = jnp.concatenate(split(sums, 2), axis=1)
    found_ref[...] = jnp.dot(parts, block_ref[...], preferred_element_type=jnp.float32)
    rows = map_ref.shape[0] // loudest_ref.shape[1]
    copies = loudest_ref.shape[0]
    per_step = LANES // rows
    for step in range(map_ref.shape[0] // LANES):
        here = pl.ds(step * LANES, LANES)
        scale_a = jnp.broadcast_to(coef_ref[here, 0:1], (LANES, LANES))
        scale_b = jnp.broadcast_to(coef_ref[here, quarter : quarter + 1], (LANES, LANES))
        best = None
        for b in range(blocks):
            ra, ia, rb, ib = (found_ref[here, pl.ds(c * templates + b * LANES, LANES)] for c in range(4))
            result = scale_a * (ra * ra + ia * ia) + scale_b * (rb * rb + ib * ib)
            map_ref[here, pl.ds(b * LANES, LANES)] = result
            best = result if best is None else jnp.maximum(best, result)
        best = jnp.max(jnp.transpose(best), axis=0, keepdims=True)
        for n in range(per_step):
            turned = best if n == 0 else pltpu.roll(best, LANES - n * rows, 1)
            for copy in range(copies):
                loudest_ref[copy, pl.ds(step * per_step + n, 1), :] = turned


def statistic(windows, mask, weigh, coef, kernel, rows, copies):
    count = mask.shape[0] // rows
    templates = kernel.shape[1]
    features = 4 * W * (templates // LANES)
    vmem = pl.BlockSpec(memory_space=pltpu.VMEM)
    return pl.pallas_call(
        statistic_kernel,
        out_shape=(
            jax.ShapeDtypeStruct((count * rows, templates), jnp.float32),
            jax.ShapeDtypeStruct((copies, count, LANES), jnp.float32),
        ),
        in_specs=[vmem] * 5,
        out_specs=(vmem, vmem),
        scratch_shapes=[
            pltpu.VMEM((2 * features, 4 * templates), jnp.bfloat16),
            pltpu.VMEM((count * rows, 4 * templates), jnp.float32),
        ],
        compiler_params=pltpu.CompilerParams(vmem_limit_bytes=16 * 1024 * 1024),
        cost_estimate=pl.CostEstimate(flops=400_000_000, bytes_accessed=4_000_000, transcendentals=0),
        name="statistic",
    )(windows, mask, weigh, coef, kernel)


def exchange(values, axis, members):
    return lax.all_to_all(values, axis, split_axis=0, concat_axis=0, axis_index_groups=[members], tiled=True)


def body(spectra, offsets, fractions, antenna, starts, durations):
    bands, cores = lax.axis_size("tmpl"), lax.axis_size("tm")
    sft_rows = spectra.shape[0]
    grid_size = starts.shape[0]
    my_rows = grid_size // cores
    by_band = order(bands, bands // 2)
    first = (cores - 1) * bands + bands // 2
    by_run = order(cores * bands, first)
    known = exchange(jnp.broadcast_to(offsets.T[None], (bands,) + offsets.T.shape), "tmpl", by_band)
    held, *late = lax.optimization_barrier((hold(spectra), durations, starts, antenna, fractions))
    prepared = prepare(*late, first, sft_rows, cores)
    held, *prepared = lax.optimization_barrier((held, *prepared))
    windows = pick(known, held, by_band, [run % bands for run in by_run])
    arrived = exchange(windows.reshape(cores * bands, sft_rows, LANES), ("tm", "tmpl"), by_run)
    fstat_map, loudest = statistic(arrived.reshape(-1, LANES), *prepared, grid_size, bands)
    loudest = jnp.max(exchange(loudest, "tmpl", by_band)[:, :, :grid_size], axis=0)
    return (fstat_map.reshape(my_rows, grid_size, -1), loudest)


def solution(mesh):
    in_specs = (
        P(("grp", "tm", "tmpl"), None, None),
        P(("grp", "tm"), "tmpl"),
        P(("grp", "tmpl")),
        P("grp", None),
        P("grp"),
        P("grp"),
    )
    out_specs = (P("tm", None, ("grp", "tmpl")), P(("grp", "tm"), None))
    return jax.shard_map(body, mesh=mesh, in_specs=in_specs, out_specs=out_specs, check_vma=False)
```

```python
import functools

import jax
import jax.numpy as jnp
from jax import lax
from jax.experimental import pallas as pl
from jax.experimental.pallas import tpu as pltpu
from jax.sharding import PartitionSpec as P

W = 16
LANES = 128
NT = (((1,), (1,)), ((), ()))


def iota(shape, axis):
    return lax.broadcasted_iota(jnp.int32, shape, axis)


def order(size, first):
    members = list(range(size))
    members[0], members[first] = first, 0
    return members


def hold_kernel(spec_ref, out_ref, sem):
    copy = pltpu.make_async_copy(spec_ref, out_ref, sem)
    copy.start()
    copy.wait()


def hold(spectra):
    return pl.pallas_call(
        hold_kernel,
        out_shape=jax.ShapeDtypeStruct(spectra.shape, spectra.dtype),
        in_specs=[pl.BlockSpec(memory_space=pl.ANY)],
        out_specs=pl.BlockSpec(memory_space=pltpu.VMEM),
        scratch_shapes=[pltpu.SemaphoreType.DMA],
        compiler_params=pltpu.CompilerParams(vmem_limit_bytes=8 * 1024 * 1024),
        cost_estimate=pl.CostEstimate(flops=0, bytes_accessed=4 * spectra.size, transcendentals=0),
        name="hold",
    )(spectra)


def pick_kernel(bands_in, bands_out, offset_ref, spec_ref, out_ref, place_ref, turn_ref):
    rows, _, bins = spec_ref.shape
    bands, blocks, _ = offset_ref.shape
    band_width = bins // bands
    groups = rows // 8
    chunks = band_width // LANES
    width = blocks * W
    first = lax.axis_index("tmpl").astype(jnp.int32) * rows
    columns = pl.ds(pl.multiple_of(first // LANES * LANES, LANES), LANES)
    offsets = jnp.concatenate([offset_ref[bands_in.index(band), :, columns] for band in range(bands)], axis=0).astype(jnp.float32)
    lane = iota(offsets.shape, 1)
    offsets = jnp.take_along_axis(offsets, (lane >> 2) + first & (LANES - 1), axis=1, mode="promise_in_bounds")
    offsets = jnp.concatenate([offsets, jnp.zeros((LANES - bands * blocks, LANES), jnp.float32)], axis=0)
    upright = jnp.transpose(offsets).astype(jnp.int32)
    lane = iota((32, LANES), 1)
    places = upright[0:32]
    for group in range(1, groups):
        turned = pltpu.roll(upright[group * 32 : group * 32 + 32], group * bands * blocks, 1)
        places = jnp.where(lane < group * bands * blocks, places, turned)
    lane = iota((8, LANES), 1)
    lane_group = lane // width
    source = lane_group * (bands * blocks) + lane // W % blocks
    for band in range(bands):
        for pair in range(4):
            place = jnp.take_along_axis(places[pair * 8 : pair * 8 + 8], source + band * blocks, axis=1, mode="promise_in_bounds")
            place_ref[band, pair] = place + ((lane & (W - 1)) + lane_group * band_width)

    def gather(band):
        for pair in range(4):
            place = place_ref[band, pair]
            lane_id = place & (LANES - 1)
            chosen = place >> 7
            tile = jnp.zeros((8, LANES), jnp.float32)
            for group in range(groups):
                for chunk in range(chunks):
                    columns = pl.ds(band * band_width + chunk * LANES, LANES)
                    values = spec_ref[pl.ds(group * 8 + pair * 2, 2), :, columns]
                    values = values.astype(jnp.float32).reshape(8, LANES)
                    moved = jnp.take_along_axis(values, lane_id, axis=1, mode="promise_in_bounds")
                    tile = jnp.where(chosen == group * chunks + chunk, moved, tile)
            turn_ref[band, pl.ds(pair * 8, 8), :] = tile

    def turn(band):
        parts = [turn_ref[band, pl.ds(part, 8, stride=4), :] for part in range(4)]
        tiles = []
        for group in range(groups):
            tile = jnp.zeros((8, LANES), jnp.float32)
            for part in range(4):
                amount = (part - group) * width % LANES
                turned = pltpu.roll(parts[part], amount, 1) if amount else parts[part]
                tile = jnp.where(lane_group == part, turned, tile)
            tiles.append(tile)
        return tiles

    tiles = {}
    for band in range(bands):
        gather(band)
        tiles[band] = turn(band)
    wanted = [tile for band in bands_out for tile in tiles[band]]
    for n in range(0, len(wanted), 2):
        out_ref[n * 8 : n * 8 + 16, :] = jnp.concatenate(wanted[n : n + 2], axis=0).astype(jnp.bfloat16)


def pick(offsets, spectra, bands_in, bands_out):
    rows, bands = spectra.shape[0], offsets.shape[0]
    out_rows = len(bands_out) * rows
    vmem = pl.BlockSpec(memory_space=pltpu.VMEM)
    return pl.pallas_call(
        functools.partial(pick_kernel, bands_in, bands_out),
        out_shape=jax.ShapeDtypeStruct((out_rows, LANES), jnp.bfloat16),
        in_specs=[vmem, vmem],
        out_specs=vmem,
        scratch_shapes=[
            pltpu.VMEM((bands, 4, 8, LANES), jnp.int32),
            pltpu.VMEM((bands, 32, LANES), jnp.float32),
        ],
        compiler_params=pltpu.CompilerParams(vmem_limit_bytes=8 * 1024 * 1024),
        cost_estimate=pl.CostEstimate(flops=10_000_000, bytes_accessed=2 * spectra.size, transcendentals=0),
        name="pick",
    )(offsets, spectra)


def split(values, count):
    parts = []
    for _ in range(count):
        part = values.astype(jnp.bfloat16)
        parts.append(part)
        values = values - part.astype(jnp.float32)
    return parts


def prepare_kernel(first, run, durations_ref, starts_ref, antenna_ref, fractions_ref, mask_ref, weigh_ref, coef_ref, kernel_ref):
    rows = starts_ref.shape[0]
    count = mask_ref.shape[0] // rows
    mine = lax.axis_index("tm").astype(jnp.int32) * count
    sfts = antenna_ref.shape[1]
    sft = iota((rows, sfts), 1)
    sft = jnp.where(sft // run == 0, sft + first * run, jnp.where(sft // run == first, sft - first * run, sft))
    start = starts_ref[:, 0:1]
    after = sft >= start
    for j in range(count):
        inside = after & (sft < start + durations_ref[mine + j])
        mask_ref[pl.ds(j * rows, rows), :] = jnp.where(inside, 1.0, 0.0).astype(jnp.bfloat16)
    antenna = jnp.concatenate([antenna_ref[...], jnp.zeros((4, sfts), jnp.float32)], axis=0)
    place = iota(antenna.shape, 1) // run
    after = pltpu.roll(antenna, sfts - first * run, 1)
    before = pltpu.roll(antenna, first * run, 1)
    antenna = jnp.where(place == 0, after, jnp.where(place == first, before, antenna))
    a1, a2, b1, b2 = (antenna[n : n + 1] for n in range(4))
    terms = jnp.concatenate([a1 * a1 + a2 * a2, b1 * b1 + b2 * b2, a1 * b1 + a2 * b2, jnp.zeros((5, sfts), jnp.float32)], axis=0)
    sums = lax.dot_general(jnp.concatenate(split(terms, 3), axis=0), mask_ref[...], NT, preferred_element_type=jnp.float32)
    sums = sums[0:8] + sums[8:16] + sums[16:24]
    wa, wb, wc = (sums[n : n + 1] for n in range(3))

    def quarters(*factors):
        shape = (LANES // 4, factors[0].shape[1])
        return jnp.transpose(jnp.concatenate([jnp.broadcast_to(factor, shape) for factor in factors], axis=0))

    coef_ref[...] = quarters(1.0 / wa, wa / (wa * wb - wc * wc), wc / wa, wc / wa)
    weigh_ref[...] = quarters(a1, a2, b2, b1)
    fractions = fractions_ref[...]
    bin_id = iota((W, fractions.shape[1]), 0)
    distance = fractions + (W // 2 - 1) - bin_id.astype(jnp.float32)
    alternate = 1.0 - 2.0 * (bin_id % 2).astype(jnp.float32)
    kernel_ref[...] = (alternate * jnp.sin(jnp.pi * fractions) / (jnp.pi * distance)).astype(jnp.bfloat16)


def prepare(durations, starts, antenna, fractions, first, run, cores):
    count, rows, sfts = durations.shape[0] // cores, starts.shape[0], antenna.shape[0]
    vmem = pl.BlockSpec(memory_space=pltpu.VMEM)
    return pl.pallas_call(
        functools.partial(prepare_kernel, first, run),
        out_shape=(
            jax.ShapeDtypeStruct((count * rows, sfts), jnp.bfloat16),
            jax.ShapeDtypeStruct((sfts, LANES), jnp.float32),
            jax.ShapeDtypeStruct((count * rows, LANES), jnp.float32),
            jax.ShapeDtypeStruct((W, fractions.shape[0]), jnp.bfloat16),
        ),
        in_specs=[pl.BlockSpec(memory_space=pltpu.SMEM), vmem, vmem, vmem],
        out_specs=(vmem,) * 4,
        compiler_params=pltpu.CompilerParams(vmem_limit_bytes=16 * 1024 * 1024),
        cost_estimate=pl.CostEstimate(flops=100_000_000, bytes_accessed=4_000_000, transcendentals=0),
        name="prepare",
    )(durations, jnp.broadcast_to(starts[:, None], (rows, LANES)), antenna.T, fractions[None, :])


def statistic_kernel(windows_ref, mask_ref, weigh_ref, coef_ref, kernel_ref, map_ref, loudest_ref, block_ref, found_ref, tile_ref, sems):
    templates = map_ref.shape[1]
    blocks = templates // LANES
    block_ref[...] = jnp.zeros_like(block_ref)
    for part in range(2):
        for c in range(4):
            for b in range(blocks):
                row, column = ((part * 4 + c) * blocks + b) * W, (c * blocks + b) * LANES
                block_ref[pl.ds(row, W), pl.ds(column, LANES)] = kernel_ref[:, b * LANES : (b + 1) * LANES]
    values = windows_ref[...].astype(jnp.float32)
    half, quarter = LANES // 2, LANES // 4
    weigh = weigh_ref[...]
    even = iota(weigh.shape, 1) // quarter % 2 == 0
    own = jnp.where(even, weigh, pltpu.roll(weigh, quarter, 1))
    other = jnp.where(even, pltpu.roll(weigh, LANES - quarter, 1), weigh)
    weighted = (own * values + other * pltpu.roll(values, half, 1)).astype(jnp.bfloat16)
    sums = jnp.dot(mask_ref[...], weighted, preferred_element_type=jnp.float32)
    sums = sums - jnp.where(iota(sums.shape, 1) < half, 0.0, coef_ref[...]) * pltpu.roll(sums, half, 1)
    parts = jnp.concatenate(split(sums, 2), axis=1)
    found_ref[...] = jnp.dot(parts, block_ref[...], preferred_element_type=jnp.float32)
    rows = map_ref.shape[0] // loudest_ref.shape[1]
    copies = loudest_ref.shape[0]
    per_step = LANES // rows
    leaving = []
    for step in range(map_ref.shape[0] // LANES):
        here = pl.ds(step * LANES, LANES)
        scale_a = jnp.broadcast_to(coef_ref[here, 0:1], (LANES, LANES))
        scale_b = jnp.broadcast_to(coef_ref[here, quarter : quarter + 1], (LANES, LANES))
        best = None
        for b in range(blocks):
            ra, ia, rb, ib = (found_ref[here, pl.ds(c * templates + b * LANES, LANES)] for c in range(4))
            result = scale_a * (ra * ra + ia * ia) + scale_b * (rb * rb + ib * ib)
            tile_ref[here, pl.ds(b * LANES, LANES)] = result
            best = result if best is None else jnp.maximum(best, result)
        leaving.append(pltpu.make_async_copy(tile_ref.at[here, :], map_ref.at[here, :], sems.at[step]))
        leaving[-1].start()
        best = jnp.max(jnp.transpose(best), axis=0, keepdims=True)
        for n in range(per_step):
            turned = best if n == 0 else pltpu.roll(best, LANES - n * rows, 1)
            loudest_ref[0, pl.ds(step * per_step + n, 1), :] = turned
    for copy in range(1, copies):
        loudest_ref[copy] = loudest_ref[0]
    for copy in leaving:
        copy.wait()


def statistic(windows, mask, weigh, coef, kernel, rows, copies):
    count = mask.shape[0] // rows
    templates = kernel.shape[1]
    features = 4 * W * (templates // LANES)
    vmem = pl.BlockSpec(memory_space=pltpu.VMEM)
    return pl.pallas_call(
        statistic_kernel,
        out_shape=(
            jax.ShapeDtypeStruct((count * rows, templates), jnp.float32),
            jax.ShapeDtypeStruct((copies, count, LANES), jnp.float32),
        ),
        in_specs=[vmem] * 5,
        out_specs=(pl.BlockSpec(memory_space=pl.ANY), vmem),
        scratch_shapes=[
            pltpu.VMEM((2 * features, 4 * templates), jnp.bfloat16),
            pltpu.VMEM((count * rows, 4 * templates), jnp.float32),
            pltpu.VMEM((count * rows, templates), jnp.float32),
            pltpu.SemaphoreType.DMA((count * rows // LANES,)),
        ],
        compiler_params=pltpu.CompilerParams(vmem_limit_bytes=16 * 1024 * 1024),
        cost_estimate=pl.CostEstimate(flops=400_000_000, bytes_accessed=4_000_000, transcendentals=0),
        name="statistic",
    )(windows, mask, weigh, coef, kernel)


def exchange(values, axis, members):
    return lax.all_to_all(values, axis, split_axis=0, concat_axis=0, axis_index_groups=[members], tiled=True)


def body(spectra, offsets, fractions, antenna, starts, durations):
    bands, cores = lax.axis_size("tmpl"), lax.axis_size("tm")
    sft_rows = spectra.shape[0]
    grid_size = starts.shape[0]
    my_rows = grid_size // cores
    by_band = order(bands, bands // 2)
    first = (cores - 1) * bands + bands // 2
    by_run = order(cores * bands, first)
    known = exchange(jnp.broadcast_to(offsets.T[None], (bands,) + offsets.T.shape), "tmpl", by_band)
    held, *late = lax.optimization_barrier((hold(spectra), durations, starts, antenna, fractions))
    prepared = prepare(*late, first, sft_rows, cores)
    held, *prepared = lax.optimization_barrier((held, *prepared))
    windows = pick(known, held, by_band, [run % bands for run in by_run])
    arrived = exchange(windows.reshape(cores * bands, sft_rows, LANES), ("tm", "tmpl"), by_run)
    fstat_map, loudest = statistic(arrived.reshape(-1, LANES), *prepared, grid_size, bands)
    loudest = jnp.max(exchange(loudest, "tmpl", by_band)[:, :, :grid_size], axis=0)
    return (fstat_map.reshape(my_rows, grid_size, -1), loudest)


def solution(mesh):
    in_specs = (
        P(("grp", "tm", "tmpl"), None, None),
        P(("grp", "tm"), "tmpl"),
        P(("grp", "tmpl")),
        P("grp", None),
        P("grp"),
        P("grp"),
    )
    out_specs = (P("tm", None, ("grp", "tmpl")), P(("grp", "tm"), None))
    return jax.shard_map(body, mesh=mesh, in_specs=in_specs, out_specs=out_specs, check_vma=False)
```

```python
import functools

import jax
import jax.numpy as jnp
from jax import lax
from jax.experimental import pallas as pl
from jax.experimental.pallas import tpu as pltpu
from jax.sharding import PartitionSpec as P

W = 16
LANES = 128
NT = (((1,), (1,)), ((), ()))


def iota(shape, axis):
    return lax.broadcasted_iota(jnp.int32, shape, axis)


def order(size, first):
    members = list(range(size))
    members[0], members[first] = first, 0
    return members


def hold_kernel(spec_ref, out_ref, sem):
    copy = pltpu.make_async_copy(spec_ref, out_ref, sem)
    copy.start()
    copy.wait()


def hold(spectra):
    return pl.pallas_call(
        hold_kernel,
        out_shape=jax.ShapeDtypeStruct(spectra.shape, spectra.dtype),
        in_specs=[pl.BlockSpec(memory_space=pl.ANY)],
        out_specs=pl.BlockSpec(memory_space=pltpu.VMEM),
        scratch_shapes=[pltpu.SemaphoreType.DMA],
        compiler_params=pltpu.CompilerParams(vmem_limit_bytes=8 * 1024 * 1024),
        cost_estimate=pl.CostEstimate(flops=0, bytes_accessed=4 * spectra.size, transcendentals=0),
        name="hold",
    )(spectra)


def pick_kernel(bands_in, bands_out, offset_ref, spec_ref, out_ref, place_ref, turn_ref):
    rows, _, bins = spec_ref.shape
    bands, blocks, _ = offset_ref.shape
    band_width = bins // bands
    groups = rows // 8
    chunks = band_width // LANES
    width = blocks * W
    first = lax.axis_index("tmpl").astype(jnp.int32) * rows
    columns = pl.ds(pl.multiple_of(first // LANES * LANES, LANES), LANES)
    offsets = jnp.concatenate([offset_ref[bands_in.index(band), :, columns] for band in range(bands)], axis=0).astype(jnp.float32)
    lane = iota(offsets.shape, 1)
    offsets = jnp.take_along_axis(offsets, (lane >> 2) + first & (LANES - 1), axis=1, mode="promise_in_bounds")
    offsets = jnp.concatenate([offsets, jnp.zeros((LANES - bands * blocks, LANES), jnp.float32)], axis=0)
    upright = jnp.transpose(offsets).astype(jnp.int32)
    lane = iota((32, LANES), 1)
    places = upright[0:32]
    for group in range(1, groups):
        turned = pltpu.roll(upright[group * 32 : group * 32 + 32], group * bands * blocks, 1)
        places = jnp.where(lane < group * bands * blocks, places, turned)
    lane = iota((8, LANES), 1)
    lane_group = lane // width
    source = lane_group * (bands * blocks) + lane // W % blocks
    for band in range(bands):
        for pair in range(4):
            place = jnp.take_along_axis(places[pair * 8 : pair * 8 + 8], source + band * blocks, axis=1, mode="promise_in_bounds")
            place_ref[band, pair] = place + ((lane & (W - 1)) + lane_group * band_width)

    def gather(band):
        for pair in range(4):
            place = place_ref[band, pair]
            lane_id = place & (LANES - 1)
            chosen = place >> 7
            tile = jnp.zeros((8, LANES), jnp.float32)
            for group in range(groups):
                for chunk in range(chunks):
                    columns = pl.ds(band * band_width + chunk * LANES, LANES)
                    values = spec_ref[pl.ds(group * 8 + pair * 2, 2), :, columns]
                    values = values.astype(jnp.float32).reshape(8, LANES)
                    moved = jnp.take_along_axis(values, lane_id, axis=1, mode="promise_in_bounds")
                    tile = jnp.where(chosen == group * chunks + chunk, moved, tile)
            turn_ref[band, pl.ds(pair * 8, 8), :] = tile

    def turn(band):
        parts = [turn_ref[band, pl.ds(part, 8, stride=4), :] for part in range(4)]
        tiles = []
        for group in range(groups):
            tile = jnp.zeros((8, LANES), jnp.float32)
            for part in range(4):
                amount = (part - group) * width % LANES
                turned = pltpu.roll(parts[part], amount, 1) if amount else parts[part]
                tile = jnp.where(lane_group == part, turned, tile)
            tiles.append(tile)
        return tiles

    tiles = {}
    for band in range(bands):
        gather(band)
        tiles[band] = turn(band)
    wanted = [tile for band in bands_out for tile in tiles[band]]
    for n in range(0, len(wanted), 2):
        out_ref[n * 8 : n * 8 + 16, :] = jnp.concatenate(wanted[n : n + 2], axis=0).astype(jnp.bfloat16)


def pick(offsets, spectra, bands_in, bands_out):
    rows, bands = spectra.shape[0], offsets.shape[0]
    out_rows = len(bands_out) * rows
    vmem = pl.BlockSpec(memory_space=pltpu.VMEM)
    return pl.pallas_call(
        functools.partial(pick_kernel, bands_in, bands_out),
        out_shape=jax.ShapeDtypeStruct((out_rows, LANES), jnp.bfloat16),
        in_specs=[vmem, vmem],
        out_specs=vmem,
        scratch_shapes=[
            pltpu.VMEM((bands, 4, 8, LANES), jnp.int32),
            pltpu.VMEM((bands, 32, LANES), jnp.float32),
        ],
        compiler_params=pltpu.CompilerParams(vmem_limit_bytes=8 * 1024 * 1024),
        cost_estimate=pl.CostEstimate(flops=10_000_000, bytes_accessed=2 * spectra.size, transcendentals=0),
        name="pick",
    )(offsets, spectra)


def split(values, count):
    parts = []
    for _ in range(count):
        part = values.astype(jnp.bfloat16)
        parts.append(part)
        values = values - part.astype(jnp.float32)
    return parts


def prepare_kernel(first, run, durations_ref, starts_ref, antenna_ref, fractions_ref, mask_ref, weigh_ref, coef_ref, kernel_ref):
    rows = starts_ref.shape[0]
    count = mask_ref.shape[0] // rows
    mine = lax.axis_index("tm").astype(jnp.int32) * count
    sfts = antenna_ref.shape[1]
    sft = iota((rows, sfts), 1)
    sft = jnp.where(sft // run == 0, sft + first * run, jnp.where(sft // run == first, sft - first * run, sft))
    start = starts_ref[:, 0:1]
    after = sft >= start
    for j in range(count):
        inside = after & (sft < start + durations_ref[mine + j])
        mask_ref[pl.ds(j * rows, rows), :] = jnp.where(inside, 1.0, 0.0).astype(jnp.bfloat16)
    antenna = jnp.concatenate([antenna_ref[...], jnp.zeros((4, sfts), jnp.float32)], axis=0)
    place = iota(antenna.shape, 1) // run
    after = pltpu.roll(antenna, sfts - first * run, 1)
    before = pltpu.roll(antenna, first * run, 1)
    antenna = jnp.where(place == 0, after, jnp.where(place == first, before, antenna))
    a1, a2, b1, b2 = (antenna[n : n + 1] for n in range(4))
    terms = jnp.concatenate([a1 * a1 + a2 * a2, b1 * b1 + b2 * b2, a1 * b1 + a2 * b2, jnp.zeros((5, sfts), jnp.float32)], axis=0)
    sums = lax.dot_general(jnp.concatenate(split(terms, 3), axis=0), mask_ref[...], NT, preferred_element_type=jnp.float32)
    sums = sums[0:8] + sums[8:16] + sums[16:24]
    wa, wb, wc = (sums[n : n + 1] for n in range(3))

    def quarters(*factors):
        shape = (LANES // 4, factors[0].shape[1])
        return jnp.transpose(jnp.concatenate([jnp.broadcast_to(factor, shape) for factor in factors], axis=0))

    coef_ref[...] = quarters(1.0 / wa, wa / (wa * wb - wc * wc), wc / wa, wc / wa)
    weigh_ref[...] = quarters(a1, a2, b2, b1)
    fractions = fractions_ref[...]
    bin_id = iota((W, fractions.shape[1]), 0)
    distance = fractions + (W // 2 - 1) - bin_id.astype(jnp.float32)
    alternate = 1.0 - 2.0 * (bin_id % 2).astype(jnp.float32)
    kernel_ref[...] = (alternate * jnp.sin(jnp.pi * fractions) / (jnp.pi * distance)).astype(jnp.bfloat16)


def prepare(durations, starts, antenna, fractions, first, run, cores):
    count, rows, sfts = durations.shape[0] // cores, starts.shape[0], antenna.shape[0]
    vmem = pl.BlockSpec(memory_space=pltpu.VMEM)
    return pl.pallas_call(
        functools.partial(prepare_kernel, first, run),
        out_shape=(
            jax.ShapeDtypeStruct((count * rows, sfts), jnp.bfloat16),
            jax.ShapeDtypeStruct((sfts, LANES), jnp.float32),
            jax.ShapeDtypeStruct((count * rows, LANES), jnp.float32),
            jax.ShapeDtypeStruct((W, fractions.shape[0]), jnp.bfloat16),
        ),
        in_specs=[pl.BlockSpec(memory_space=pltpu.SMEM), vmem, vmem, vmem],
        out_specs=(vmem,) * 4,
        compiler_params=pltpu.CompilerParams(vmem_limit_bytes=16 * 1024 * 1024),
        cost_estimate=pl.CostEstimate(flops=100_000_000, bytes_accessed=4_000_000, transcendentals=0),
        name="prepare",
    )(durations, jnp.broadcast_to(starts[:, None], (rows, LANES)), antenna.T, fractions[None, :])


def statistic_kernel(windows_ref, mask_ref, weigh_ref, coef_ref, kernel_ref, map_ref, loudest_ref, block_ref, found_ref, tile_ref, sems):
    templates = map_ref.shape[1]
    blocks = templates // LANES
    block_ref[...] = jnp.zeros_like(block_ref)
    for part in range(2):
        for c in range(4):
            for b in range(blocks):
                row, column = ((part * 4 + c) * blocks + b) * W, (c * blocks + b) * LANES
                block_ref[pl.ds(row, W), pl.ds(column, LANES)] = kernel_ref[:, b * LANES : (b + 1) * LANES]
    values = windows_ref[...].astype(jnp.float32)
    half, quarter = LANES // 2, LANES // 4
    weigh = weigh_ref[...]
    even = iota(weigh.shape, 1) // quarter % 2 == 0
    own = jnp.where(even, weigh, pltpu.roll(weigh, quarter, 1))
    other = jnp.where(even, pltpu.roll(weigh, LANES - quarter, 1), weigh)
    weighted = (own * values + other * pltpu.roll(values, half, 1)).astype(jnp.bfloat16)
    sums = jnp.dot(mask_ref[...], weighted, preferred_element_type=jnp.float32)
    sums = sums - jnp.where(iota(sums.shape, 1) < half, 0.0, coef_ref[...]) * pltpu.roll(sums, half, 1)
    parts = jnp.concatenate(split(sums, 2), axis=1)
    found_ref[...] = jnp.dot(parts, block_ref[...], preferred_element_type=jnp.float32)
    leaving = []
    for step in range(map_ref.shape[0] // LANES):
        here = pl.ds(step * LANES, LANES)
        scale_a = jnp.broadcast_to(coef_ref[here, 0:1], (LANES, LANES))
        scale_b = jnp.broadcast_to(coef_ref[here, quarter : quarter + 1], (LANES, LANES))
        best = None
        for b in range(blocks):
            ra, ia, rb, ib = (found_ref[here, pl.ds(c * templates + b * LANES, LANES)] for c in range(4))
            result = scale_a * (ra * ra + ia * ia) + scale_b * (rb * rb + ib * ib)
            tile_ref[here, pl.ds(b * LANES, LANES)] = result
            best = result if best is None else jnp.maximum(best, result)
        leaving.append(pltpu.make_async_copy(tile_ref.at[here, :], map_ref.at[here, :], sems.at[step]))
        leaving[-1].start()
        best = jnp.max(jnp.transpose(best), axis=0, keepdims=True)
        for copy in range(loudest_ref.shape[0]):
            loudest_ref[copy, pl.ds(step, 1), :] = best
    for copy in leaving:
        copy.wait()


def statistic(windows, mask, weigh, coef, kernel, copies):
    total = mask.shape[0]
    templates = kernel.shape[1]
    features = 4 * W * (templates // LANES)
    vmem = pl.BlockSpec(memory_space=pltpu.VMEM)
    return pl.pallas_call(
        statistic_kernel,
        out_shape=(
            jax.ShapeDtypeStruct((total, templates), jnp.float32),
            jax.ShapeDtypeStruct((copies, total // LANES, LANES), jnp.float32),
        ),
        in_specs=[vmem] * 5,
        out_specs=(pl.BlockSpec(memory_space=pl.ANY), vmem),
        scratch_shapes=[
            pltpu.VMEM((2 * features, 4 * templates), jnp.bfloat16),
            pltpu.VMEM((total, 4 * templates), jnp.float32),
            pltpu.VMEM((total, templates), jnp.float32),
            pltpu.SemaphoreType.DMA((total // LANES,)),
        ],
        compiler_params=pltpu.CompilerParams(vmem_limit_bytes=16 * 1024 * 1024),
        cost_estimate=pl.CostEstimate(flops=400_000_000, bytes_accessed=4_000_000, transcendentals=0),
        name="statistic",
    )(windows, mask, weigh, coef, kernel)


def loudest_kernel(found_ref, out_ref):
    best = found_ref[0]
    for n in range(1, found_ref.shape[0]):
        best = jnp.maximum(best, found_ref[n])
    width = out_ref.shape[1]
    for row in range(out_ref.shape[0]):
        start = row * width
        line = best[start // LANES : start // LANES + 1]
        line = pltpu.roll(line, LANES - start % LANES, 1) if start % LANES else line
        out_ref[row : row + 1, :] = line[:, :width]


def largest(found, count, width):
    vmem = pl.BlockSpec(memory_space=pltpu.VMEM)
    return pl.pallas_call(
        loudest_kernel,
        out_shape=jax.ShapeDtypeStruct((count, width), jnp.float32),
        in_specs=[vmem],
        out_specs=vmem,
        compiler_params=pltpu.CompilerParams(vmem_limit_bytes=8 * 1024 * 1024),
        name="largest",
    )(found)


def exchange(values, axis, members):
    return lax.all_to_all(values, axis, split_axis=0, concat_axis=0, axis_index_groups=[members], tiled=True)


def body(spectra, offsets, fractions, antenna, starts, durations):
    bands, cores = lax.axis_size("tmpl"), lax.axis_size("tm")
    sft_rows = spectra.shape[0]
    grid_size = starts.shape[0]
    my_rows = grid_size // cores
    by_band = order(bands, bands // 2)
    first = (cores - 1) * bands + bands // 2
    by_run = order(cores * bands, first)
    known = exchange(jnp.broadcast_to(offsets.T[None], (bands,) + offsets.T.shape), "tmpl", by_band)
    held, *late = lax.optimization_barrier((hold(spectra), durations, starts, antenna, fractions))
    prepared = prepare(*late, first, sft_rows, cores)
    held, *prepared = lax.optimization_barrier((held, *prepared))
    windows = pick(known, held, by_band, [run % bands for run in by_run])
    arrived = exchange(windows.reshape(cores * bands, sft_rows, LANES), ("tm", "tmpl"), by_run)
    fstat_map, loudest = statistic(arrived.reshape(-1, LANES), *prepared, bands)
    loudest = largest(exchange(loudest, "tmpl", by_band), my_rows, grid_size)
    return (fstat_map.reshape(my_rows, grid_size, -1), loudest)


def solution(mesh):
    in_specs = (
        P(("grp", "tm", "tmpl"), None, None),
        P(("grp", "tm"), "tmpl"),
        P(("grp", "tmpl")),
        P("grp", None),
        P("grp"),
        P("grp"),
    )
    out_specs = (P("tm", None, ("grp", "tmpl")), P(("grp", "tm"), None))
    return jax.shard_map(body, mesh=mesh, in_specs=in_specs, out_specs=out_specs, check_vma=False)
```

```python
import functools

import jax
import jax.numpy as jnp
from jax import lax
from jax.experimental import pallas as pl
from jax.experimental.pallas import tpu as pltpu
from jax.sharding import PartitionSpec as P

W = 16
LANES = 128
NT = (((1,), (1,)), ((), ()))


def iota(shape, axis):
    return lax.broadcasted_iota(jnp.int32, shape, axis)


def order(size, first):
    members = list(range(size))
    members[0], members[first] = first, 0
    return members


def hold_kernel(spec_ref, out_ref, sem):
    copy = pltpu.make_async_copy(spec_ref, out_ref, sem)
    copy.start()
    copy.wait()


def hold(spectra):
    return pl.pallas_call(
        hold_kernel,
        out_shape=jax.ShapeDtypeStruct(spectra.shape, spectra.dtype),
        in_specs=[pl.BlockSpec(memory_space=pl.ANY)],
        out_specs=pl.BlockSpec(memory_space=pltpu.VMEM),
        scratch_shapes=[pltpu.SemaphoreType.DMA],
        compiler_params=pltpu.CompilerParams(vmem_limit_bytes=8 * 1024 * 1024),
        cost_estimate=pl.CostEstimate(flops=0, bytes_accessed=4 * spectra.size, transcendentals=0),
        name="hold",
    )(spectra)


def pick_kernel(bands_in, bands_out, offset_ref, spec_ref, out_ref, place_ref, turn_ref):
    rows, _, bins = spec_ref.shape
    bands, blocks, _ = offset_ref.shape
    band_width = bins // bands
    groups = rows // 8
    chunks = band_width // LANES
    width = blocks * W
    first = lax.axis_index("tmpl").astype(jnp.int32) * rows
    columns = pl.ds(pl.multiple_of(first // LANES * LANES, LANES), LANES)
    offsets = jnp.concatenate([offset_ref[bands_in.index(band), :, columns] for band in range(bands)], axis=0).astype(jnp.float32)
    lane = iota(offsets.shape, 1)
    offsets = jnp.take_along_axis(offsets, (lane >> 2) + first & (LANES - 1), axis=1, mode="promise_in_bounds")
    offsets = jnp.concatenate([offsets, jnp.zeros((LANES - bands * blocks, LANES), jnp.float32)], axis=0)
    upright = jnp.transpose(offsets).astype(jnp.int32)
    lane = iota((32, LANES), 1)
    places = upright[0:32]
    for group in range(1, groups):
        turned = pltpu.roll(upright[group * 32 : group * 32 + 32], group * bands * blocks, 1)
        places = jnp.where(lane < group * bands * blocks, places, turned)
    lane = iota((8, LANES), 1)
    lane_group = lane // width
    source = lane_group * (bands * blocks) + lane // W % blocks
    for band in range(bands):
        for pair in range(4):
            place = jnp.take_along_axis(places[pair * 8 : pair * 8 + 8], (source + band * blocks) & (LANES - 1), axis=1, mode="promise_in_bounds")
            place_ref[band, pair] = place + ((lane & (W - 1)) + lane_group * band_width)

    def gather(band):
        for pair in range(4):
            place = place_ref[band, pair]
            lane_id = place & (LANES - 1)
            chosen = place >> 7
            tile = jnp.zeros((8, LANES), jnp.float32)
            for group in range(groups):
                for chunk in range(chunks):
                    columns = pl.ds(band * band_width + chunk * LANES, LANES)
                    values = spec_ref[pl.ds(group * 8 + pair * 2, 2), :, columns]
                    values = values.astype(jnp.float32).reshape(8, LANES)
                    moved = jnp.take_along_axis(values, lane_id, axis=1, mode="promise_in_bounds")
                    tile = jnp.where(chosen == group * chunks + chunk, moved, tile)
            turn_ref[band, pl.ds(pair * 8, 8), :] = tile

    def turn(band):
        parts = [turn_ref[band, pl.ds(part, 8, stride=4), :] for part in range(4)]
        tiles = []
        for group in range(groups):
            tile = jnp.zeros((8, LANES), jnp.float32)
            for part in range(4):
                amount = (part - group) * width % LANES
                turned = pltpu.roll(parts[part], amount, 1) if amount else parts[part]
                tile = jnp.where(lane_group == part, turned, tile)
            tiles.append(tile)
        return tiles

    tiles = {}
    for band in range(bands):
        gather(band)
        tiles[band] = turn(band)
    wanted = [tile for band in bands_out for tile in tiles[band]]
    for n in range(0, len(wanted), 2):
        out_ref[n * 8 : n * 8 + 16, :] = jnp.concatenate(wanted[n : n + 2], axis=0).astype(jnp.bfloat16)


def pick(offsets, spectra, bands_in, bands_out):
    rows, bands = spectra.shape[0], offsets.shape[0]
    out_rows = len(bands_out) * rows
    vmem = pl.BlockSpec(memory_space=pltpu.VMEM)
    return pl.pallas_call(
        functools.partial(pick_kernel, bands_in, bands_out),
        out_shape=jax.ShapeDtypeStruct((out_rows, LANES), jnp.bfloat16),
        in_specs=[vmem, vmem],
        out_specs=vmem,
        scratch_shapes=[
            pltpu.VMEM((bands, 4, 8, LANES), jnp.int32),
            pltpu.VMEM((bands, 32, LANES), jnp.float32),
        ],
        compiler_params=pltpu.CompilerParams(vmem_limit_bytes=8 * 1024 * 1024),
        cost_estimate=pl.CostEstimate(flops=10_000_000, bytes_accessed=2 * spectra.size, transcendentals=0),
        name="pick",
    )(offsets, spectra)


def split(values, count):
    parts = []
    for _ in range(count):
        part = values.astype(jnp.bfloat16)
        parts.append(part)
        values = values - part.astype(jnp.float32)
    return parts


def prepare_kernel(first, run, durations_ref, starts_ref, antenna_ref, fractions_ref, mask_ref, weigh_ref, coef_ref, kernel_ref):
    rows = starts_ref.shape[0]
    count = mask_ref.shape[0] // rows
    mine = lax.axis_index("tm").astype(jnp.int32) * count
    sfts = antenna_ref.shape[1]
    sft = iota((rows, sfts), 1)
    sft = jnp.where(sft // run == 0, sft + first * run, jnp.where(sft // run == first, sft - first * run, sft))
    start = starts_ref[:, 0:1]
    after = sft >= start
    for j in range(count):
        inside = after & (sft < start + durations_ref[mine + j])
        mask_ref[pl.ds(j * rows, rows), :] = jnp.where(inside, 1.0, 0.0).astype(jnp.bfloat16)
    antenna = jnp.concatenate([antenna_ref[...], jnp.zeros((4, sfts), jnp.float32)], axis=0)
    place = iota(antenna.shape, 1) // run
    after = pltpu.roll(antenna, sfts - first * run, 1)
    before = pltpu.roll(antenna, first * run, 1)
    antenna = jnp.where(place == 0, after, jnp.where(place == first, before, antenna))
    a1, a2, b1, b2 = (antenna[n : n + 1] for n in range(4))
    terms = jnp.concatenate([a1 * a1 + a2 * a2, b1 * b1 + b2 * b2, a1 * b1 + a2 * b2, jnp.zeros((5, sfts), jnp.float32)], axis=0)
    sums = lax.dot_general(jnp.concatenate(split(terms, 3), axis=0), mask_ref[...], NT, preferred_element_type=jnp.float32)
    sums = sums[0:8] + sums[8:16] + sums[16:24]
    wa, wb, wc = (sums[n : n + 1] for n in range(3))

    def quarters(*factors):
        shape = (LANES // 4, factors[0].shape[1])
        return jnp.transpose(jnp.concatenate([jnp.broadcast_to(factor, shape) for factor in factors], axis=0))

    coef_ref[...] = quarters(1.0 / wa, wa / (wa * wb - wc * wc), wc / wa, wc / wa)
    weigh_ref[...] = quarters(a1, a2, b2, b1)
    fractions = fractions_ref[...]
    bin_id = iota((W, fractions.shape[1]), 0)
    distance = fractions + (W // 2 - 1) - bin_id.astype(jnp.float32)
    alternate = 1.0 - 2.0 * (bin_id % 2).astype(jnp.float32)
    kernel_ref[...] = (alternate * jnp.sin(jnp.pi * fractions) / (jnp.pi * distance)).astype(jnp.bfloat16)


def prepare(durations, starts, antenna, fractions, first, run, cores):
    count, rows, sfts = durations.shape[0] // cores, starts.shape[0], antenna.shape[0]
    vmem = pl.BlockSpec(memory_space=pltpu.VMEM)
    return pl.pallas_call(
        functools.partial(prepare_kernel, first, run),
        out_shape=(
            jax.ShapeDtypeStruct((count * rows, sfts), jnp.bfloat16),
            jax.ShapeDtypeStruct((sfts, LANES), jnp.float32),
            jax.ShapeDtypeStruct((count * rows, LANES), jnp.float32),
            jax.ShapeDtypeStruct((W, fractions.shape[0]), jnp.bfloat16),
        ),
        in_specs=[pl.BlockSpec(memory_space=pltpu.SMEM), vmem, vmem, vmem],
        out_specs=(vmem,) * 4,
        compiler_params=pltpu.CompilerParams(vmem_limit_bytes=16 * 1024 * 1024),
        cost_estimate=pl.CostEstimate(flops=100_000_000, bytes_accessed=4_000_000, transcendentals=0),
        name="prepare",
    )(durations, jnp.broadcast_to(starts[:, None], (rows, LANES)), antenna.T, fractions[None, :])


def statistic_kernel(windows_ref, mask_ref, weigh_ref, coef_ref, kernel_ref, map_ref, loudest_ref, block_ref, found_ref, tile_ref, sems):
    templates = map_ref.shape[1]
    blocks = templates // LANES
    block_ref[...] = jnp.zeros_like(block_ref)
    for part in range(2):
        for c in range(4):
            for b in range(blocks):
                row, column = ((part * 4 + c) * blocks + b) * W, (c * blocks + b) * LANES
                block_ref[pl.ds(row, W), pl.ds(column, LANES)] = kernel_ref[:, b * LANES : (b + 1) * LANES]
    values = windows_ref[...].astype(jnp.float32)
    half, quarter = LANES // 2, LANES // 4
    weigh = weigh_ref[...]
    even = iota(weigh.shape, 1) // quarter % 2 == 0
    own = jnp.where(even, weigh, pltpu.roll(weigh, quarter, 1))
    other = jnp.where(even, pltpu.roll(weigh, LANES - quarter, 1), weigh)
    weighted = (own * values + other * pltpu.roll(values, half, 1)).astype(jnp.bfloat16)
    sums = jnp.dot(mask_ref[...], weighted, preferred_element_type=jnp.float32)
    sums = sums - jnp.where(iota(sums.shape, 1) < half, 0.0, coef_ref[...]) * pltpu.roll(sums, half, 1)
    parts = jnp.concatenate(split(sums, 2), axis=1)
    found_ref[...] = jnp.dot(parts, block_ref[...], preferred_element_type=jnp.float32)
    leaving = []
    for step in range(map_ref.shape[0] // LANES):
        here = pl.ds(step * LANES, LANES)
        scale_a = jnp.broadcast_to(coef_ref[here, 0:1], (LANES, LANES))
        scale_b = jnp.broadcast_to(coef_ref[here, quarter : quarter + 1], (LANES, LANES))
        best = None
        for b in range(blocks):
            ra, ia, rb, ib = (found_ref[here, pl.ds(c * templates + b * LANES, LANES)] for c in range(4))
            result = scale_a * (ra * ra + ia * ia) + scale_b * (rb * rb + ib * ib)
            tile_ref[here, pl.ds(b * LANES, LANES)] = result
            best = result if best is None else jnp.maximum(best, result)
        leaving.append(pltpu.make_async_copy(tile_ref.at[here, :], map_ref.at[here, :], sems.at[step]))
        leaving[-1].start()
        best = jnp.max(jnp.transpose(best), axis=0, keepdims=True)
        for copy in range(loudest_ref.shape[0]):
            loudest_ref[copy, pl.ds(step, 1), :] = best
    for copy in leaving:
        copy.wait()


def statistic(windows, mask, weigh, coef, kernel, copies):
    total = mask.shape[0]
    templates = kernel.shape[1]
    features = 4 * W * (templates // LANES)
    vmem = pl.BlockSpec(memory_space=pltpu.VMEM)
    return pl.pallas_call(
        statistic_kernel,
        out_shape=(
            jax.ShapeDtypeStruct((total, templates), jnp.float32),
            jax.ShapeDtypeStruct((copies, total // LANES, LANES), jnp.float32),
        ),
        in_specs=[vmem] * 5,
        out_specs=(pl.BlockSpec(memory_space=pl.ANY), vmem),
        scratch_shapes=[
            pltpu.VMEM((2 * features, 4 * templates), jnp.bfloat16),
            pltpu.VMEM((total, 4 * templates), jnp.float32),
            pltpu.VMEM((total, templates), jnp.float32),
            pltpu.SemaphoreType.DMA((total // LANES,)),
        ],
        compiler_params=pltpu.CompilerParams(vmem_limit_bytes=16 * 1024 * 1024),
        cost_estimate=pl.CostEstimate(flops=400_000_000, bytes_accessed=4_000_000, transcendentals=0),
        name="statistic",
    )(windows, mask, weigh, coef, kernel)


def loudest_kernel(found_ref, out_ref):
    best = found_ref[0]
    for n in range(1, found_ref.shape[0]):
        best = jnp.maximum(best, found_ref[n])
    width = out_ref.shape[1]
    for row in range(out_ref.shape[0]):
        start = row * width
        line = best[start // LANES : start // LANES + 1]
        line = pltpu.roll(line, LANES - start % LANES, 1) if start % LANES else line
        out_ref[row : row + 1, :] = line[:, :width]


def largest(found, count, width):
    vmem = pl.BlockSpec(memory_space=pltpu.VMEM)
    return pl.pallas_call(
        loudest_kernel,
        out_shape=jax.ShapeDtypeStruct((count, width), jnp.float32),
        in_specs=[vmem],
        out_specs=vmem,
        compiler_params=pltpu.CompilerParams(vmem_limit_bytes=8 * 1024 * 1024),
        name="largest",
    )(found)


def exchange(values, axis, members):
    return lax.all_to_all(values, axis, split_axis=0, concat_axis=0, axis_index_groups=[members], tiled=True)


def body(spectra, offsets, fractions, antenna, starts, durations):
    bands, cores = lax.axis_size("tmpl"), lax.axis_size("tm")
    sft_rows = spectra.shape[0]
    grid_size = starts.shape[0]
    my_rows = grid_size // cores
    by_band = order(bands, bands // 2)
    first = (cores - 1) * bands + bands // 2
    by_run = order(cores * bands, first)
    known = exchange(jnp.broadcast_to(offsets.T[None], (bands,) + offsets.T.shape), "tmpl", by_band)
    held, *late = lax.optimization_barrier((hold(spectra), durations, starts, antenna, fractions))
    prepared = prepare(*late, first, sft_rows, cores)
    held, *prepared = lax.optimization_barrier((held, *prepared))
    windows = pick(known, held, by_band, [run % bands for run in by_run])
    arrived = exchange(windows.reshape(cores * bands, sft_rows, LANES), ("tm", "tmpl"), by_run)
    fstat_map, loudest = statistic(arrived.reshape(-1, LANES), *prepared, bands)
    loudest = largest(exchange(loudest, "tmpl", by_band), my_rows, grid_size)
    return (fstat_map.reshape(my_rows, grid_size, -1), loudest)


def solution(mesh):
    in_specs = (
        P(("grp", "tm", "tmpl"), None, None),
        P(("grp", "tm"), "tmpl"),
        P(("grp", "tmpl")),
        P("grp", None),
        P("grp"),
        P("grp"),
    )
    out_specs = (P("tm", None, ("grp", "tmpl")), P(("grp", "tm"), None))
    return jax.shard_map(body, mesh=mesh, in_specs=in_specs, out_specs=out_specs, check_vma=False)
```
